32 devices in a mesh: seq: 32 (over z, y, x, core).
Axes of the slice: x: 2, y: 2, z: 4, core: 2. Of those that a mesh axis runs over, the one named last changes fastest.
Arguments:
- queries: bfloat16 [32768, 1024], P('seq'), may hold values from -8 to 8, as said below
- keys: bfloat16 [32768, 1024], P('seq'), may hold values from -8 to 8
- values: bfloat16 [32768, 1024], P('seq'), may hold values from -6 to 6
- w_out: bfloat16 [1024, 2048], replicated, may hold values from -0.1875 to 0.1875
Outputs:
- output: bfloat16 [32768, 2048], P('seq')
The draws below stay inside these ranges and needn't reach their ends.
Inputs may be any that keep to these rules, and one draw needn't show every extreme that they name: `queries`: query entries lie in the range.
All inputs are finite; a program needn't handle non-finite values.
Results may differ from the reference program's by a relative error of at most 0.0023.
The reference program's roundings to bfloat16 on the way count: a program that leaves them out, or rounds other values in their place, can miss the bound.
Values may be sent and summed in bfloat16 or wider, within the bound.
No kernel may reach another device: no remote copies, remote signals or barrier semaphores. Data moves between devices by JAX's collectives and lax.ppermute only.
A program may use at most 128 MiB of HBM per device.

```python
import jax
import jax.numpy as jnp
from jax import lax

HEADS = 8
HEAD_DIM = 128
D_MODEL = 2048
BLOCK = 256
TOK_DEV = 1024
SEQ = 32768
LEVELS = 6
WIDTH = 1024


def draw_queries(key, part):
    key = jax.random.fold_in(key, 11)
    base = jnp.clip(jax.random.normal(key, (SEQ, HEADS * HEAD_DIM), jnp.float32), -4.0, 4.0)
    return base.astype(jnp.bfloat16)


def draw_keys(key, part):
    key = jax.random.fold_in(key, 23)
    base = jnp.clip(jax.random.normal(key, (SEQ, HEADS * HEAD_DIM), jnp.float32), -4.0, 4.0)
    return base.astype(jnp.bfloat16)


def steps_of(own_key, shape, shards, low, largest):
    def one(dim, shards_of):
        draws = jax.random.uniform(jax.random.fold_in(jax.random.fold_in(own_key, 6), dim), (shards_of,), jnp.float32, low / len(shards), largest / len(shards))
        return jnp.repeat(jnp.exp(draws), shape[dim] // shards_of).reshape((-1,) + (1,) * (len(shape) - dim - 1))

    factor_of = one(*shards[0])
    for cut in shards[1:]:
        factor_of = factor_of * one(*cut)
    return factor_of


def centred(stream_key, extent, scale, limit, pieces=(), kind=jnp.bfloat16):
    values = scale * jax.random.normal(stream_key, extent, jnp.float32)
    if pieces:
        values = values * steps_of(stream_key, extent, pieces, -0.22, 0.18)
    return jnp.clip(values, -limit, limit).astype(kind)


def setup_inputs(seed: int = 0) -> dict:
    splits = jax.random.split(jax.random.key(seed), 5)
    queries = draw_queries(jax.random.fold_in(splits[4], 71), 0)
    keys = draw_keys(jax.random.fold_in(splits[4], 71), 0)
    values = centred(splits[2], (SEQ, WIDTH), 1.0, 6.0, ((0, 32),))
    w_out = centred(splits[3], (WIDTH, D_MODEL), WIDTH ** -0.5, 0.1875)
    return {"queries": queries, "keys": keys, "values": values, "w_out": w_out}


NEG = -1e30


def block_term(query_rows, key_rows, value_rows, allowed, factor):
    count_q = query_rows.shape[0]
    count_k = key_rows.shape[0]
    q_heads = query_rows.reshape(count_q, HEADS, HEAD_DIM).astype(jnp.float32)
    k_heads = key_rows.reshape(count_k, HEADS, HEAD_DIM).astype(jnp.float32)
    v_heads = value_rows.reshape(count_k, HEADS, HEAD_DIM).astype(jnp.float32)
    scores = jnp.einsum("ghd,khd->hgk", q_heads, k_heads) * (HEAD_DIM ** -0.5)
    scores = jnp.where(allowed[None], scores, NEG)
    peak = jnp.max(scores, axis=-1)
    probs = jnp.exp(scores - peak[..., None])
    total = factor * jnp.sum(probs, axis=-1)
    rounded = lax.optimization_barrier(probs.astype(jnp.bfloat16)).astype(jnp.float32)
    weighted = factor * jnp.einsum("hgk,khd->ghd", rounded, v_heads)
    return weighted.reshape(count_q, HEADS * HEAD_DIM), peak.T, total.T


def level_zero(q_rows, k_rows, v_rows):
    count = q_rows.shape[0]
    pairs = count // (2 * BLOCK)
    index = jnp.arange(2 * BLOCK)
    causal = index[None, :] <= index[:, None]
    width = HEADS * HEAD_DIM
    fn = jax.vmap(lambda a, b, c: block_term(a, b, c, causal, 1.0))
    num, peak, total = fn(q_rows.reshape(pairs, 2 * BLOCK, width), k_rows.reshape(pairs, 2 * BLOCK, width),
                          v_rows.reshape(pairs, 2 * BLOCK, width))
    return num.reshape(count, width), peak.reshape(count, HEADS), total.reshape(count, HEADS)


def coarse_level(coarse_q, coarse_k, coarse_v, start, count, level):
    group = min(count, BLOCK)
    blocks = count // group
    offsets = start + jnp.arange(blocks, dtype=jnp.int32) * group
    allowed = jnp.ones((group, BLOCK), dtype=bool)

    def one(offset):
        query_rows = lax.dynamic_slice_in_dim(coarse_q, offset, group, 0)
        index = offset // BLOCK
        key_start = (jnp.maximum(index - 1, 0) * BLOCK).astype(jnp.int32)
        key_rows = lax.dynamic_slice_in_dim(coarse_k, key_start, BLOCK, 0)
        value_rows = lax.dynamic_slice_in_dim(coarse_v, key_start, BLOCK, 0)
        num, peak, total = block_term(query_rows, key_rows, value_rows, allowed, float(2 ** level))
        live = index % 2 == 1
        return jnp.where(live, num, 0.0), jnp.where(live, peak, NEG), jnp.where(live, total, 0.0)

    num, peak, total = jax.vmap(one)(offsets)
    return num.reshape(count, -1), peak.reshape(count, HEADS), total.reshape(count, HEADS)


def combine(terms, count):
    peaks = [jnp.repeat(term[1], 2 ** term[3], axis=0) for term in terms]
    top = peaks[0]
    for item in peaks[1:]:
        top = jnp.maximum(top, item)
    acc_num = jnp.zeros((count, HEADS, HEAD_DIM), jnp.float32)
    acc_den = jnp.zeros((count, HEADS), jnp.float32)
    for term, fine_peak in zip(terms, peaks):
        factor = jnp.exp(fine_peak - top)
        fine_num = jnp.repeat(term[0], 2 ** term[3], axis=0).reshape(count, HEADS, HEAD_DIM)
        acc_num = acc_num + factor[:, :, None] * fine_num
        acc_den = acc_den + factor * jnp.repeat(term[2], 2 ** term[3], axis=0)
    return (acc_num / acc_den[:, :, None]).reshape(count, HEADS * HEAD_DIM).astype(jnp.bfloat16)


def reference(queries, keys, values, w_out):
    width = HEADS * HEAD_DIM
    coarse = []
    for level in range(1, LEVELS + 1):
        trio = []
        for source in (queries, keys, values):
            summed = jnp.sum(source.reshape(SEQ >> level, 2 ** level, width), axis=1, dtype=jnp.float32)
            trio.append((summed / (2 ** level)).astype(jnp.bfloat16))
        coarse.append(trio)

    def stretch(index):
        start = (index * TOK_DEV).astype(jnp.int32)
        q_rows = lax.dynamic_slice_in_dim(queries, start, TOK_DEV, 0)
        k_rows = lax.dynamic_slice_in_dim(keys, start, TOK_DEV, 0)
        v_rows = lax.dynamic_slice_in_dim(values, start, TOK_DEV, 0)
        terms = [level_zero(q_rows, k_rows, v_rows) + (0,)]
        for level in range(1, LEVELS + 1):
            count = TOK_DEV >> level
            trio = coarse[level - 1]
            terms.append(coarse_level(trio[0], trio[1], trio[2], (index * count).astype(jnp.int32), count, level) + (level,))
        attended = combine(terms, TOK_DEV)
        return jnp.dot(attended, w_out, preferred_element_type=jnp.float32).astype(jnp.bfloat16)

    result = lax.map(stretch, jnp.arange(SEQ // TOK_DEV, dtype=jnp.int32))
    return result.reshape(SEQ, D_MODEL)
```

```python
import functools

import jax
import jax.numpy as jnp
import numpy as np
from jax import lax
from jax.experimental import pallas as pl
from jax.experimental.pallas import tpu as pltpu
from jax.sharding import PartitionSpec as P

HEADS = 8
HEAD = 128
BLOCK = 256
TOK = 1024
UNITS = TOK // BLOCK
WIDTH = HEADS * HEAD
NEG = -1e30
FIRST = 2
SCALE = HEAD**-0.5
LOG2E = 1.4426950408889634
MIB = 1 << 20
SLICES = 4
VMEM_CLAIM = 60 * MIB
HBM = pl.BlockSpec(memory_space=pltpu.HBM)


def token_of(position):
    token = (position & 7) << 5
    for bit in range(5):
        token = token | (((position >> (3 + bit)) & 1) << (4 - bit))
    return token


def count_of(level):
    return max(BLOCK >> level, 8)


def pool_rows(level):
    rows = token_of(np.arange(count_of(level))) >> level
    columns = np.arange(BLOCK) >> level
    return (rows[:, None] == columns[None, :]) * 2.0**-level


def natural_pool(level, span):
    rows = np.arange(span >> level)
    return (rows[:, None] == (np.arange(span) >> level)[None, :]) * 2.0**-level


def padded(array, multiple):
    return np.pad(array, ((0, -len(array) % multiple), (0, 0)))


def as_bf16(array):
    return jnp.asarray(array.astype(np.float32)).astype(jnp.bfloat16)


def dot(a, b):
    return jnp.dot(a, b, preferred_element_type=jnp.float32)


def dot_t(a, b):
    return lax.dot_general(a, b, (((1,), (1,)), ((), ())), preferred_element_type=jnp.float32)


def twice(array):
    return jnp.concatenate([array, array], axis=0)


def merge(first, second):
    top = jnp.maximum(first[1], second[1])
    a = jnp.exp(first[1] - top)
    b = jnp.exp(second[1] - top)
    return (a * first[0] + b * second[0], top, a * first[2] + b * second[2])


def soft_rows(sources, targets, biases, rows, chunk):
    peaks, totals = [], []
    for start in range(0, rows, chunk):
        span = slice(start, start + chunk)
        scores = [
            source[span, :] if bias is None else source[span, :] + bias[span, :]
            for source, bias in zip(sources, biases)
        ]
        peak = functools.reduce(jnp.maximum, [jnp.max(item, axis=1, keepdims=True) for item in scores])
        total = 0.0
        for item, target in zip(scores, targets):
            probs = jnp.exp2((item - peak) * (SCALE * LOG2E))
            total = total + jnp.sum(probs, axis=1, keepdims=True)
            target[span, :] = probs.astype(jnp.bfloat16)
        peaks.append(peak * SCALE)
        totals.append(total)
    return jnp.concatenate(peaks, axis=0), jnp.concatenate(totals, axis=0)


def pool_kernel(levels, small_ref, large_ref, keys_ref, values_ref, *refs):
    count = levels - FIRST + 1
    targets, (small, large, buffers, *outs, sems, out_sems) = refs[:count], refs[count:]
    step = WIDTH // 4
    fixed = [pltpu.make_async_copy(small_ref, small, sems.at[8]), pltpu.make_async_copy(large_ref, large, sems.at[9])]
    copies = []
    for index, source in enumerate((keys_ref, values_ref)):
        for part in range(4):
            cols = slice(part * step, (part + 1) * step)
            copies.append(pltpu.make_async_copy(source.at[:, cols], buffers.at[index, :, cols], sems.at[index * 4 + part]))
    for copy in fixed + copies:
        copy.start()
    for copy in fixed:
        copy.wait()
    sends = []
    for index in range(2):
        for part in range(4):
            cols = slice(part * step, (part + 1) * step)
            copies[index * 4 + part].wait()
            tiles = [
                dot(small[...], buffers[index, i * 2 * BLOCK : (i + 1) * 2 * BLOCK, cols]) for i in range(UNITS // 2)
            ]
            offset = 0
            for level in range(FIRST, min(levels, 6) + 1):
                rows = 2 * BLOCK >> level
                both = jnp.concatenate([tile[offset : offset + rows] for tile in tiles], axis=0)
                outs[level - FIRST][index, :, cols] = both.astype(jnp.bfloat16)
                offset += rows
            if levels > 6:
                rest = dot(large[...], buffers[index, :, cols])
                for level in range(7, levels + 1):
                    start = (level - 7) * 8
                    outs[level - FIRST][index, :, cols] = rest[start : start + (TOK >> level)].astype(jnp.bfloat16)
        for place, (out, target) in enumerate(zip(outs, targets)):
            sends.append(pltpu.make_async_copy(out.at[index], target.at[index], out_sems.at[index, place]))
            sends[-1].start()
    for send in sends:
        send.wait()


def pool_call(keys, values, levels):
    small = as_bf16(padded(np.concatenate([natural_pool(level, 2 * BLOCK) for level in range(FIRST, min(levels, 6) + 1)]), 16))
    parts = [padded(natural_pool(level, TOK), 8) for level in range(7, levels + 1)] + [np.zeros((8, TOK))]
    large = as_bf16(padded(np.concatenate(parts), 16))
    crossing = range(FIRST, levels + 1)
    return pl.pallas_call(
        functools.partial(pool_kernel, levels),
        in_specs=[HBM] * 4,
        out_specs=[HBM] * len(crossing),
        out_shape=[jax.ShapeDtypeStruct((2, TOK >> level, WIDTH), jnp.bfloat16) for level in crossing],
        scratch_shapes=[
            pltpu.VMEM(small.shape, jnp.bfloat16),
            pltpu.VMEM(large.shape, jnp.bfloat16),
            pltpu.VMEM((2, TOK, WIDTH), jnp.bfloat16),
        ]
        + [pltpu.VMEM((2, TOK >> level, WIDTH), jnp.bfloat16) for level in crossing]
        + [
            pltpu.SemaphoreType.DMA((10,)),
            pltpu.SemaphoreType.DMA((2, len(crossing))),
        ],
        compiler_params=pltpu.CompilerParams(vmem_limit_bytes=VMEM_CLAIM),
        cost_estimate=pl.CostEstimate(flops=2 * 256 * 512 * 4096, bytes_accessed=6 * MIB, transcendentals=0),
        name="pool_keys_values",
    )(small, large, keys, values)


def far_offsets(levels):
    offsets, total = {}, 0
    for level in range(FIRST, levels + 1):
        offsets[level] = total
        total += UNITS * count_of(level)
    return offsets, total


def near_kernel(levels, first, pool_ref, q_ref, k_ref, v_ref, num_out, stat_out, far_out, *scratch):
    (pool, q, k, v, num, stat, far, ordered, coarse_q, coarse_k, coarse_v, bias, scores_a, scores_b, scores_c) = scratch[:15]
    probs_a, probs_b, probs_c, sems = scratch[15:]
    heads = HEADS // SLICES
    width = heads * HEAD
    cols = slice(first * HEAD, first * HEAD + width)
    copies = [pltpu.make_async_copy(pool_ref, pool, sems.at[0])]
    copies += [
        pltpu.make_async_copy(source.at[:, cols], target, sems.at[1 + index])
        for index, (source, target) in enumerate(((q_ref, q), (k_ref, k), (v_ref, v)))
    ]
    for copy in copies:
        copy.start()
    position = lax.broadcasted_iota(jnp.int32, (BLOCK, BLOCK), 0)
    column = lax.broadcasted_iota(jnp.int32, (BLOCK, BLOCK), 1)
    bias[...] = jnp.where(column <= token_of(position), 0.0, NEG)
    stat[...] = jnp.zeros_like(stat)
    for copy in copies:
        copy.wait()

    far_parts = []
    for unit in range(UNITS):
        pooled = dot(pool[...], q[unit * BLOCK : (unit + 1) * BLOCK, :])
        ordered[unit] = pooled[:BLOCK].astype(jnp.bfloat16)
        if unit >= 2:
            coarse_q[unit - 2] = pooled[BLOCK : BLOCK + 128].astype(jnp.bfloat16)
        far_parts.append(pooled[BLOCK + 128 :])
    offsets, _ = far_offsets(levels)
    start = 0
    for level in range(FIRST, levels + 1):
        count = count_of(level)
        parts = [item[start : start + count].reshape(count // 8, 1, 8, width) for item in far_parts]
        both = jnp.concatenate(parts, axis=1).reshape(UNITS * count, width)
        far[offsets[level] : offsets[level] + UNITS * count, :] = both.astype(jnp.bfloat16)
        start += count
    for unit in range(2):
        rows = slice(unit * BLOCK, (unit + 1) * BLOCK)
        half = slice(unit * 128, (unit + 1) * 128)
        coarse_k[half, :] = dot(pool[BLOCK : BLOCK + 128, :], k[rows, :]).astype(jnp.bfloat16)
        coarse_v[half, :] = dot(pool[BLOCK : BLOCK + 128, :], v[rows, :]).astype(jnp.bfloat16)
    sends = [pltpu.make_async_copy(far, far_out, sems.at[4])]
    sends[0].start()

    lane = lax.broadcasted_iota(jnp.int32, (BLOCK, HEAD), 1)

    def one_head(head, carry):
        own = pl.ds(pl.multiple_of(head * HEAD, HEAD), HEAD)

        def dots(tile):
            rows_a = slice(2 * tile * BLOCK, (2 * tile + 1) * BLOCK)
            rows_b = slice((2 * tile + 1) * BLOCK, (2 * tile + 2) * BLOCK)
            both = ordered[2 * tile : 2 * tile + 2, :, own].reshape(2 * BLOCK, HEAD)
            scores_a[tile] = dot_t(both, k[rows_a, own])
            scores_b[tile] = dot_t(ordered[2 * tile + 1, :, own], k[rows_b, own])

        def soft(tile):
            first_half = soft_rows([scores_a.at[tile, :BLOCK]], [probs_a.at[tile, :BLOCK]], [bias], BLOCK, 64)
            second_half = soft_rows(
                [scores_a.at[tile, BLOCK:], scores_b.at[tile]],
                [probs_a.at[tile, BLOCK:], probs_b.at[tile]],
                [None, bias],
                BLOCK,
                64,
            )
            return first_half, second_half

        def weigh(tile, stats):
            rows_a = slice(2 * tile * BLOCK, (2 * tile + 1) * BLOCK)
            rows_b = slice((2 * tile + 1) * BLOCK, (2 * tile + 2) * BLOCK)
            both = dot(probs_a[tile], v[rows_a, own])
            more = dot(probs_b[tile], v[rows_b, own])
            return (both[:BLOCK],) + stats[0], (both[BLOCK:] + more,) + stats[1]

        def finish(unit, state):
            num[:, unit, :, own] = state[0].reshape(BLOCK // 8, 8, HEAD)
            old = stat[:, unit].reshape(BLOCK, HEAD)
            old = jnp.where(lane == first + head, state[1], old)
            old = jnp.where(lane == first + head + HEADS, state[2], old)
            stat[:, unit] = old.reshape(BLOCK // 8, 8, HEAD)

        dots(0)
        scores_c[...] = dot_t(coarse_q[:, :, own].reshape(BLOCK, HEAD), coarse_k[:, own])
        dots(1)
        stats0 = soft(0)
        states = weigh(0, stats0)
        peak1, total1 = soft_rows([scores_c], [probs_c], [None], BLOCK, 64)
        stats1 = soft(1)
        num1 = 2.0 * dot(probs_c[...], coarse_v[:, own])
        total1 = 2.0 * total1
        states = states + weigh(1, stats1)
        for unit in range(UNITS):
            state = states[unit]
            if unit >= 2:
                half = slice((unit - 2) * 128, (unit - 1) * 128)
                state = merge(state, (twice(num1[half]), twice(peak1[half]), twice(total1[half])))
            finish(unit, state)
        return carry

    lax.fori_loop(0, heads, one_head, 0)
    sends += [pltpu.make_async_copy(num, num_out, sems.at[5]), pltpu.make_async_copy(stat, stat_out, sems.at[6])]
    for send in sends[1:]:
        send.start()
    for send in sends:
        send.wait()


def near_call(queries, keys, values, levels, index):
    pool = as_bf16(padded(np.concatenate([pool_rows(level) for level in range(levels + 1)]), 16))
    heads = HEADS // SLICES
    width = heads * HEAD
    _, far_rows = far_offsets(levels)
    bf16, f32 = jnp.bfloat16, jnp.float32
    return pl.pallas_call(
        functools.partial(near_kernel, levels, index * heads),
        in_specs=[HBM] * 4,
        out_specs=[HBM] * 3,
        out_shape=[
            jax.ShapeDtypeStruct((BLOCK // 8, UNITS, 8, width), f32),
            jax.ShapeDtypeStruct((BLOCK // 8, UNITS, 8, HEAD), f32),
            jax.ShapeDtypeStruct((far_rows, width), bf16),
        ],
        scratch_shapes=[
            pltpu.VMEM(pool.shape, bf16),
            pltpu.VMEM((TOK, width), bf16),
            pltpu.VMEM((TOK, width), bf16),
            pltpu.VMEM((TOK, width), bf16),
            pltpu.VMEM((BLOCK // 8, UNITS, 8, width), f32),
            pltpu.VMEM((BLOCK // 8, UNITS, 8, HEAD), f32),
            pltpu.VMEM((far_rows, width), bf16),
            pltpu.VMEM((UNITS, BLOCK, width), bf16),
            pltpu.VMEM((2, 128, width), bf16),
            pltpu.VMEM((BLOCK, width), bf16),
            pltpu.VMEM((BLOCK, width), bf16),
            pltpu.VMEM((BLOCK, BLOCK), f32),
            pltpu.VMEM((2, 2 * BLOCK, BLOCK), f32),
            pltpu.VMEM((2, BLOCK, BLOCK), f32),
            pltpu.VMEM((BLOCK, BLOCK), f32),
            pltpu.VMEM((2, 2 * BLOCK, BLOCK), bf16),
            pltpu.VMEM((2, BLOCK, BLOCK), bf16),
            pltpu.VMEM((BLOCK, BLOCK), bf16),
            pltpu.SemaphoreType.DMA((7,)),
        ],
        compiler_params=pltpu.CompilerParams(vmem_limit_bytes=VMEM_CLAIM),
        cost_estimate=pl.CostEstimate(flops=2_000_000_000, bytes_accessed=4 * MIB, transcendentals=1_000_000),
        name="near_levels",
    )(pool, queries, keys, values)


def far_kernel(levels, plan, flags_ref, *refs):
    crossing = range(FIRST, levels + 1)
    bundles = 1 + max(bundle for _, bundle, _ in plan)
    kv_refs = refs[:bundles]
    refs = refs[bundles:]
    far_refs, num_refs, stat_refs = refs[:SLICES], refs[SLICES : 2 * SLICES], refs[2 * SLICES : 3 * SLICES]
    turn_ref, w_ref, out_ref = refs[3 * SLICES : 3 * SLICES + 3]
    kv, queries, num, stat, turn, weights, scores, probs = refs[3 * SLICES + 3 : 3 * SLICES + 11]
    wide, peaks, totals, mixed, natural, stage, kv_sems, near_sems, out_sems = refs[3 * SLICES + 11 :]
    heads = HEADS // SLICES
    width = heads * HEAD
    model = w_ref.shape[1]
    step = 512
    offsets, far_rows = far_offsets(levels)

    def kv_copies(index):
        cols = pl.ds(pl.multiple_of(index * width, width), width)
        made = []
        for number, (level, bundle, spans) in enumerate(plan):
            source_start, target_start, rows = spans
            made.append(
                pltpu.make_async_copy(
                    kv_refs[bundle].at[:, source_start : source_start + rows, cols],
                    kv.at[level - FIRST, :, target_start : target_start + rows, cols],
                    kv_sems.at[index, number],
                )
            )
        return made

    near_copies = []
    for index in range(SLICES):
        cols = slice(index * width, (index + 1) * width)
        near_copies.append(pltpu.make_async_copy(far_refs[index], queries.at[:, cols], near_sems.at[index]))
    for index in range(SLICES):
        cols = slice(index * width, (index + 1) * width)
        near_copies.append(pltpu.make_async_copy(num_refs[index], num.at[:, :, :, cols], near_sems.at[SLICES + index]))
    for index in range(SLICES):
        near_copies.append(pltpu.make_async_copy(stat_refs[index], stat.at[index], near_sems.at[2 * SLICES + index]))
    near_copies.append(pltpu.make_async_copy(turn_ref, turn, near_sems.at[3 * SLICES]))
    near_copies.append(pltpu.make_async_copy(w_ref, weights, near_sems.at[3 * SLICES + 1]))
    for copy in near_copies[:SLICES]:
        copy.start()
    for index in range(SLICES):
        for copy in kv_copies(index):
            copy.start()
    for copy in near_copies[SLICES:]:
        copy.start()
    for copy in near_copies[:SLICES]:
        copy.wait()

    rows2 = UNITS * count_of(FIRST)
    lane = lax.broadcasted_iota(jnp.int32, (rows2, HEAD), 1)
    peaks[...] = jnp.full_like(peaks, NEG)
    totals[...] = jnp.zeros_like(totals)

    def group(index, carry):
        for copy in kv_copies(index):
            copy.wait()
        stats = []
        for inner in range(heads):
            own = pl.ds(pl.multiple_of(index * width + inner * HEAD, HEAD), HEAD)
            for level in crossing:
                span = slice(offsets[level], offsets[level] + UNITS * count_of(level))
                scores[inner, span, :] = dot_t(queries[span, own], kv[level - FIRST, 0, :, own])
        for inner in range(heads):
            stats.append(soft_rows([scores.at[inner]], [probs.at[inner]], [None], far_rows, 64))
        for inner in range(heads):
            own = pl.ds(pl.multiple_of(index * width + inner * HEAD, HEAD), HEAD)
            state = None
            for level in reversed(crossing):
                span = slice(offsets[level], offsets[level] + UNITS * count_of(level))
                live = flags_ref[level - FIRST] == 1
                factor = jnp.where(live, 2.0**level, 0.0)
                term = (
                    factor * dot(probs[inner, span, :], kv[level - FIRST, 1, :, own]),
                    jnp.where(live, stats[inner][0][span], NEG),
                    factor * stats[inner][1][span],
                )
                if state is None:
                    state = term
                else:
                    if count_of(level) > count_of(level + 1):
                        state = tuple(twice(item) for item in state)
                    state = merge(state, term)
            wide[:, :, :, own] = state[0].reshape(rows2 // (8 * UNITS), UNITS, 8, HEAD)
            head = index * heads + inner
            peaks[...] = jnp.where(lane == head, state[1], peaks[...])
            totals[...] = jnp.where(lane == head, state[2], totals[...])
        return carry

    lax.fori_loop(0, SLICES, group, 0)

    for copy in near_copies[SLICES:]:
        copy.wait()

    def widened(array, unit):
        array = array.reshape(rows2 // (8 * UNITS), UNITS, 8, HEAD)[:, unit]
        return twice(twice(array.reshape(rows2 // UNITS, HEAD)))

    def mix(unit):
        near = sum(stat[index, :, unit] for index in range(SLICES)).reshape(BLOCK, HEAD)
        near_total = pltpu.roll(near, HEAD - HEADS, 1)
        far_peak = widened(peaks[...], unit)
        far_total = widened(totals[...], unit)
        top = jnp.maximum(near, far_peak)
        a = jnp.exp(near - top)
        b = jnp.exp(far_peak - top)
        inverse = 1.0 / (a * near_total + b * far_total)
        a = a * inverse
        b = b * inverse
        for head in range(HEADS):
            own = slice(head * HEAD, (head + 1) * HEAD)
            far_num = twice(twice(wide[:, unit, :, own].reshape(rows2 // UNITS, HEAD)))
            near_num = num[:, unit, :, own].reshape(BLOCK, HEAD)
            both = a[:, head : head + 1] * near_num + b[:, head : head + 1] * far_num
            mixed[unit, :, own] = both.astype(jnp.bfloat16)
        natural[unit * BLOCK : (unit + 1) * BLOCK, :] = dot(turn[...], mixed[unit]).astype(jnp.bfloat16)

    sends = []

    def project(half):
        rows = slice(half * 2 * BLOCK, (half + 1) * 2 * BLOCK)
        for index in range(model // step):
            cols = slice(index * step, (index + 1) * step)
            stage[rows, cols] = dot(natural[rows, :], weights[:, cols]).astype(jnp.bfloat16)
            sends.append(
                pltpu.make_async_copy(stage.at[rows, cols], out_ref.at[rows, cols], out_sems.at[half * (model // step) + index])
            )
            sends[-1].start()

    mix(0)
    mix(1)
    project(0)
    mix(2)
    mix(3)
    project(1)
    for send in sends:
        send.wait()


def far_call(flags, bundles, plan, near, w_out, levels):
    turn = np.zeros((BLOCK, BLOCK))
    turn[token_of(np.arange(BLOCK)), np.arange(BLOCK)] = 1.0
    nums, stats, fars = [[item[place] for item in near] for place in range(3)]
    model = w_out.shape[1]
    _, far_rows = far_offsets(levels)
    count = levels - FIRST + 1
    heads = HEADS // SLICES
    rows2 = UNITS * count_of(FIRST)
    bf16, f32 = jnp.bfloat16, jnp.float32
    return pl.pallas_call(
        functools.partial(far_kernel, levels, plan),
        in_specs=[pl.BlockSpec(memory_space=pltpu.SMEM)]
        + [pl.BlockSpec(memory_space=pl.ANY)] * len(bundles)
        + [HBM] * (3 * SLICES + 2),
        out_specs=HBM,
        out_shape=jax.ShapeDtypeStruct((TOK, model), bf16),
        scratch_shapes=[
            pltpu.VMEM((count, 2, BLOCK, WIDTH), bf16),
            pltpu.VMEM((far_rows, WIDTH), bf16),
            pltpu.VMEM((BLOCK // 8, UNITS, 8, WIDTH), f32),
            pltpu.VMEM((SLICES, BLOCK // 8, UNITS, 8, HEAD), f32),
            pltpu.VMEM((BLOCK, BLOCK), bf16),
            pltpu.VMEM((WIDTH, model), bf16),
            pltpu.VMEM((heads, far_rows, BLOCK), f32),
            pltpu.VMEM((heads, far_rows, BLOCK), bf16),
            pltpu.VMEM((rows2 // (8 * UNITS), UNITS, 8, WIDTH), f32),
            pltpu.VMEM((rows2, HEAD), f32),
            pltpu.VMEM((rows2, HEAD), f32),
            pltpu.VMEM((UNITS, BLOCK, WIDTH), bf16),
            pltpu.VMEM((TOK, WIDTH), bf16),
            pltpu.VMEM((TOK, model), bf16),
            pltpu.SemaphoreType.DMA((SLICES, len(plan))),
            pltpu.SemaphoreType.DMA((3 * SLICES + 2,)),
            pltpu.SemaphoreType.DMA((2 * model // 512,)),
        ],
        compiler_params=pltpu.CompilerParams(vmem_limit_bytes=VMEM_CLAIM),
        cost_estimate=pl.CostEstimate(flops=6_500_000_000, bytes_accessed=18 * MIB, transcendentals=3_000_000),
        name="far_levels_projection",
    )(flags, *bundles, *fars, *nums, *stats, as_bf16(turn), w_out)


def moved(array, distance, upper_of=0):
    size = lax.axis_size("seq")
    pairs = [(i ^ distance, i) for i in range(size) if not upper_of or i & upper_of]
    return lax.ppermute(array, "seq", pairs)


def gathered(blocks, distance):
    sent = jnp.concatenate(blocks, axis=1) if len(blocks) > 1 else blocks[0]
    got = moved(sent, distance)
    joined, start = [], 0
    for block in blocks:
        rows = block.shape[1]
        joined.append(jnp.concatenate([block, got[:, start : start + rows]], axis=1))
        start += rows
    return joined


def after(arrays, others):
    return lax.optimization_barrier((arrays, others))[0]


def on_device(queries, keys, values, w_out):
    size = lax.axis_size("seq")
    levels = (TOK * size // (2 * BLOCK)).bit_length() - 1
    position = lax.axis_index("seq")
    flags = jnp.stack([(position >> (level - FIRST)) & 1 for level in range(FIRST, levels + 1)]).astype(jnp.int32)
    pooled = pool_call(keys, values, levels)
    blocks = {}
    for level in range(levels, FIRST - 1, -1):
        distance = 1 << (level - FIRST)
        blocks[level] = moved(pooled[level - FIRST], distance, distance)
    high = list(range(5, levels + 1))
    near = []
    for index in range(SLICES):
        source = after(queries, near[-1] if near else pooled)
        near.append(near_call(source, keys, values, levels, index))
    rounds = [1 << bit for bit in range(1, levels - FIRST)]
    for number, distance in enumerate(rounds):
        members = [level for level in high if (1 << (level - FIRST)) > distance]
        if members:
            items = after([blocks[level] for level in members], near[min(number, SLICES - 1)])
            for level, item in zip(members, gathered(items, distance)):
                blocks[level] = item
        if distance == 2:
            blocks[4] = gathered([after(blocks[4], near[min(1, SLICES - 1)])], 2)[0]
    low = jnp.concatenate([after(blocks[3], near[2]), blocks[4]], axis=1)
    low_got = moved(low, 1)
    top = jnp.concatenate([after(blocks[level], near[SLICES - 1]) for level in high], axis=1)
    top_got = moved(top, 1)
    plan = [(2, 0, (0, 0, BLOCK))]
    for place, level in enumerate((3, 4)):
        plan += [(level, 1, (place * 128, 0, 128)), (level, 2, (place * 128, 128, 128))]
    for place, level in enumerate(high):
        plan += [(level, 3, (place * 128, 0, 128)), (level, 4, (place * 128, 128, 128))]
    return far_call(flags, [blocks[2], low, low_got, top, top_got], plan, near, w_out, levels)


def solution(mesh):
    return jax.shard_map(
        on_device,
        mesh=mesh,
        in_specs=(P("seq", None), P("seq", None), P("seq", None), P()),
        out_specs=P("seq", None),
        check_vma=False,
    )
```

```python
import functools

import jax
import jax.numpy as jnp
import numpy as np
from jax import lax
from jax.experimental import pallas as pl
from jax.experimental.pallas import tpu as pltpu
from jax.sharding import PartitionSpec as P

HEADS = 8
HEAD = 128
BLOCK = 256
TOK = 1024
UNITS = TOK // BLOCK
WIDTH = HEADS * HEAD
NEG = -1e30
FIRST = 2
SCALE = HEAD**-0.5
LOG2E = 1.4426950408889634
MIB = 1 << 20
SLICES = 2
VMEM_CLAIM = 60 * MIB
HBM = pl.BlockSpec(memory_space=pltpu.HBM)


def token_of(position):
    return ((position & 31) << 3) | (((position >> 5) & 1) << 2) | (((position >> 6) & 1) << 1) | (position >> 7)


def count_of(level):
    return max(BLOCK >> level, 32)


def pool_rows(level):
    rows = token_of(np.arange(count_of(level))) >> level
    columns = np.arange(BLOCK) >> level
    return (rows[:, None] == columns[None, :]) * 2.0**-level


def natural_pool(level, span):
    rows = np.arange(span >> level)
    return (rows[:, None] == (np.arange(span) >> level)[None, :]) * 2.0**-level


def padded(array, multiple):
    return np.pad(array, ((0, -len(array) % multiple), (0, 0)))


def as_bf16(array):
    return jnp.asarray(array.astype(np.float32)).astype(jnp.bfloat16)


def dot(a, b):
    return jnp.dot(a, b, preferred_element_type=jnp.float32)


def dot_t(a, b):
    return lax.dot_general(a, b, (((1,), (1,)), ((), ())), preferred_element_type=jnp.float32)


def dot_first(a, b):
    return lax.dot_general(a, b, (((0,), (0,)), ((), ())), preferred_element_type=jnp.float32)


def merge(first, second):
    top = jnp.maximum(first[1], second[1])
    a = jnp.exp(first[1] - top)
    b = jnp.exp(second[1] - top)
    return (a * first[0] + b * second[0], top, a * first[2] + b * second[2])


ROWS = 64


def soft_columns(loads, targets):
    spans = [slice(start, start + ROWS) for start in range(0, BLOCK, ROWS)]
    peak = None
    for load in loads:
        for span in spans:
            rows = jnp.max(load(span).reshape(ROWS // 8, 8, HEAD), axis=0)
            peak = rows if peak is None else jnp.maximum(peak, rows)
    peak = jnp.max(peak, axis=0, keepdims=True)
    total = jnp.zeros((8, HEAD), jnp.float32)
    for load, target in zip(loads, targets):
        for span in spans:
            probs = jnp.exp2((load(span) - peak) * (SCALE * LOG2E))
            total = total + jnp.sum(probs.reshape(ROWS // 8, 8, HEAD), axis=0)
            target[span, :] = probs.astype(jnp.bfloat16)
    return peak * SCALE, jnp.sum(total, axis=0, keepdims=True)


def pool_kernel(levels, small_ref, large_ref, keys_ref, values_ref, *refs):
    count = levels - FIRST + 1
    targets, (small, large, buffers, *outs, sems, out_sems) = refs[:count], refs[count:]
    step = WIDTH // 4
    fixed = [pltpu.make_async_copy(small_ref, small, sems.at[8]), pltpu.make_async_copy(large_ref, large, sems.at[9])]
    copies = []
    for index, source in enumerate((keys_ref, values_ref)):
        for part in range(4):
            cols = slice(part * step, (part + 1) * step)
            copies.append(pltpu.make_async_copy(source.at[:, cols], buffers.at[index, :, cols], sems.at[index * 4 + part]))
    for copy in fixed + copies:
        copy.start()
    for copy in fixed:
        copy.wait()
    sends = []
    for index in range(2):
        for part in range(4):
            cols = slice(part * step, (part + 1) * step)
            copies[index * 4 + part].wait()
            tiles = [
                dot(small[...], buffers[index, i * 2 * BLOCK : (i + 1) * 2 * BLOCK, cols]) for i in range(UNITS // 2)
            ]
            offset = 0
            for level in range(FIRST, min(levels, 6) + 1):
                rows = 2 * BLOCK >> level
                both = jnp.concatenate([tile[offset : offset + rows] for tile in tiles], axis=0)
                outs[level - FIRST][index, :, cols] = both.astype(jnp.bfloat16)
                offset += rows
            if levels > 6:
                rest = dot(large[...], buffers[index, :, cols])
                for level in range(7, levels + 1):
                    start = (level - 7) * 8
                    outs[level - FIRST][index, :, cols] = rest[start : start + (TOK >> level)].astype(jnp.bfloat16)
        for place, (out, target) in enumerate(zip(outs, targets)):
            sends.append(pltpu.make_async_copy(out.at[index], target.at[index], out_sems.at[index, place]))
            sends[-1].start()
    for send in sends:
        send.wait()


def pool_call(keys, values, levels):
    small = as_bf16(padded(np.concatenate([natural_pool(level, 2 * BLOCK) for level in range(FIRST, min(levels, 6) + 1)]), 16))
    parts = [padded(natural_pool(level, TOK), 8) for level in range(7, levels + 1)] + [np.zeros((8, TOK))]
    large = as_bf16(padded(np.concatenate(parts), 16))
    crossing = range(FIRST, levels + 1)
    return pl.pallas_call(
        functools.partial(pool_kernel, levels),
        in_specs=[HBM] * 4,
        out_specs=[HBM] * len(crossing),
        out_shape=[jax.ShapeDtypeStruct((2, TOK >> level, WIDTH), jnp.bfloat16) for level in crossing],
        scratch_shapes=[
            pltpu.VMEM(small.shape, jnp.bfloat16),
            pltpu.VMEM(large.shape, jnp.bfloat16),
            pltpu.VMEM((2, TOK, WIDTH), jnp.bfloat16),
        ]
        + [pltpu.VMEM((2, TOK >> level, WIDTH), jnp.bfloat16) for level in crossing]
        + [
            pltpu.SemaphoreType.DMA((10,)),
            pltpu.SemaphoreType.DMA((2, len(crossing))),
        ],
        compiler_params=pltpu.CompilerParams(vmem_limit_bytes=VMEM_CLAIM),
        cost_estimate=pl.CostEstimate(flops=2 * 256 * 512 * 4096, bytes_accessed=6 * MIB, transcendentals=0),
        name="pool_keys_values",
    )(small, large, keys, values)


def far_offsets(levels):
    offsets, total = {}, 0
    for level in range(FIRST, levels + 1):
        offsets[level] = total
        total += UNITS * count_of(level)
    return offsets, total


def lane_block(index):
    return slice(index * HEAD, (index + 1) * HEAD)


def near_kernel(levels, first, pool_ref, q_ref, k_ref, v_ref, num_out, stat_out, far_out, *scratch):
    (pool, q, k, v, num, stat, far, ordered, coarse_q, coarse_k, coarse_v, bias, scores_a, scores_b, scores_c) = scratch[:15]
    probs_a, probs_b, probs_c, sems, head_sems = scratch[15:]
    heads = HEADS // SLICES
    width = heads * HEAD
    cols = slice(first * HEAD, first * HEAD + width)
    copies = [
        pltpu.make_async_copy(pool_ref, pool, sems.at[0]),
        pltpu.make_async_copy(q_ref.at[:, cols], q, sems.at[1]),
        pltpu.make_async_copy(k_ref.at[:, cols], k, sems.at[2]),
        pltpu.make_async_copy(v_ref.at[:, cols], v, sems.at[3]),
    ]
    for copy in copies:
        copy.start()
    row = lax.broadcasted_iota(jnp.int32, (BLOCK, BLOCK), 0)
    position = lax.broadcasted_iota(jnp.int32, (BLOCK, BLOCK), 1)
    bias[...] = jnp.where(row <= token_of(position), 0.0, NEG)
    copies[0].wait()
    copies[1].wait()

    offsets, _ = far_offsets(levels)
    for unit in range(UNITS):
        pooled = dot(pool[...], q[unit * BLOCK : (unit + 1) * BLOCK, :])
        ordered[unit * BLOCK : (unit + 1) * BLOCK, :] = pooled[:BLOCK].astype(jnp.bfloat16)
        if unit >= 2:
            coarse_q[(unit - 2) * 128 : (unit - 1) * 128, :] = pooled[BLOCK : BLOCK + 128].astype(jnp.bfloat16)
        start = BLOCK + 128
        for level in range(FIRST, levels + 1):
            count = count_of(level)
            place = offsets[level] + unit * count
            far[place : place + count, :] = pooled[start : start + count].astype(jnp.bfloat16)
            start += count
    sends = [pltpu.make_async_copy(far, far_out, sems.at[4])]
    sends[0].start()
    copies[2].wait()
    copies[3].wait()
    for unit in range(2):
        rows = slice(unit * BLOCK, (unit + 1) * BLOCK)
        half = slice(unit * 128, (unit + 1) * 128)
        coarse_k[half, :] = dot(pool[BLOCK : BLOCK + 128, :], k[rows, :]).astype(jnp.bfloat16)
        coarse_v[half, :] = dot(pool[BLOCK : BLOCK + 128, :], v[rows, :]).astype(jnp.bfloat16)

    def num_copy(head):
        rows = pl.ds(pl.multiple_of(head * HEAD, HEAD), HEAD)
        return pltpu.make_async_copy(num.at[rows, :], num_out.at[rows, :], head_sems.at[head])

    def one_head(head, carry):
        own = pl.ds(pl.multiple_of(head * HEAD, HEAD), HEAD)

        def dots(tile):
            base = 2 * tile * BLOCK
            both = ordered[base : base + 2 * BLOCK, own]
            scores_a[tile] = dot_t(k[base : base + BLOCK, own], both)
            scores_b[tile] = dot_t(k[base + BLOCK : base + 2 * BLOCK, own], ordered[base + BLOCK : base + 2 * BLOCK, own])

        def soft(tile):
            stats = []
            for block in range(2):
                lanes = lane_block(block)
                stats.append(
                    soft_columns(
                        [lambda span: scores_a[tile, span, lanes] + bias[span, lanes]], [probs_a.at[tile, :, lanes]]
                    )
                )
            for block in range(2):
                lanes, late = lane_block(block), lane_block(2 + block)
                stats.append(
                    soft_columns(
                        [
                            lambda span: scores_a[tile, span, late],
                            lambda span: scores_b[tile, span, lanes] + bias[span, lanes],
                        ],
                        [probs_a.at[tile, :, late], probs_b.at[tile, :, lanes]],
                    )
                )
            return stats

        def weigh(tile, stats):
            base = 2 * tile * BLOCK
            both = dot_first(v[base : base + BLOCK, own], probs_a[tile])
            more = dot_first(v[base + BLOCK : base + 2 * BLOCK, own], probs_b[tile])
            nums = [both[:, lane_block(0)], both[:, lane_block(1)]]
            nums += [both[:, lane_block(2 + block)] + more[:, lane_block(block)] for block in range(2)]
            return [(item,) + pair for item, pair in zip(nums, stats)]

        dots(0)
        scores_c[...] = dot_t(coarse_k[:, own], coarse_q[:, own])
        dots(1)
        stats0 = soft(0)
        states = weigh(0, stats0)
        stats_c = [
            soft_columns([lambda span: scores_c[span, lane_block(block)]], [probs_c.at[:, lane_block(block)]])
            for block in range(2)
        ]
        stats1 = soft(1)
        num_c = 2.0 * dot_first(coarse_v[:, own], probs_c[...])
        late = weigh(1, stats1)
        for block, state in enumerate(late):
            unit = block // 2
            coarse = (num_c[:, lane_block(unit)], stats_c[unit][0], 2.0 * stats_c[unit][1])
            states.append(merge(state, coarse))
        for block, state in enumerate(states):
            num[own, lane_block(block)] = state[0]
            stat[head, 0:1, lane_block(block)] = state[1]
            stat[head, 1:2, lane_block(block)] = state[2]
        num_copy(head).start()
        return carry

    lax.fori_loop(0, heads, one_head, 0)
    sends.append(pltpu.make_async_copy(stat, stat_out, sems.at[5]))
    sends[-1].start()
    for send in sends:
        send.wait()
    for head in range(heads):
        num_copy(head).wait()


def near_call(queries, keys, values, levels, index):
    pool = as_bf16(padded(np.concatenate([pool_rows(level) for level in range(levels + 1)]), 16))
    heads = HEADS // SLICES
    width = heads * HEAD
    _, far_rows = far_offsets(levels)
    bf16, f32 = jnp.bfloat16, jnp.float32
    return pl.pallas_call(
        functools.partial(near_kernel, levels, index * heads),
        in_specs=[HBM] * 4,
        out_specs=[HBM] * 3,
        out_shape=[
            jax.ShapeDtypeStruct((width, TOK), f32),
            jax.ShapeDtypeStruct((heads, 8, TOK), f32),
            jax.ShapeDtypeStruct((far_rows, width), bf16),
        ],
        scratch_shapes=[
            pltpu.VMEM(pool.shape, bf16),
            pltpu.VMEM((TOK, width), bf16),
            pltpu.VMEM((TOK, width), bf16),
            pltpu.VMEM((TOK, width), bf16),
            pltpu.VMEM((width, TOK), f32),
            pltpu.VMEM((heads, 8, TOK), f32),
            pltpu.VMEM((far_rows, width), bf16),
            pltpu.VMEM((TOK, width), bf16),
            pltpu.VMEM((BLOCK, width), bf16),
            pltpu.VMEM((BLOCK, width), bf16),
            pltpu.VMEM((BLOCK, width), bf16),
            pltpu.VMEM((BLOCK, BLOCK), f32),
            pltpu.VMEM((2, BLOCK, 2 * BLOCK), f32),
            pltpu.VMEM((2, BLOCK, BLOCK), f32),
            pltpu.VMEM((BLOCK, BLOCK), f32),
            pltpu.VMEM((2, BLOCK, 2 * BLOCK), bf16),
            pltpu.VMEM((2, BLOCK, BLOCK), bf16),
            pltpu.VMEM((BLOCK, BLOCK), bf16),
            pltpu.SemaphoreType.DMA((6,)),
            pltpu.SemaphoreType.DMA((heads,)),
        ],
        compiler_params=pltpu.CompilerParams(vmem_limit_bytes=VMEM_CLAIM),
        cost_estimate=pl.CostEstimate(flops=4_000_000_000, bytes_accessed=8 * MIB, transcendentals=2_000_000),
        name="near_levels",
    )(pool, queries, keys, values)


def by_lane_group(arrays, size):
    lane = lax.broadcasted_iota(jnp.int32, arrays[0].shape, 1)
    result = arrays[-1]
    for index in range(len(arrays) - 2, -1, -1):
        result = jnp.where(lane < (index + 1) * size, arrays[index], result)
    return result


def widen_to_second(array):
    r32, r64, r96 = [pltpu.roll(array, shift, 1) for shift in (32, 64, 96)]
    return [by_lane_group([array, r32, r32, r64], 32), by_lane_group([r64, r96, r96, array], 32)]


def widen_to_units(arrays):
    units = []
    for array in arrays:
        turned = pltpu.roll(array, 64, 1)
        units += [by_lane_group([array, turned], 64), by_lane_group([turned, array], 64)]
    return units


def far_kernel(levels, plan, flags_ref, *refs):
    crossing = range(FIRST, levels + 1)
    bundles = 1 + max(bundle for _, bundle, _ in plan)
    kv_refs = refs[:bundles]
    refs = refs[bundles:]
    far_refs, num_refs, stat_refs = refs[:SLICES], refs[SLICES : 2 * SLICES], refs[2 * SLICES : 3 * SLICES]
    turn_ref, w_ref, out_ref = refs[3 * SLICES : 3 * SLICES + 3]
    kv, queries, num, stat, turn, weights, scores, probs = refs[3 * SLICES + 3 : 3 * SLICES + 11]
    mixed, natural, stage, kv_sems, near_sems, out_sems = refs[3 * SLICES + 11 :]
    heads = HEADS // SLICES
    width = heads * HEAD
    pair = 2 * HEAD
    model = w_ref.shape[1]
    step = 512
    offsets, far_rows = far_offsets(levels)

    def kv_copies(index):
        cols = pl.ds(pl.multiple_of(index * pair, pair), pair)
        made = []
        for number, (level, bundle, spans) in enumerate(plan):
            source_start, target_start, rows = spans
            made.append(
                pltpu.make_async_copy(
                    kv_refs[bundle].at[:, source_start : source_start + rows, cols],
                    kv.at[level - FIRST, :, target_start : target_start + rows, cols],
                    kv_sems.at[index, number],
                )
            )
        return made

    far_copies, near_copies = [], []
    for index in range(SLICES):
        cols = slice(index * width, (index + 1) * width)
        group = slice(index * heads, (index + 1) * heads)
        sems = [near_sems.at[place * SLICES + index] for place in range(3)]
        far_copies.append(pltpu.make_async_copy(far_refs[index], queries.at[:, cols], sems[0]))
        near_copies.append(pltpu.make_async_copy(num_refs[index], num.at[cols, :], sems[1]))
        near_copies.append(pltpu.make_async_copy(stat_refs[index], stat.at[group], sems[2]))
    last_copies = [
        pltpu.make_async_copy(turn_ref, turn, near_sems.at[3 * SLICES]),
        pltpu.make_async_copy(w_ref, weights, near_sems.at[3 * SLICES + 1]),
    ]
    for copy in far_copies + kv_copies(0) + near_copies:
        copy.start()
    for index in range(1, HEADS // 2):
        for copy in kv_copies(index):
            copy.start()
    for copy in last_copies:
        copy.start()
    for copy in far_copies:
        copy.wait()

    def group(index, carry):
        for copy in kv_copies(index):
            copy.wait()
        stats = []
        for inner in range(2):
            own = pl.ds(pl.multiple_of(index * pair + inner * HEAD, HEAD), HEAD)
            for level in crossing:
                span = slice(offsets[level], offsets[level] + UNITS * count_of(level))
                scores[inner, :, span] = dot_t(kv[level - FIRST, 0, :, own], queries[span, own])
        for inner in range(2):
            stats.append(
                [
                    soft_columns(
                        [lambda span: scores[inner, span, lane_block(block)]], [probs.at[inner, :, lane_block(block)]]
                    )
                    for block in range(far_rows // HEAD)
                ]
            )

        @pl.when(index == 0)
        def _():
            for copy in near_copies:
                copy.wait()

        for inner in range(2):
            head = 2 * index + inner
            own = pl.ds(pl.multiple_of(head * HEAD, HEAD), HEAD)
            state = None
            for level in reversed(crossing):
                span = slice(offsets[level], offsets[level] + UNITS * count_of(level))
                live = flags_ref[level - FIRST] == 1
                factor = jnp.where(live, 2.0**level, 0.0)
                weighted = factor * dot_first(kv[level - FIRST, 1, :, own], probs[inner, :, span])
                terms = []
                for block in range(UNITS * count_of(level) // HEAD):
                    peak, total = stats[inner][offsets[level] // HEAD + block]
                    terms.append((weighted[:, lane_block(block)], jnp.where(live, peak, NEG), factor * total))
                if state is None:
                    state = terms
                    continue
                if len(terms) > len(state):
                    wide = [widen_to_second(item) for item in state[0]]
                    state = [tuple(item[side] for item in wide) for side in range(2)]
                state = [merge(old, new) for old, new in zip(state, terms)]
            wide = [widen_to_units([half[place] for half in state]) for place in range(3)]
            for unit in range(UNITS):
                far_num, far_peak, far_total = [item[unit] for item in wide]
                for block in range(2 * unit, 2 * unit + 2):
                    peak = stat[head, 0:1, lane_block(block)]
                    total = stat[head, 1:2, lane_block(block)]
                    top = jnp.maximum(peak, far_peak)
                    a = jnp.exp(peak - top)
                    b = jnp.exp(far_peak - top)
                    inverse = 1.0 / (a * total + b * far_total)
                    both = (a * inverse) * num[own, lane_block(block)] + (b * inverse) * far_num
                    mixed[own, lane_block(block)] = both.astype(jnp.bfloat16)
        return carry

    lax.fori_loop(0, HEADS // 2, group, 0)

    for copy in last_copies:
        copy.wait()
    for unit in range(UNITS):
        rows = slice(unit * BLOCK, (unit + 1) * BLOCK)
        natural[rows, :] = dot_t(turn[...], mixed[:, rows]).astype(jnp.bfloat16)
    sends = []
    for index in range(model // step):
        cols = slice(index * step, (index + 1) * step)
        stage[:, cols] = dot(natural[...], weights[:, cols]).astype(jnp.bfloat16)
        sends.append(pltpu.make_async_copy(stage.at[:, cols], out_ref.at[:, cols], out_sems.at[index]))
        sends[-1].start()
    for send in sends:
        send.wait()


def far_call(flags, bundles, plan, near, w_out, levels):
    turn = np.zeros((BLOCK, BLOCK))
    turn[token_of(np.arange(BLOCK)), np.arange(BLOCK)] = 1.0
    nums, stats, fars = [[item[place] for item in near] for place in range(3)]
    model = w_out.shape[1]
    _, far_rows = far_offsets(levels)
    count = levels - FIRST + 1
    bf16, f32 = jnp.bfloat16, jnp.float32
    return pl.pallas_call(
        functools.partial(far_kernel, levels, plan),
        in_specs=[pl.BlockSpec(memory_space=pltpu.SMEM)] + [HBM] * (len(bundles) + 3 * SLICES + 2),
        out_specs=HBM,
        out_shape=jax.ShapeDtypeStruct((TOK, model), bf16),
        scratch_shapes=[
            pltpu.VMEM((count, 2, BLOCK, WIDTH), bf16),
            pltpu.VMEM((far_rows, WIDTH), bf16),
            pltpu.VMEM((WIDTH, TOK), f32),
            pltpu.VMEM((HEADS, 8, TOK), f32),
            pltpu.VMEM((BLOCK, BLOCK), bf16),
            pltpu.VMEM((WIDTH, model), bf16),
            pltpu.VMEM((2, BLOCK, far_rows), f32),
            pltpu.VMEM((2, BLOCK, far_rows), bf16),
            pltpu.VMEM((WIDTH, TOK), bf16),
            pltpu.VMEM((TOK, WIDTH), bf16),
            pltpu.VMEM((TOK, model), bf16),
            pltpu.SemaphoreType.DMA((HEADS // 2, len(plan))),
            pltpu.SemaphoreType.DMA((3 * SLICES + 2,)),
            pltpu.SemaphoreType.DMA((model // 512,)),
        ],
        compiler_params=pltpu.CompilerParams(vmem_limit_bytes=VMEM_CLAIM),
        cost_estimate=pl.CostEstimate(flops=6_500_000_000, bytes_accessed=18 * MIB, transcendentals=3_000_000),
        name="far_levels_projection",
    )(flags, *bundles, *fars, *nums, *stats, as_bf16(turn), w_out)


def moved(array, distance, upper_of=0):
    size = lax.axis_size("seq")
    pairs = [(i ^ distance, i) for i in range(size) if not upper_of or i & upper_of]
    return lax.ppermute(array, "seq", pairs)


def gathered(blocks, distance):
    sent = jnp.concatenate(blocks, axis=1) if len(blocks) > 1 else blocks[0]
    got = moved(sent, distance)
    joined, start = [], 0
    for block in blocks:
        rows = block.shape[1]
        joined.append(jnp.concatenate([block, got[:, start : start + rows]], axis=1))
        start += rows
    return joined


def after(arrays, others):
    return lax.optimization_barrier((arrays, others))[0]


def on_device(queries, keys, values, w_out):
    size = lax.axis_size("seq")
    levels = (TOK * size // (2 * BLOCK)).bit_length() - 1
    position = lax.axis_index("seq")
    flags = jnp.stack([(position >> (level - FIRST)) & 1 for level in range(FIRST, levels + 1)]).astype(jnp.int32)
    pooled = pool_call(keys, values, levels)
    blocks = {}
    for level in range(levels, FIRST - 1, -1):
        distance = 1 << (level - FIRST)
        blocks[level] = moved(pooled[level - FIRST], distance, distance)
    high = list(range(5, levels + 1))
    near = []
    for index in range(SLICES):
        source = after(queries, (near[-1], [blocks[level] for level in range(4, levels + 1)]) if near else pooled)
        near.append(near_call(source, keys, values, levels, index))
    rounds = [1 << bit for bit in range(1, levels - FIRST)]
    for number, distance in enumerate(rounds):
        members = [level for level in high if (1 << (level - FIRST)) > distance]
        if members:
            items = after([blocks[level] for level in members], near[min(number, SLICES - 1)])
            for level, item in zip(members, gathered(items, distance)):
                blocks[level] = item
        if distance == 2:
            blocks[4] = gathered([after(blocks[4], near[0])], 2)[0]
    low = jnp.concatenate([after(blocks[3], near[SLICES - 1]), blocks[4]], axis=1)
    low_got = moved(low, 1)
    top = jnp.concatenate([blocks[level] for level in high], axis=1)
    top_got = moved(top, 1)
    plan = [(2, 0, (0, 0, BLOCK))]
    for place, level in enumerate((3, 4)):
        plan += [(level, 1, (place * 128, 0, 128)), (level, 2, (place * 128, 128, 128))]
    for place, level in enumerate(high):
        plan += [(level, 3, (place * 128, 0, 128)), (level, 4, (place * 128, 128, 128))]
    return far_call(flags, [blocks[2], low, low_got, top, top_got], plan, near, w_out, levels)


def solution(mesh):
    return jax.shard_map(
        on_device,
        mesh=mesh,
        in_specs=(P("seq", None), P("seq", None), P("seq", None), P()),
        out_specs=P("seq", None),
        check_vma=False,
    )
```

```python
import functools

import jax
import jax.numpy as jnp
import numpy as np
from jax import lax
from jax.experimental import pallas as pl
from jax.experimental.pallas import tpu as pltpu
from jax.sharding import PartitionSpec as P

HEADS = 8
HEAD = 128
BLOCK = 256
TOK = 1024
UNITS = TOK // BLOCK
WIDTH = HEADS * HEAD
NEG = -1e30
FIRST = 2
SCALE = HEAD**-0.5
LOG2E = 1.4426950408889634
MIB = 1 << 20
SLICES = 4
NEAR_FLOPS = 8_000_000_000
VMEM_CLAIM = 60 * MIB
HBM = pl.BlockSpec(memory_space=pltpu.HBM)


def token_of(position):
    return ((position & 31) << 3) | (((position >> 5) & 1) << 2) | (((position >> 6) & 1) << 1) | (position >> 7)


def count_of(level):
    return max(BLOCK >> level, 32)


def pool_rows(level):
    rows = token_of(np.arange(count_of(level))) >> level
    columns = np.arange(BLOCK) >> level
    return (rows[:, None] == columns[None, :]) * 2.0**-level


def natural_pool(level, span):
    rows = np.arange(span >> level)
    return (rows[:, None] == (np.arange(span) >> level)[None, :]) * 2.0**-level


def padded(array, multiple):
    return np.pad(array, ((0, -len(array) % multiple), (0, 0)))


def as_bf16(array):
    return jnp.asarray(array.astype(np.float32)).astype(jnp.bfloat16)


def dot(a, b):
    return jnp.dot(a, b, preferred_element_type=jnp.float32)


def dot_t(a, b):
    return lax.dot_general(a, b, (((1,), (1,)), ((), ())), preferred_element_type=jnp.float32)


def dot_first(a, b):
    return lax.dot_general(a, b, (((0,), (0,)), ((), ())), preferred_element_type=jnp.float32)


def merge(first, second):
    top = jnp.maximum(first[1], second[1])
    a = jnp.exp(first[1] - top)
    b = jnp.exp(second[1] - top)
    return (a * first[0] + b * second[0], top, a * first[2] + b * second[2])


ROWS = 64


def soft_columns(loads, targets):
    spans = [slice(start, start + ROWS) for start in range(0, BLOCK, ROWS)]
    peak = None
    for load in loads:
        for span in spans:
            rows = jnp.max(load(span).reshape(ROWS // 8, 8, HEAD), axis=0)
            peak = rows if peak is None else jnp.maximum(peak, rows)
    peak = jnp.max(peak, axis=0, keepdims=True)
    total = jnp.zeros((8, HEAD), jnp.float32)
    for load, target in zip(loads, targets):
        for span in spans:
            probs = jnp.exp2((load(span) - peak) * (SCALE * LOG2E))
            total = total + jnp.sum(probs.reshape(ROWS // 8, 8, HEAD), axis=0)
            target[span, :] = probs.astype(jnp.bfloat16)
    return peak * SCALE, jnp.sum(total, axis=0, keepdims=True)


def pool_kernel(levels, small_ref, large_ref, keys_ref, values_ref, *refs):
    count = levels - FIRST + 1
    targets, (small, large, buffers, *outs, sems, out_sems) = refs[:count], refs[count:]
    step = WIDTH // 4
    fixed = [pltpu.make_async_copy(small_ref, small, sems.at[8]), pltpu.make_async_copy(large_ref, large, sems.at[9])]
    copies = []
    for index, source in enumerate((keys_ref, values_ref)):
        for part in range(4):
            cols = slice(part * step, (part + 1) * step)
            copies.append(pltpu.make_async_copy(source.at[:, cols], buffers.at[index, :, cols], sems.at[index * 4 + part]))
    for copy in fixed + copies:
        copy.start()
    for copy in fixed:
        copy.wait()
    sends = []
    for index in range(2):
        for part in range(4):
            cols = slice(part * step, (part + 1) * step)
            copies[index * 4 + part].wait()
            tiles = [
                dot(small[...], buffers[index, i * 2 * BLOCK : (i + 1) * 2 * BLOCK, cols]) for i in range(UNITS // 2)
            ]
            offset = 0
            for level in range(FIRST, min(levels, 6) + 1):
                rows = 2 * BLOCK >> level
                both = jnp.concatenate([tile[offset : offset + rows] for tile in tiles], axis=0)
                outs[level - FIRST][index, :, cols] = both.astype(jnp.bfloat16)
                offset += rows
            if levels > 6:
                rest = dot(large[...], buffers[index, :, cols])
                for level in range(7, levels + 1):
                    start = (level - 7) * 8
                    outs[level - FIRST][index, :, cols] = rest[start : start + (TOK >> level)].astype(jnp.bfloat16)
        for place, (out, target) in enumerate(zip(outs, targets)):
            sends.append(pltpu.make_async_copy(out.at[index], target.at[index], out_sems.at[index, place]))
            sends[-1].start()
    for send in sends:
        send.wait()


def pool_call(keys, values, levels):
    small = as_bf16(padded(np.concatenate([natural_pool(level, 2 * BLOCK) for level in range(FIRST, min(levels, 6) + 1)]), 16))
    parts = [padded(natural_pool(level, TOK), 8) for level in range(7, levels + 1)] + [np.zeros((8, TOK))]
    large = as_bf16(padded(np.concatenate(parts), 16))
    crossing = range(FIRST, levels + 1)
    return pl.pallas_call(
        functools.partial(pool_kernel, levels),
        in_specs=[HBM] * 4,
        out_specs=[HBM] * len(crossing),
        out_shape=[jax.ShapeDtypeStruct((2, TOK >> level, WIDTH), jnp.bfloat16) for level in crossing],
        scratch_shapes=[
            pltpu.VMEM(small.shape, jnp.bfloat16),
            pltpu.VMEM(large.shape, jnp.bfloat16),
            pltpu.VMEM((2, TOK, WIDTH), jnp.bfloat16),
        ]
        + [pltpu.VMEM((2, TOK >> level, WIDTH), jnp.bfloat16) for level in crossing]
        + [
            pltpu.SemaphoreType.DMA((10,)),
            pltpu.SemaphoreType.DMA((2, len(crossing))),
        ],
        compiler_params=pltpu.CompilerParams(vmem_limit_bytes=VMEM_CLAIM),
        cost_estimate=pl.CostEstimate(flops=2 * 256 * 512 * 4096, bytes_accessed=6 * MIB, transcendentals=0),
        name="pool_keys_values",
    )(small, large, keys, values)


def far_offsets(levels):
    offsets, total = {}, 0
    for level in range(FIRST, levels + 1):
        offsets[level] = total
        total += UNITS * count_of(level)
    return offsets, total


def lane_block(index):
    return slice(index * HEAD, (index + 1) * HEAD)


def near_kernel(levels, first, pool_ref, q_ref, k_ref, v_ref, num_out, stat_out, far_out, *scratch):
    (pool, q, k, v, num, stat, far, ordered, coarse_q, coarse_k, coarse_v, bias, scores_a, scores_b, scores_c) = scratch[:15]
    probs_a, probs_b, probs_c, sems, head_sems = scratch[15:]
    heads = HEADS // SLICES
    width = heads * HEAD
    cols = slice(first * HEAD, first * HEAD + width)
    copies = [
        pltpu.make_async_copy(pool_ref, pool, sems.at[0]),
        pltpu.make_async_copy(q_ref.at[:, cols], q, sems.at[1]),
        pltpu.make_async_copy(k_ref.at[:, cols], k, sems.at[2]),
        pltpu.make_async_copy(v_ref.at[:, cols], v, sems.at[3]),
    ]
    for copy in copies:
        copy.start()
    row = lax.broadcasted_iota(jnp.int32, (BLOCK, BLOCK), 0)
    position = lax.broadcasted_iota(jnp.int32, (BLOCK, BLOCK), 1)
    bias[...] = jnp.where(row <= token_of(position), 0.0, NEG)
    copies[0].wait()
    copies[1].wait()

    offsets, _ = far_offsets(levels)
    for unit in range(UNITS):
        pooled = dot(pool[...], q[unit * BLOCK : (unit + 1) * BLOCK, :])
        ordered[unit * BLOCK : (unit + 1) * BLOCK, :] = pooled[:BLOCK].astype(jnp.bfloat16)
        if unit >= 2:
            coarse_q[(unit - 2) * 128 : (unit - 1) * 128, :] = pooled[BLOCK : BLOCK + 128].astype(jnp.bfloat16)
        start = BLOCK + 128
        for level in range(FIRST, levels + 1):
            count = count_of(level)
            place = offsets[level] + unit * count
            far[place : place + count, :] = pooled[start : start + count].astype(jnp.bfloat16)
            start += count
    sends = [pltpu.make_async_copy(far, far_out, sems.at[4])]
    sends[0].start()
    copies[2].wait()
    copies[3].wait()
    for unit in range(2):
        rows = slice(unit * BLOCK, (unit + 1) * BLOCK)
        half = slice(unit * 128, (unit + 1) * 128)
        coarse_k[half, :] = dot(pool[BLOCK : BLOCK + 128, :], k[rows, :]).astype(jnp.bfloat16)
        coarse_v[half, :] = dot(pool[BLOCK : BLOCK + 128, :], v[rows, :]).astype(jnp.bfloat16)

    def num_copy(head, tile):
        rows = lane_block(head)
        lanes = slice(tile * 2 * BLOCK, (tile + 1) * 2 * BLOCK)
        return pltpu.make_async_copy(num.at[rows, lanes], num_out.at[rows, lanes], head_sems.at[head, tile])

    def dots(head, tile):
        own, base = lane_block(head), 2 * tile * BLOCK
        both = ordered[base : base + 2 * BLOCK, own]
        scores_a[head, tile] = dot_t(k[base : base + BLOCK, own], both)
        scores_b[head, tile] = dot_t(k[base + BLOCK : base + 2 * BLOCK, own], ordered[base + BLOCK : base + 2 * BLOCK, own])

    def dots_coarse(head):
        own = lane_block(head)
        scores_c[head] = dot_t(coarse_k[:, own], coarse_q[:, own])

    def soft(head, tile):
        stats = []
        for block in range(2):
            lanes = lane_block(block)
            stats.append(
                soft_columns(
                    [lambda span: scores_a[head, tile, span, lanes] + bias[span, lanes]],
                    [probs_a.at[head, tile, :, lanes]],
                )
            )
        for block in range(2):
            lanes, late = lane_block(block), lane_block(2 + block)
            stats.append(
                soft_columns(
                    [
                        lambda span: scores_a[head, tile, span, late],
                        lambda span: scores_b[head, tile, span, lanes] + bias[span, lanes],
                    ],
                    [probs_a.at[head, tile, :, late], probs_b.at[head, tile, :, lanes]],
                )
            )
        return stats

    def soft_coarse(head):
        return [
            soft_columns([lambda span: scores_c[head, span, lane_block(block)]], [probs_c.at[head, :, lane_block(block)]])
            for block in range(2)
        ]

    def weigh(head, tile, stats):
        own, base = lane_block(head), 2 * tile * BLOCK
        both = dot_first(v[base : base + BLOCK, own], probs_a[head, tile])
        more = dot_first(v[base + BLOCK : base + 2 * BLOCK, own], probs_b[head, tile])
        nums = [both[:, lane_block(0)], both[:, lane_block(1)]]
        nums += [both[:, lane_block(2 + block)] + more[:, lane_block(block)] for block in range(2)]
        return [(item,) + pair for item, pair in zip(nums, stats)]

    def keep(head, tile, states):
        for index, state in enumerate(states):
            lanes = lane_block(4 * tile + index)
            num[lane_block(head), lanes] = state[0]
            stat[head, 0:1, lanes] = state[1]
            stat[head, 1:2, lanes] = state[2]
        num_copy(head, tile).start()

    for head in range(heads):
        dots_coarse(head)
        dots(head, 1)
        dots(head, 0)
    for head in range(heads):
        coarse_stats = soft_coarse(head)
        coarse_num = 2.0 * dot_first(coarse_v[:, lane_block(head)], probs_c[head])
        states = []
        for block, state in enumerate(weigh(head, 1, soft(head, 1))):
            unit = block // 2
            coarse = (coarse_num[:, lane_block(unit)], coarse_stats[unit][0], 2.0 * coarse_stats[unit][1])
            states.append(merge(state, coarse))
        keep(head, 1, states)
        keep(head, 0, weigh(head, 0, soft(head, 0)))
    sends.append(pltpu.make_async_copy(stat, stat_out, sems.at[5]))
    sends[-1].start()
    for send in sends:
        send.wait()
    for head in range(heads):
        for tile in range(2):
            num_copy(head, tile).wait()


def near_call(queries, keys, values, levels, index):
    pool = as_bf16(padded(np.concatenate([pool_rows(level) for level in range(levels + 1)]), 16))
    heads = HEADS // SLICES
    width = heads * HEAD
    _, far_rows = far_offsets(levels)
    bf16, f32 = jnp.bfloat16, jnp.float32
    return pl.pallas_call(
        functools.partial(near_kernel, levels, index * heads),
        in_specs=[HBM] * 4,
        out_specs=[HBM] * 3,
        out_shape=[
            jax.ShapeDtypeStruct((width, TOK), f32),
            jax.ShapeDtypeStruct((heads, 8, TOK), f32),
            jax.ShapeDtypeStruct((far_rows, width), bf16),
        ],
        scratch_shapes=[
            pltpu.VMEM(pool.shape, bf16),
            pltpu.VMEM((TOK, width), bf16),
            pltpu.VMEM((TOK, width), bf16),
            pltpu.VMEM((TOK, width), bf16),
            pltpu.VMEM((width, TOK), f32),
            pltpu.VMEM((heads, 8, TOK), f32),
            pltpu.VMEM((far_rows, width), bf16),
            pltpu.VMEM((TOK, width), bf16),
            pltpu.VMEM((BLOCK, width), bf16),
            pltpu.VMEM((BLOCK, width), bf16),
            pltpu.VMEM((BLOCK, width), bf16),
            pltpu.VMEM((BLOCK, BLOCK), f32),
            pltpu.VMEM((heads, 2, BLOCK, 2 * BLOCK), f32),
            pltpu.VMEM((heads, 2, BLOCK, BLOCK), f32),
            pltpu.VMEM((heads, BLOCK, BLOCK), f32),
            pltpu.VMEM((heads, 2, BLOCK, 2 * BLOCK), bf16),
            pltpu.VMEM((heads, 2, BLOCK, BLOCK), bf16),
            pltpu.VMEM((heads, BLOCK, BLOCK), bf16),
            pltpu.SemaphoreType.DMA((6,)),
            pltpu.SemaphoreType.DMA((heads, 2)),
        ],
        compiler_params=pltpu.CompilerParams(vmem_limit_bytes=VMEM_CLAIM),
        cost_estimate=pl.CostEstimate(flops=NEAR_FLOPS, bytes_accessed=MIB // 4, transcendentals=0),
        name="near_levels",
    )(pool, queries, keys, values)


def by_lane_group(arrays, size):
    lane = lax.broadcasted_iota(jnp.int32, arrays[0].shape, 1)
    result = arrays[-1]
    for index in range(len(arrays) - 2, -1, -1):
        result = jnp.where(lane < (index + 1) * size, arrays[index], result)
    return result


def widen_to_second(array):
    r32, r64, r96 = [pltpu.roll(array, shift, 1) for shift in (32, 64, 96)]
    return [by_lane_group([array, r32, r32, r64], 32), by_lane_group([r64, r96, r96, array], 32)]


def widen_to_units(arrays):
    units = []
    for array in arrays:
        turned = pltpu.roll(array, 64, 1)
        units += [by_lane_group([array, turned], 64), by_lane_group([turned, array], 64)]
    return units


def far_kernel(levels, plan, flags_ref, *refs):
    crossing = range(FIRST, levels + 1)
    bundles = 1 + max(bundle for _, bundle, _ in plan)
    kv_refs = refs[:bundles]
    refs = refs[bundles:]
    far_refs, num_refs, stat_refs = refs[:SLICES], refs[SLICES : 2 * SLICES], refs[2 * SLICES : 3 * SLICES]
    turn_ref, w_ref, out_ref = refs[3 * SLICES : 3 * SLICES + 3]
    kv, queries, num, stat, turn, weights, scores, probs = refs[3 * SLICES + 3 : 3 * SLICES + 11]
    mixed, natural, stage, kv_sems, near_sems, last_sems, out_sems = refs[3 * SLICES + 11 :]
    heads = HEADS // SLICES
    width = heads * HEAD
    pair = 2 * HEAD
    model = w_ref.shape[1]
    step = 512
    offsets, far_rows = far_offsets(levels)

    def kv_copies(index):
        cols = pl.ds(pl.multiple_of(index * pair, pair), pair)
        made = []
        for number, (level, bundle, spans) in enumerate(plan):
            source_start, target_start, rows = spans
            made.append(
                pltpu.make_async_copy(
                    kv_refs[bundle].at[:, source_start : source_start + rows, cols],
                    kv.at[level - FIRST, :, target_start : target_start + rows, cols],
                    kv_sems.at[index, number],
                )
            )
        return made

    def near_copies(index):
        cols = slice(index * pair, (index + 1) * pair)
        group = slice(index * heads, (index + 1) * heads)
        sems = [near_sems.at[place, index] for place in range(3)]
        return [
            pltpu.make_async_copy(far_refs[index], queries.at[:, cols], sems[0]),
            pltpu.make_async_copy(num_refs[index], num.at[cols, :], sems[1]),
            pltpu.make_async_copy(stat_refs[index], stat.at[group], sems[2]),
        ]

    turn_copy = pltpu.make_async_copy(turn_ref, turn, last_sems.at[0])
    w_copies = [
        pltpu.make_async_copy(
            w_ref.at[:, index * step : (index + 1) * step], weights.at[:, index * step : (index + 1) * step], last_sems.at[1 + index]
        )
        for index in range(model // step)
    ]
    for index in range(SLICES):
        for copy in near_copies(index)[:1] + kv_copies(index) + near_copies(index)[1:]:
            copy.start()
    for copy in [turn_copy] + w_copies:
        copy.start()

    def wait_scores(index):
        for number in range(SLICES):

            @pl.when(index == number)
            def _():
                near_copies(number)[0].wait()
                for copy in kv_copies(number):
                    copy.wait()

    def wait_near(index):
        for number in range(SLICES):

            @pl.when(index == number)
            def _():
                for copy in near_copies(number)[1:]:
                    copy.wait()

    def dots(index, slot):
        for inner in range(2):
            own = pl.ds(pl.multiple_of(index * pair + inner * HEAD, HEAD), HEAD)
            for level in crossing:
                span = slice(offsets[level], offsets[level] + UNITS * count_of(level))
                scores[slot, inner, :, span] = dot_t(kv[level - FIRST, 0, :, own], queries[span, own])

    wait_scores(0)
    dots(0, 0)

    def group(index, carry):
        slot = lax.rem(index, 2)
        following = lax.rem(index + 1, SLICES)
        wait_scores(index + 1)
        wait_near(index)
        dots(following, 1 - slot)
        stats = []
        for inner in range(2):
            stats.append(
                [
                    soft_columns(
                        [lambda span: scores[slot, inner, span, lane_block(block)]], [probs.at[inner, :, lane_block(block)]]
                    )
                    for block in range(far_rows // HEAD)
                ]
            )
        for inner in range(2):
            head = 2 * index + inner
            own = pl.ds(pl.multiple_of(head * HEAD, HEAD), HEAD)
            state = None
            for level in reversed(crossing):
                span = slice(offsets[level], offsets[level] + UNITS * count_of(level))
                live = flags_ref[level - FIRST] == 1
                factor = jnp.where(live, 2.0**level, 0.0)
                weighted = factor * dot_first(kv[level - FIRST, 1, :, own], probs[inner, :, span])
                terms = []
                for block in range(UNITS * count_of(level) // HEAD):
                    peak, total = stats[inner][offsets[level] // HEAD + block]
                    terms.append((weighted[:, lane_block(block)], jnp.where(live, peak, NEG), factor * total))
                if state is None:
                    state = terms
                    continue
                if len(terms) > len(state):
                    wide = [widen_to_second(item) for item in state[0]]
                    state = [tuple(item[side] for item in wide) for side in range(2)]
                state = [merge(old, new) for old, new in zip(state, terms)]
            wide = [widen_to_units([half[place] for half in state]) for place in range(3)]
            for unit in range(UNITS):
                far_num, far_peak, far_total = [item[unit] for item in wide]
                for block in range(2 * unit, 2 * unit + 2):
                    peak = stat[head, 0:1, lane_block(block)]
                    total = stat[head, 1:2, lane_block(block)]
                    top = jnp.maximum(peak, far_peak)
                    a = jnp.exp(peak - top)
                    b = jnp.exp(far_peak - top)
                    inverse = 1.0 / (a * total + b * far_total)
                    both = (a * inverse) * num[own, lane_block(block)] + (b * inverse) * far_num
                    mixed[own, lane_block(block)] = both.astype(jnp.bfloat16)
        return carry

    lax.fori_loop(0, SLICES, group, 0)

    turn_copy.wait()
    for unit in range(UNITS):
        rows = slice(unit * BLOCK, (unit + 1) * BLOCK)
        natural[rows, :] = dot_t(turn[...], mixed[:, rows]).astype(jnp.bfloat16)
    sends = []
    for index in range(model // step):
        cols = slice(index * step, (index + 1) * step)
        w_copies[index].wait()
        stage[:, cols] = dot(natural[...], weights[:, cols]).astype(jnp.bfloat16)
        sends.append(pltpu.make_async_copy(stage.at[:, cols], out_ref.at[:, cols], out_sems.at[index]))
        sends[-1].start()
    for send in sends:
        send.wait()


def far_call(flags, bundles, plan, near, w_out, levels):
    turn = np.zeros((BLOCK, BLOCK))
    turn[token_of(np.arange(BLOCK)), np.arange(BLOCK)] = 1.0
    nums, stats, fars = [[item[place] for item in near] for place in range(3)]
    model = w_out.shape[1]
    _, far_rows = far_offsets(levels)
    count = levels - FIRST + 1
    bf16, f32 = jnp.bfloat16, jnp.float32
    return pl.pallas_call(
        functools.partial(far_kernel, levels, plan),
        in_specs=[pl.BlockSpec(memory_space=pltpu.SMEM)] + [HBM] * (len(bundles) + 3 * SLICES + 2),
        out_specs=HBM,
        out_shape=jax.ShapeDtypeStruct((TOK, model), bf16),
        scratch_shapes=[
            pltpu.VMEM((count, 2, BLOCK, WIDTH), bf16),
            pltpu.VMEM((far_rows, WIDTH), bf16),
            pltpu.VMEM((WIDTH, TOK), f32),
            pltpu.VMEM((HEADS, 8, TOK), f32),
            pltpu.VMEM((BLOCK, BLOCK), bf16),
            pltpu.VMEM((WIDTH, model), bf16),
            pltpu.VMEM((2, 2, BLOCK, far_rows), f32),
            pltpu.VMEM((2, BLOCK, far_rows), bf16),
            pltpu.VMEM((WIDTH, TOK), bf16),
            pltpu.VMEM((TOK, WIDTH), bf16),
            pltpu.VMEM((TOK, model), bf16),
            pltpu.SemaphoreType.DMA((HEADS // 2, len(plan))),
            pltpu.SemaphoreType.DMA((3, SLICES)),
            pltpu.SemaphoreType.DMA((1 + model // 512,)),
            pltpu.SemaphoreType.DMA((model // 512,)),
        ],
        compiler_params=pltpu.CompilerParams(vmem_limit_bytes=VMEM_CLAIM),
        cost_estimate=pl.CostEstimate(flops=6_500_000_000, bytes_accessed=18 * MIB, transcendentals=3_000_000),
        name="far_levels_projection",
    )(flags, *bundles, *fars, *nums, *stats, as_bf16(turn), w_out)


def moved(array, distance, upper_of=0):
    size = lax.axis_size("seq")
    pairs = [(i ^ distance, i) for i in range(size) if not upper_of or i & upper_of]
    return lax.ppermute(array, "seq", pairs)


def gathered(blocks, distance):
    sent = jnp.concatenate(blocks, axis=1) if len(blocks) > 1 else blocks[0]
    got = moved(sent, distance)
    joined, start = [], 0
    for block in blocks:
        rows = block.shape[1]
        joined.append(jnp.concatenate([block, got[:, start : start + rows]], axis=1))
        start += rows
    return joined


def after(arrays, others):
    return lax.optimization_barrier((arrays, others))[0]


def on_device(queries, keys, values, w_out):
    size = lax.axis_size("seq")
    levels = (TOK * size // (2 * BLOCK)).bit_length() - 1
    position = lax.axis_index("seq")
    flags = jnp.stack([(position >> (level - FIRST)) & 1 for level in range(FIRST, levels + 1)]).astype(jnp.int32)
    pooled = pool_call(keys, values, levels)
    blocks = {}
    for level in range(levels, FIRST - 1, -1):
        distance = 1 << (level - FIRST)
        blocks[level] = moved(pooled[level - FIRST], distance, distance)
    high = list(range(5, levels + 1))
    near = []

    def near_slice(arrived):
        source = after(queries, (near[-1:], arrived))
        near.append(near_call(source, keys, values, levels, len(near)))

    near_slice(pooled)
    rounds = [1 << bit for bit in range(1, levels - FIRST)]
    for number, distance in enumerate(rounds):
        arrived = dict(blocks)
        members = [level for level in high if (1 << (level - FIRST)) > distance]
        if number == 0:
            blocks[4] = gathered([blocks[4]], 2)[0]
        if members:
            waited = after([blocks[level] for level in members], near[-1])
            for level, item in zip(members, gathered(waited, distance)):
                blocks[level] = item
        if len(near) < SLICES:
            near_slice([arrived[level] for level in range(max(4 - number, 2), levels + 1)])
    low = jnp.concatenate([after(blocks[3], near[2]), blocks[4]], axis=1)
    low_got = moved(low, 1)
    top = jnp.concatenate(after([blocks[level] for level in high], near[-1]), axis=1)
    top_got = moved(top, 1)
    plan = [(2, 0, (0, 0, BLOCK))]
    for first, members in ((1, (3, 4)), (3, high)):
        for place, level in enumerate(members):
            plan += [(level, first, (place * 128, 0, 128)), (level, first + 1, (place * 128, 128, 128))]
    return far_call(flags, [blocks[2], low, low_got, top, top_got], plan, near, w_out, levels)


def solution(mesh):
    return jax.shard_map(
        on_device,
        mesh=mesh,
        in_specs=(P("seq", None), P("seq", None), P("seq", None), P()),
        out_specs=P("seq", None),
        check_vma=False,
    )
```

```python
import functools

import jax
import jax.numpy as jnp
import numpy as np
from jax import lax
from jax.experimental import pallas as pl
from jax.experimental.pallas import tpu as pltpu
from jax.sharding import PartitionSpec as P

HEADS = 8
HEAD = 128
BLOCK = 256
TOK = 1024
UNITS = TOK // BLOCK
WIDTH = HEADS * HEAD
NEG = -1e30
FIRST = 2
TOP = 5
GROUP = 8
SCALE = HEAD**-0.5
LOG2E = 1.4426950408889634
MIB = 1 << 20
SLICES = 2
VMEM_CLAIM = 60 * MIB
HBM = pl.BlockSpec(memory_space=pltpu.HBM)


def token_of(position):
    return ((position & 31) << 3) | (((position >> 5) & 1) << 2) | (((position >> 6) & 1) << 1) | (position >> 7)


def count_of(level):
    return max(BLOCK >> level, 32)


def pool_rows(level):
    rows = token_of(np.arange(count_of(level))) >> level
    columns = np.arange(BLOCK) >> level
    return (rows[:, None] == columns[None, :]) * 2.0**-level


def natural_pool(level, span):
    rows = np.arange(span >> level)
    return (rows[:, None] == (np.arange(span) >> level)[None, :]) * 2.0**-level


def padded(array, multiple):
    return np.pad(array, ((0, -len(array) % multiple), (0, 0)))


def as_bf16(array):
    return jnp.asarray(array.astype(np.float32)).astype(jnp.bfloat16)


def dot(a, b):
    return jnp.dot(a, b, preferred_element_type=jnp.float32)


def dot_t(a, b):
    return lax.dot_general(a, b, (((1,), (1,)), ((), ())), preferred_element_type=jnp.float32)


def dot_first(a, b):
    return lax.dot_general(a, b, (((0,), (0,)), ((), ())), preferred_element_type=jnp.float32)


def merge(first, second):
    top = jnp.maximum(first[1], second[1])
    a = jnp.exp(first[1] - top)
    b = jnp.exp(second[1] - top)
    return (a * first[0] + b * second[0], top, a * first[2] + b * second[2])


ROWS = 64


def soft_columns(loads, targets):
    spans = [slice(start, start + ROWS) for start in range(0, BLOCK, ROWS)]
    peak = None
    for load in loads:
        for span in spans:
            rows = jnp.max(load(span).reshape(ROWS // 8, 8, HEAD), axis=0)
            peak = rows if peak is None else jnp.maximum(peak, rows)
    peak = jnp.max(peak, axis=0, keepdims=True)
    total = jnp.zeros((8, HEAD), jnp.float32)
    for load, target in zip(loads, targets):
        for span in spans:
            probs = jnp.exp2((load(span) - peak) * (SCALE * LOG2E))
            total = total + jnp.sum(probs.reshape(ROWS // 8, 8, HEAD), axis=0)
            target[span, :] = probs.astype(jnp.bfloat16)
    return peak * SCALE, jnp.sum(total, axis=0, keepdims=True)


def pool_kernel(levels, small_ref, large_ref, keys_ref, values_ref, *refs):
    count = levels - FIRST + 1
    targets, (small, large, buffers, *outs, sems, out_sems) = refs[:count], refs[count:]
    step = WIDTH // 4
    fixed = [pltpu.make_async_copy(small_ref, small, sems.at[8]), pltpu.make_async_copy(large_ref, large, sems.at[9])]
    copies = []
    for index, source in enumerate((keys_ref, values_ref)):
        for part in range(4):
            cols = slice(part * step, (part + 1) * step)
            copies.append(pltpu.make_async_copy(source.at[:, cols], buffers.at[index, :, cols], sems.at[index * 4 + part]))
    for copy in fixed + copies:
        copy.start()
    for copy in fixed:
        copy.wait()
    sends = []
    for index in range(2):
        for part in range(4):
            cols = slice(part * step, (part + 1) * step)
            copies[index * 4 + part].wait()
            tiles = [
                dot(small[...], buffers[index, i * 2 * BLOCK : (i + 1) * 2 * BLOCK, cols]) for i in range(UNITS // 2)
            ]
            offset = 0
            for level in range(FIRST, min(levels, 6) + 1):
                rows = 2 * BLOCK >> level
                both = jnp.concatenate([tile[offset : offset + rows] for tile in tiles], axis=0)
                outs[level - FIRST][index, :, cols] = both.astype(jnp.bfloat16)
                offset += rows
            if levels > 6:
                rest = dot(large[...], buffers[index, :, cols])
                for level in range(7, levels + 1):
                    start = (level - 7) * 8
                    outs[level - FIRST][index, :, cols] = rest[start : start + (TOK >> level)].astype(jnp.bfloat16)
        for place, (out, target) in enumerate(zip(outs, targets)):
            sends.append(pltpu.make_async_copy(out.at[index], target.at[index], out_sems.at[index, place]))
            sends[-1].start()
    for send in sends:
        send.wait()


def pool_call(keys, values, levels):
    small = as_bf16(padded(np.concatenate([natural_pool(level, 2 * BLOCK) for level in range(FIRST, min(levels, 6) + 1)]), 16))
    parts = [padded(natural_pool(level, TOK), 8) for level in range(7, levels + 1)] + [np.zeros((8, TOK))]
    large = as_bf16(padded(np.concatenate(parts), 16))
    crossing = range(FIRST, levels + 1)
    return pl.pallas_call(
        functools.partial(pool_kernel, levels),
        in_specs=[HBM] * 4,
        out_specs=[HBM] * len(crossing),
        out_shape=[jax.ShapeDtypeStruct((2, TOK >> level, WIDTH), jnp.bfloat16) for level in crossing],
        scratch_shapes=[
            pltpu.VMEM(small.shape, jnp.bfloat16),
            pltpu.VMEM(large.shape, jnp.bfloat16),
            pltpu.VMEM((2, TOK, WIDTH), jnp.bfloat16),
        ]
        + [pltpu.VMEM((2, TOK >> level, WIDTH), jnp.bfloat16) for level in crossing]
        + [
            pltpu.SemaphoreType.DMA((10,)),
            pltpu.SemaphoreType.DMA((2, len(crossing))),
        ],
        compiler_params=pltpu.CompilerParams(vmem_limit_bytes=VMEM_CLAIM),
        cost_estimate=pl.CostEstimate(flops=2 * 256 * 512 * 4096, bytes_accessed=6 * MIB, transcendentals=0),
        name="pool_keys_values",
    )(small, large, keys, values)


def far_offsets(levels):
    offsets, total = {}, 0
    for level in range(FIRST, levels + 1):
        offsets[level] = total
        total += UNITS * count_of(level)
    return offsets, total


def lane_block(index):
    return slice(index * HEAD, (index + 1) * HEAD)


def near_kernel(levels, first, pool_ref, q_ref, k_ref, v_ref, num_out, stat_out, far_out, *scratch):
    (pool, q, k, v, num, stat, far, ordered, coarse_q, coarse_k, coarse_v, bias, scores_a, scores_b, scores_c) = scratch[:15]
    probs_a, probs_b, probs_c, sems, head_sems = scratch[15:]
    heads = HEADS // SLICES
    width = heads * HEAD
    cols = slice(first * HEAD, first * HEAD + width)
    copies = [
        pltpu.make_async_copy(pool_ref, pool, sems.at[0]),
        pltpu.make_async_copy(q_ref.at[:, cols], q, sems.at[1]),
        pltpu.make_async_copy(k_ref.at[:, cols], k, sems.at[2]),
        pltpu.make_async_copy(v_ref.at[:, cols], v, sems.at[3]),
    ]
    for copy in copies:
        copy.start()
    row = lax.broadcasted_iota(jnp.int32, (BLOCK, BLOCK), 0)
    position = lax.broadcasted_iota(jnp.int32, (BLOCK, BLOCK), 1)
    bias[...] = jnp.where(row <= token_of(position), 0.0, NEG)
    copies[0].wait()
    copies[1].wait()

    offsets, _ = far_offsets(levels)
    for unit in range(UNITS):
        pooled = dot(pool[...], q[unit * BLOCK : (unit + 1) * BLOCK, :])
        ordered[unit * BLOCK : (unit + 1) * BLOCK, :] = pooled[:BLOCK].astype(jnp.bfloat16)
        if unit >= 2:
            coarse_q[(unit - 2) * 128 : (unit - 1) * 128, :] = pooled[BLOCK : BLOCK + 128].astype(jnp.bfloat16)
        start = BLOCK + 128
        for level in range(FIRST, levels + 1):
            count = count_of(level)
            place = offsets[level] + unit * count
            far[place : place + count, :] = pooled[start : start + count].astype(jnp.bfloat16)
            start += count
    sends = [pltpu.make_async_copy(far, far_out, sems.at[4])]
    sends[0].start()
    copies[2].wait()
    copies[3].wait()
    for unit in range(2):
        rows = slice(unit * BLOCK, (unit + 1) * BLOCK)
        half = slice(unit * 128, (unit + 1) * 128)
        coarse_k[half, :] = dot(pool[BLOCK : BLOCK + 128, :], k[rows, :]).astype(jnp.bfloat16)
        coarse_v[half, :] = dot(pool[BLOCK : BLOCK + 128, :], v[rows, :]).astype(jnp.bfloat16)

    def num_copy(head):
        rows = pl.ds(pl.multiple_of(head * HEAD, HEAD), HEAD)
        return pltpu.make_async_copy(num.at[rows, :], num_out.at[rows, :], head_sems.at[head])

    def one_head(head, carry):
        own = pl.ds(pl.multiple_of(head * HEAD, HEAD), HEAD)

        def dots(tile):
            base = 2 * tile * BLOCK
            both = ordered[base : base + 2 * BLOCK, own]
            scores_a[tile] = dot_t(k[base : base + BLOCK, own], both)
            scores_b[tile] = dot_t(k[base + BLOCK : base + 2 * BLOCK, own], ordered[base + BLOCK : base + 2 * BLOCK, own])

        def soft(tile):
            stats = []
            for block in range(2):
                lanes = lane_block(block)
                stats.append(
                    soft_columns(
                        [lambda span: scores_a[tile, span, lanes] + bias[span, lanes]], [probs_a.at[tile, :, lanes]]
                    )
                )
            for block in range(2):
                lanes, late = lane_block(block), lane_block(2 + block)
                stats.append(
                    soft_columns(
                        [
                            lambda span: scores_a[tile, span, late],
                            lambda span: scores_b[tile, span, lanes] + bias[span, lanes],
                        ],
                        [probs_a.at[tile, :, late], probs_b.at[tile, :, lanes]],
                    )
                )
            return stats

        def weigh(tile, stats):
            base = 2 * tile * BLOCK
            both = dot_first(v[base : base + BLOCK, own], probs_a[tile])
            more = dot_first(v[base + BLOCK : base + 2 * BLOCK, own], probs_b[tile])
            nums = [both[:, lane_block(0)], both[:, lane_block(1)]]
            nums += [both[:, lane_block(2 + block)] + more[:, lane_block(block)] for block in range(2)]
            return [(item,) + pair for item, pair in zip(nums, stats)]

        dots(0)
        scores_c[...] = dot_t(coarse_k[:, own], coarse_q[:, own])
        dots(1)
        stats0 = soft(0)
        states = weigh(0, stats0)
        stats_c = [
            soft_columns([lambda span: scores_c[span, lane_block(block)]], [probs_c.at[:, lane_block(block)]])
            for block in range(2)
        ]
        stats1 = soft(1)
        num_c = 2.0 * dot_first(coarse_v[:, own], probs_c[...])
        late = weigh(1, stats1)
        for block, state in enumerate(late):
            unit = block // 2
            coarse = (num_c[:, lane_block(unit)], stats_c[unit][0], 2.0 * stats_c[unit][1])
            states.append(merge(state, coarse))
        for block, state in enumerate(states):
            num[own, lane_block(block)] = state[0]
            stat[head, 0:1, lane_block(block)] = state[1]
            stat[head, 1:2, lane_block(block)] = state[2]
        num_copy(head).start()
        return carry

    lax.fori_loop(0, heads, one_head, 0)
    sends.append(pltpu.make_async_copy(stat, stat_out, sems.at[5]))
    sends[-1].start()
    for send in sends:
        send.wait()
    for head in range(heads):
        num_copy(head).wait()


def near_call(queries, keys, values, levels, index):
    pool = as_bf16(padded(np.concatenate([pool_rows(level) for level in range(levels + 1)]), 16))
    heads = HEADS // SLICES
    width = heads * HEAD
    _, far_rows = far_offsets(levels)
    bf16, f32 = jnp.bfloat16, jnp.float32
    return pl.pallas_call(
        functools.partial(near_kernel, levels, index * heads),
        in_specs=[HBM] * 4,
        out_specs=[HBM] * 3,
        out_shape=[
            jax.ShapeDtypeStruct((width, TOK), f32),
            jax.ShapeDtypeStruct((heads, 8, TOK), f32),
            jax.ShapeDtypeStruct((far_rows, width), bf16),
        ],
        scratch_shapes=[
            pltpu.VMEM(pool.shape, bf16),
            pltpu.VMEM((TOK, width), bf16),
            pltpu.VMEM((TOK, width), bf16),
            pltpu.VMEM((TOK, width), bf16),
            pltpu.VMEM((width, TOK), f32),
            pltpu.VMEM((heads, 8, TOK), f32),
            pltpu.VMEM((far_rows, width), bf16),
            pltpu.VMEM((TOK, width), bf16),
            pltpu.VMEM((BLOCK, width), bf16),
            pltpu.VMEM((BLOCK, width), bf16),
            pltpu.VMEM((BLOCK, width), bf16),
            pltpu.VMEM((BLOCK, BLOCK), f32),
            pltpu.VMEM((2, BLOCK, 2 * BLOCK), f32),
            pltpu.VMEM((2, BLOCK, BLOCK), f32),
            pltpu.VMEM((BLOCK, BLOCK), f32),
            pltpu.VMEM((2, BLOCK, 2 * BLOCK), bf16),
            pltpu.VMEM((2, BLOCK, BLOCK), bf16),
            pltpu.VMEM((BLOCK, BLOCK), bf16),
            pltpu.SemaphoreType.DMA((6,)),
            pltpu.SemaphoreType.DMA((heads,)),
        ],
        compiler_params=pltpu.CompilerParams(vmem_limit_bytes=VMEM_CLAIM),
        cost_estimate=pl.CostEstimate(flops=8_000_000_000, bytes_accessed=4 * MIB, transcendentals=0),
        name="near_levels",
    )(pool, queries, keys, values)


def by_lane_group(arrays, size):
    lane = lax.broadcasted_iota(jnp.int32, arrays[0].shape, 1)
    result = arrays[-1]
    for index in range(len(arrays) - 2, -1, -1):
        result = jnp.where(lane < (index + 1) * size, arrays[index], result)
    return result


def widen_to_second(array):
    r32, r64, r96 = [pltpu.roll(array, shift, 1) for shift in (32, 64, 96)]
    return [by_lane_group([array, r32, r32, r64], 32), by_lane_group([r64, r96, r96, array], 32)]


def widen_to_units(arrays):
    units = []
    for array in arrays:
        turned = pltpu.roll(array, 64, 1)
        units += [by_lane_group([array, turned], 64), by_lane_group([turned, array], 64)]
    return units


def far_kernel(levels, plan, flags_ref, *refs):
    crossing = range(FIRST, levels + 1)
    bundles = 1 + max(bundle for _, bundle, _ in plan)
    kv_refs = refs[:bundles]
    refs = refs[bundles:]
    far_refs, num_refs, stat_refs = refs[:SLICES], refs[SLICES : 2 * SLICES], refs[2 * SLICES : 3 * SLICES]
    turn_ref, w_ref, out_ref = refs[3 * SLICES : 3 * SLICES + 3]
    kv, queries, num, stat, turn, weights, scores, probs = refs[3 * SLICES + 3 : 3 * SLICES + 11]
    mixed, natural, stage, kv_sems, near_sems, out_sems = refs[3 * SLICES + 11 :]
    heads = HEADS // SLICES
    width = heads * HEAD
    pair = 2 * HEAD
    model = w_ref.shape[1]
    step = 512
    offsets, far_rows = far_offsets(levels)

    def kv_copies(index):
        cols = pl.ds(pl.multiple_of(index * pair, pair), pair)
        made = []
        for number, (level, bundle, spans) in enumerate(plan):
            source_start, target_start, rows = spans
            made.append(
                pltpu.make_async_copy(
                    kv_refs[bundle].at[:, source_start : source_start + rows, cols],
                    kv.at[level - FIRST, :, target_start : target_start + rows, cols],
                    kv_sems.at[index, number],
                )
            )
        return made

    far_copies, near_copies = [], []
    for index in range(SLICES):
        cols = slice(index * width, (index + 1) * width)
        group = slice(index * heads, (index + 1) * heads)
        sems = [near_sems.at[place * SLICES + index] for place in range(3)]
        far_copies.append(pltpu.make_async_copy(far_refs[index], queries.at[:, cols], sems[0]))
        near_copies.append(pltpu.make_async_copy(num_refs[index], num.at[cols, :], sems[1]))
        near_copies.append(pltpu.make_async_copy(stat_refs[index], stat.at[group], sems[2]))
    last_copies = [
        pltpu.make_async_copy(turn_ref, turn, near_sems.at[3 * SLICES]),
        pltpu.make_async_copy(w_ref, weights, near_sems.at[3 * SLICES + 1]),
    ]
    for copy in far_copies + kv_copies(0) + near_copies:
        copy.start()
    for index in range(1, HEADS // 2):
        for copy in kv_copies(index):
            copy.start()
    for copy in last_copies:
        copy.start()
    for copy in far_copies:
        copy.wait()

    def group(index, carry):
        for copy in kv_copies(index):
            copy.wait()
        stats = []
        for inner in range(2):
            own = pl.ds(pl.multiple_of(index * pair + inner * HEAD, HEAD), HEAD)
            for level in crossing:
                span = slice(offsets[level], offsets[level] + UNITS * count_of(level))
                scores[inner, :, span] = dot_t(kv[level - FIRST, 0, :, own], queries[span, own])
        for inner in range(2):
            stats.append(
                [
                    soft_columns(
                        [lambda span: scores[inner, span, lane_block(block)]], [probs.at[inner, :, lane_block(block)]]
                    )
                    for block in range(far_rows // HEAD)
                ]
            )

        @pl.when(index == 0)
        def _():
            for copy in near_copies:
                copy.wait()

        for inner in range(2):
            head = 2 * index + inner
            own = pl.ds(pl.multiple_of(head * HEAD, HEAD), HEAD)
            state = None
            for level in reversed(crossing):
                span = slice(offsets[level], offsets[level] + UNITS * count_of(level))
                live = flags_ref[level - FIRST] == 1
                factor = jnp.where(live, 2.0**level, 0.0)
                weighted = factor * dot_first(kv[level - FIRST, 1, :, own], probs[inner, :, span])
                terms = []
                for block in range(UNITS * count_of(level) // HEAD):
                    peak, total = stats[inner][offsets[level] // HEAD + block]
                    terms.append((weighted[:, lane_block(block)], jnp.where(live, peak, NEG), factor * total))
                if state is None:
                    state = terms
                    continue
                if len(terms) > len(state):
                    wide = [widen_to_second(item) for item in state[0]]
                    state = [tuple(item[side] for item in wide) for side in range(2)]
                state = [merge(old, new) for old, new in zip(state, terms)]
            wide = [widen_to_units([half[place] for half in state]) for place in range(3)]
            for unit in range(UNITS):
                far_num, far_peak, far_total = [item[unit] for item in wide]
                for block in range(2 * unit, 2 * unit + 2):
                    peak = stat[head, 0:1, lane_block(block)]
                    total = stat[head, 1:2, lane_block(block)]
                    top = jnp.maximum(peak, far_peak)
                    a = jnp.exp(peak - top)
                    b = jnp.exp(far_peak - top)
                    inverse = 1.0 / (a * total + b * far_total)
                    both = (a * inverse) * num[own, lane_block(block)] + (b * inverse) * far_num
                    mixed[own, lane_block(block)] = both.astype(jnp.bfloat16)
        return carry

    lax.fori_loop(0, HEADS // 2, group, 0)

    for copy in last_copies:
        copy.wait()
    for unit in range(UNITS):
        rows = slice(unit * BLOCK, (unit + 1) * BLOCK)
        natural[rows, :] = dot_t(turn[...], mixed[:, rows]).astype(jnp.bfloat16)
    sends = []
    for index in range(model // step):
        cols = slice(index * step, (index + 1) * step)
        stage[:, cols] = dot(natural[...], weights[:, cols]).astype(jnp.bfloat16)
        sends.append(pltpu.make_async_copy(stage.at[:, cols], out_ref.at[:, cols], out_sems.at[index]))
        sends[-1].start()
    for send in sends:
        send.wait()


def far_call(flags, bundles, plan, near, w_out, levels):
    turn = np.zeros((BLOCK, BLOCK))
    turn[token_of(np.arange(BLOCK)), np.arange(BLOCK)] = 1.0
    nums, stats, fars = [[item[place] for item in near] for place in range(3)]
    model = w_out.shape[1]
    _, far_rows = far_offsets(levels)
    count = levels - FIRST + 1
    bf16, f32 = jnp.bfloat16, jnp.float32
    return pl.pallas_call(
        functools.partial(far_kernel, levels, plan),
        in_specs=[pl.BlockSpec(memory_space=pltpu.SMEM)] + [HBM] * (len(bundles) + 3 * SLICES + 2),
        out_specs=HBM,
        out_shape=jax.ShapeDtypeStruct((TOK, model), bf16),
        scratch_shapes=[
            pltpu.VMEM((count, 2, BLOCK, WIDTH), bf16),
            pltpu.VMEM((far_rows, WIDTH), bf16),
            pltpu.VMEM((WIDTH, TOK), f32),
            pltpu.VMEM((HEADS, 8, TOK), f32),
            pltpu.VMEM((BLOCK, BLOCK), bf16),
            pltpu.VMEM((WIDTH, model), bf16),
            pltpu.VMEM((2, BLOCK, far_rows), f32),
            pltpu.VMEM((2, BLOCK, far_rows), bf16),
            pltpu.VMEM((WIDTH, TOK), bf16),
            pltpu.VMEM((TOK, WIDTH), bf16),
            pltpu.VMEM((TOK, model), bf16),
            pltpu.SemaphoreType.DMA((HEADS // 2, len(plan))),
            pltpu.SemaphoreType.DMA((3 * SLICES + 2,)),
            pltpu.SemaphoreType.DMA((model // 512,)),
        ],
        compiler_params=pltpu.CompilerParams(vmem_limit_bytes=VMEM_CLAIM),
        cost_estimate=pl.CostEstimate(flops=6_500_000_000, bytes_accessed=18 * MIB, transcendentals=3_000_000),
        name="far_levels_projection",
    )(flags, *bundles, *fars, *nums, *stats, as_bf16(turn), w_out)


def moved(array, distance, upper_of=0):
    size = lax.axis_size("seq")
    pairs = [(i ^ distance, i) for i in range(size) if not upper_of or i & upper_of]
    return lax.ppermute(array, "seq", pairs)


def gathered(blocks, distance):
    sent = jnp.concatenate(blocks, axis=1) if len(blocks) > 1 else blocks[0]
    got = moved(sent, distance)
    joined, start = [], 0
    for block in blocks:
        rows = block.shape[1]
        joined.append(jnp.concatenate([block, got[:, start : start + rows]], axis=1))
        start += rows
    return joined


def after(arrays, others):
    return lax.optimization_barrier((arrays, others))[0]


def on_device(queries, keys, values, w_out):
    size = lax.axis_size("seq")
    levels = (TOK * size // (2 * BLOCK)).bit_length() - 1
    position = lax.axis_index("seq")
    flags = jnp.stack([(position >> (level - FIRST)) & 1 for level in range(FIRST, levels + 1)]).astype(jnp.int32)
    pooled = pool_call(keys, values, levels)

    blocks = {}
    for level in list(range(levels, TOP - 1, -1)) + [3, 4, 2]:
        cross = 1 << (level - FIRST)
        parts = max(cross // GROUP, 1)
        pieces = [moved(pooled[level - FIRST], cross + GROUP * part, cross) for part in range(parts)]
        blocks[level] = jnp.concatenate(pieces, axis=1) if parts > 1 else pieces[0]
    high = list(range(TOP, levels + 1))

    first = gathered([blocks[level] for level in high], 2)
    near = [near_call(after(queries, [blocks[level] for level in high]), keys, values, levels, 0)]
    second = gathered(after(first, near[0]), 4)
    blocks[4] = gathered([after(blocks[4], near[0])], 2)[0]
    near.append(near_call(after(queries, (near[0], first)), keys, values, levels, 1))
    low = jnp.concatenate([after(blocks[3], near[0]), blocks[4]], axis=1)
    low_got = moved(low, 1)
    top = jnp.concatenate(after(second, near[1]), axis=1)
    top_got = moved(top, 1)
    plan = [(2, 0, (0, 0, BLOCK))]
    for number, members in ((1, (3, 4)), (3, high)):
        for place, level in enumerate(members):
            plan += [(level, number, (place * 128, 0, 128)), (level, number + 1, (place * 128, 128, 128))]
    return far_call(flags, [blocks[2], low, low_got, top, top_got], plan, near, w_out, levels)


def solution(mesh):
    return jax.shard_map(
        on_device,
        mesh=mesh,
        in_specs=(P("seq", None), P("seq", None), P("seq", None), P()),
        out_specs=P("seq", None),
        check_vma=False,
    )
```

```python
import functools

import jax
import jax.numpy as jnp
import numpy as np
from jax import lax
from jax.experimental import pallas as pl
from jax.experimental.pallas import tpu as pltpu
from jax.sharding import PartitionSpec as P

HEADS = 8
HEAD = 128
BLOCK = 256
TOK = 1024
UNITS = TOK // BLOCK
WIDTH = HEADS * HEAD
NEG = -1e30
FIRST = 2
TOP = 5
GROUP = 8
SCALE = HEAD**-0.5
LOG2E = 1.4426950408889634
MIB = 1 << 20
SLICES = ((0, 3), (3, 3), (6, 2))
VMEM_CLAIM = 60 * MIB
HBM = pl.BlockSpec(memory_space=pltpu.HBM)


def token_of(position):
    return ((position & 31) << 3) | (((position >> 5) & 1) << 2) | (((position >> 6) & 1) << 1) | (position >> 7)


def count_of(level):
    return max(BLOCK >> level, 32)


def pool_rows(level):
    rows = token_of(np.arange(count_of(level))) >> level
    columns = np.arange(BLOCK) >> level
    return (rows[:, None] == columns[None, :]) * 2.0**-level


def natural_pool(level, span):
    rows = np.arange(span >> level)
    return (rows[:, None] == (np.arange(span) >> level)[None, :]) * 2.0**-level


def padded(array, multiple):
    return np.pad(array, ((0, -len(array) % multiple), (0, 0)))


def as_bf16(array):
    return jnp.asarray(array.astype(np.float32)).astype(jnp.bfloat16)


def dot(a, b):
    return jnp.dot(a, b, preferred_element_type=jnp.float32)


def dot_t(a, b):
    return lax.dot_general(a, b, (((1,), (1,)), ((), ())), preferred_element_type=jnp.float32)


def dot_first(a, b):
    return lax.dot_general(a, b, (((0,), (0,)), ((), ())), preferred_element_type=jnp.float32)


def merge(first, second):
    top = jnp.maximum(first[1], second[1])
    a = jnp.exp(first[1] - top)
    b = jnp.exp(second[1] - top)
    return (a * first[0] + b * second[0], top, a * first[2] + b * second[2])


ROWS = 64


def soft_columns(loads, targets):
    spans = [slice(start, start + ROWS) for start in range(0, BLOCK, ROWS)]
    peak = None
    for load in loads:
        for span in spans:
            rows = jnp.max(load(span).reshape(ROWS // 8, 8, HEAD), axis=0)
            peak = rows if peak is None else jnp.maximum(peak, rows)
    peak = jnp.max(peak, axis=0, keepdims=True)
    total = jnp.zeros((8, HEAD), jnp.float32)
    for load, target in zip(loads, targets):
        for span in spans:
            probs = jnp.exp2((load(span) - peak) * (SCALE * LOG2E))
            total = total + jnp.sum(probs.reshape(ROWS // 8, 8, HEAD), axis=0)
            target[span, :] = probs.astype(jnp.bfloat16)
    return peak * SCALE, jnp.sum(total, axis=0, keepdims=True)


def packed(levels):
    places, rows = {level: (level - FIRST, 0) for level in range(FIRST, TOP)}, 0
    for level in range(TOP, levels + 1):
        places[level] = (TOP - FIRST, rows)
        rows += TOK >> level
    return places, [TOK >> level for level in range(FIRST, TOP)] + [rows]


def pool_kernel(levels, small_ref, large_ref, keys_ref, values_ref, *refs):
    places, sizes = packed(levels)
    count = len(sizes)
    targets, (small, large, buffers, *outs, sems, out_sems) = refs[:count], refs[count:]
    step = WIDTH // 4
    fixed = [pltpu.make_async_copy(small_ref, small, sems.at[8]), pltpu.make_async_copy(large_ref, large, sems.at[9])]
    copies = []
    for index, source in enumerate((keys_ref, values_ref)):
        for part in range(4):
            cols = slice(part * step, (part + 1) * step)
            copies.append(pltpu.make_async_copy(source.at[:, cols], buffers.at[index, :, cols], sems.at[index * 4 + part]))
    for copy in fixed + copies:
        copy.start()
    for copy in fixed:
        copy.wait()
    sends = []
    for index in range(2):
        for part in range(4):
            cols = slice(part * step, (part + 1) * step)
            copies[index * 4 + part].wait()
            tiles = [
                dot(small[...], buffers[index, i * 2 * BLOCK : (i + 1) * 2 * BLOCK, cols]) for i in range(UNITS // 2)
            ]
            offset = 0
            for level in range(FIRST, min(levels, 6) + 1):
                rows = 2 * BLOCK >> level
                both = jnp.concatenate([tile[offset : offset + rows] for tile in tiles], axis=0)
                place, first = places[level]
                outs[place][index, first : first + 2 * rows, cols] = both.astype(jnp.bfloat16)
                offset += rows
            if levels > 6:
                rest = dot(large[...], buffers[index, :, cols])
                for level in range(7, levels + 1):
                    start = (level - 7) * 8
                    place, first = places[level]
                    outs[place][index, first : first + (TOK >> level), cols] = rest[start : start + (TOK >> level)].astype(jnp.bfloat16)
        for place, (out, target) in enumerate(zip(outs, targets)):
            sends.append(pltpu.make_async_copy(out.at[index], target.at[index], out_sems.at[index, place]))
            sends[-1].start()
    for send in sends:
        send.wait()


def pool_call(keys, values, levels):
    small = as_bf16(padded(np.concatenate([natural_pool(level, 2 * BLOCK) for level in range(FIRST, min(levels, 6) + 1)]), 16))
    parts = [padded(natural_pool(level, TOK), 8) for level in range(7, levels + 1)] + [np.zeros((8, TOK))]
    large = as_bf16(padded(np.concatenate(parts), 16))
    _, sizes = packed(levels)
    return pl.pallas_call(
        functools.partial(pool_kernel, levels),
        in_specs=[HBM] * 4,
        out_specs=[HBM] * len(sizes),
        out_shape=[jax.ShapeDtypeStruct((2, rows, WIDTH), jnp.bfloat16) for rows in sizes],
        scratch_shapes=[
            pltpu.VMEM(small.shape, jnp.bfloat16),
            pltpu.VMEM(large.shape, jnp.bfloat16),
            pltpu.VMEM((2, TOK, WIDTH), jnp.bfloat16),
        ]
        + [pltpu.VMEM((2, rows, WIDTH), jnp.bfloat16) for rows in sizes]
        + [
            pltpu.SemaphoreType.DMA((10,)),
            pltpu.SemaphoreType.DMA((2, len(sizes))),
        ],
        compiler_params=pltpu.CompilerParams(vmem_limit_bytes=VMEM_CLAIM),
        cost_estimate=pl.CostEstimate(flops=2 * 256 * 512 * 4096, bytes_accessed=6 * MIB, transcendentals=0),
        name="pool_keys_values",
    )(small, large, keys, values)


def far_offsets(levels):
    offsets, total = {}, 0
    for level in range(FIRST, levels + 1):
        offsets[level] = total
        total += UNITS * count_of(level)
    return offsets, total


def lane_block(index):
    return slice(index * HEAD, (index + 1) * HEAD)


def near_kernel(levels, first, heads, pool_ref, q_ref, k_ref, v_ref, num_out, stat_out, far_out, *scratch):
    (pool, q, k, v, num, stat, far, ordered, coarse_q, coarse_k, coarse_v, bias, scores_a, scores_b, scores_c) = scratch[:15]
    probs_a, probs_b, probs_c, sems, head_sems = scratch[15:]
    width = heads * HEAD
    cols = slice(first * HEAD, first * HEAD + width)
    copies = [
        pltpu.make_async_copy(pool_ref, pool, sems.at[0]),
        pltpu.make_async_copy(q_ref.at[:, cols], q, sems.at[1]),
        pltpu.make_async_copy(k_ref.at[:, cols], k, sems.at[2]),
        pltpu.make_async_copy(v_ref.at[:, cols], v, sems.at[3]),
    ]
    for copy in copies:
        copy.start()
    row = lax.broadcasted_iota(jnp.int32, (BLOCK, BLOCK), 0)
    position = lax.broadcasted_iota(jnp.int32, (BLOCK, BLOCK), 1)
    bias[...] = jnp.where(row <= token_of(position), 0.0, NEG)
    copies[0].wait()
    copies[1].wait()

    offsets, _ = far_offsets(levels)
    for unit in range(UNITS):
        pooled = dot(pool[...], q[unit * BLOCK : (unit + 1) * BLOCK, :])
        ordered[unit * BLOCK : (unit + 1) * BLOCK, :] = pooled[:BLOCK].astype(jnp.bfloat16)
        if unit >= 2:
            coarse_q[(unit - 2) * 128 : (unit - 1) * 128, :] = pooled[BLOCK : BLOCK + 128].astype(jnp.bfloat16)
        start = BLOCK + 128
        for level in range(FIRST, levels + 1):
            count = count_of(level)
            place = offsets[level] + unit * count
            far[place : place + count, :] = pooled[start : start + count].astype(jnp.bfloat16)
            start += count
    sends = [pltpu.make_async_copy(far, far_out, sems.at[4])]
    sends[0].start()
    copies[2].wait()
    copies[3].wait()
    for unit in range(2):
        rows = slice(unit * BLOCK, (unit + 1) * BLOCK)
        half = slice(unit * 128, (unit + 1) * 128)
        coarse_k[half, :] = dot(pool[BLOCK : BLOCK + 128, :], k[rows, :]).astype(jnp.bfloat16)
        coarse_v[half, :] = dot(pool[BLOCK : BLOCK + 128, :], v[rows, :]).astype(jnp.bfloat16)

    def num_copy(head, tile):
        rows = lane_block(head)
        lanes = slice(tile * 2 * BLOCK, (tile + 1) * 2 * BLOCK)
        return pltpu.make_async_copy(num.at[rows, lanes], num_out.at[rows, lanes], head_sems.at[head, tile])

    def dot_pieces(head):
        slot, own = head % 2, lane_block(head)

        def coarse():
            scores_c[slot] = dot_t(coarse_k[:, own], coarse_q[:, own])

        def part(tile, piece):
            base = 2 * tile * BLOCK
            if piece < 2:
                rows = slice(base + piece * BLOCK, base + (piece + 1) * BLOCK)
                scores_a[slot, tile, :, piece * BLOCK : (piece + 1) * BLOCK] = dot_t(
                    k[base : base + BLOCK, own], ordered[rows, own]
                )
            else:
                rows = slice(base + BLOCK, base + 2 * BLOCK)
                scores_b[slot, tile] = dot_t(k[rows, own], ordered[rows, own])

        return [coarse] + [functools.partial(part, tile, piece) for tile in (1, 0) for piece in range(3)]

    def soft_a(head, tile, block):
        slot, lanes = head % 2, lane_block(block)
        return soft_columns(
            [lambda span: scores_a[slot, tile, span, lanes] + bias[span, lanes]], [probs_a.at[slot, tile, :, lanes]]
        )

    def soft_b(head, tile, block):
        slot, lanes, late = head % 2, lane_block(block), lane_block(2 + block)
        return soft_columns(
            [
                lambda span: scores_a[slot, tile, span, late],
                lambda span: scores_b[slot, tile, span, lanes] + bias[span, lanes],
            ],
            [probs_a.at[slot, tile, :, late], probs_b.at[slot, tile, :, lanes]],
        )

    def soft_c(head, block):
        slot, lanes = head % 2, lane_block(block)
        return soft_columns([lambda span: scores_c[slot, span, lanes]], [probs_c.at[slot, :, lanes]])

    def weigh(head, tile):
        slot, own, base = head % 2, lane_block(head), 2 * tile * BLOCK
        both = dot_first(v[base : base + BLOCK, own], probs_a[slot, tile])
        more = dot_first(v[base + BLOCK : base + 2 * BLOCK, own], probs_b[slot, tile])
        nums = [both[:, lane_block(0)], both[:, lane_block(1)]]
        return nums + [both[:, lane_block(2 + block)] + more[:, lane_block(block)] for block in range(2)]

    def keep(head, tile, states):
        for index, state in enumerate(states):
            lanes = lane_block(4 * tile + index)
            num[lane_block(head), lanes] = state[0]
            stat[head, 0:1, lanes] = state[1]
            stat[head, 1:2, lanes] = state[2]
        num_copy(head, tile).start()

    def finish_late(head, nums, stats, coarse_num, coarse_stats):
        states = []
        for block in range(4):
            unit = block // 2
            coarse = (2.0 * coarse_num[:, lane_block(unit)], coarse_stats[unit][0], 2.0 * coarse_stats[unit][1])
            states.append(merge((nums[block],) + stats[block], coarse))
        keep(head, 1, states)

    for piece in dot_pieces(0):
        piece()
    pending = None
    for head in range(heads):
        pieces = dot_pieces(head + 1) if head + 1 < heads else []

        def more():
            if pieces:
                pieces.pop(0)()

        coarse_stats = [soft_c(head, 0)]
        more()
        if pending is not None:
            pending()
        coarse_stats.append(soft_c(head, 1))
        more()
        coarse_num = dot_first(coarse_v[:, lane_block(head)], probs_c[head % 2])
        late_stats = []
        for block in range(2):
            late_stats.append(soft_a(head, 1, block))
            more()
        for block in range(2):
            late_stats.append(soft_b(head, 1, block))
            more()
        nums = weigh(head, 1)
        stats = [soft_a(head, 0, 0)]
        more()
        stats.append(soft_a(head, 0, 1))
        finish_late(head, nums, late_stats, coarse_num, coarse_stats)
        for block in range(2):
            stats.append(soft_b(head, 0, block))

        def pending(head=head, stats=stats):
            keep(head, 0, [(item,) + pair for item, pair in zip(weigh(head, 0), stats)])

    pending()
    sends.append(pltpu.make_async_copy(stat, stat_out, sems.at[5]))
    sends[-1].start()
    for send in sends:
        send.wait()
    for head in range(heads):
        for tile in range(2):
            num_copy(head, tile).wait()


def near_call(queries, keys, values, levels, index):
    pool = as_bf16(padded(np.concatenate([pool_rows(level) for level in range(levels + 1)]), 16))
    first, heads = SLICES[index]
    width = heads * HEAD
    _, far_rows = far_offsets(levels)
    bf16, f32 = jnp.bfloat16, jnp.float32
    return pl.pallas_call(
        functools.partial(near_kernel, levels, first, heads),
        in_specs=[HBM] * 4,
        out_specs=[HBM] * 3,
        out_shape=[
            jax.ShapeDtypeStruct((width, TOK), f32),
            jax.ShapeDtypeStruct((heads, 8, TOK), f32),
            jax.ShapeDtypeStruct((far_rows, width), bf16),
        ],
        scratch_shapes=[
            pltpu.VMEM(pool.shape, bf16),
            pltpu.VMEM((TOK, width), bf16),
            pltpu.VMEM((TOK, width), bf16),
            pltpu.VMEM((TOK, width), bf16),
            pltpu.VMEM((width, TOK), f32),
            pltpu.VMEM((heads, 8, TOK), f32),
            pltpu.VMEM((far_rows, width), bf16),
            pltpu.VMEM((TOK, width), bf16),
            pltpu.VMEM((BLOCK, width), bf16),
            pltpu.VMEM((BLOCK, width), bf16),
            pltpu.VMEM((BLOCK, width), bf16),
            pltpu.VMEM((BLOCK, BLOCK), f32),
            pltpu.VMEM((2, 2, BLOCK, 2 * BLOCK), f32),
            pltpu.VMEM((2, 2, BLOCK, BLOCK), f32),
            pltpu.VMEM((2, BLOCK, BLOCK), f32),
            pltpu.VMEM((2, 2, BLOCK, 2 * BLOCK), bf16),
            pltpu.VMEM((2, 2, BLOCK, BLOCK), bf16),
            pltpu.VMEM((2, BLOCK, BLOCK), bf16),
            pltpu.SemaphoreType.DMA((6,)),
            pltpu.SemaphoreType.DMA((heads, 2)),
        ],
        compiler_params=pltpu.CompilerParams(vmem_limit_bytes=VMEM_CLAIM),
        cost_estimate=pl.CostEstimate(flops=8_000_000_000, bytes_accessed=4 * MIB, transcendentals=0),
        name="near_levels",
    )(pool, queries, keys, values)


def by_lane_group(arrays, size):
    lane = lax.broadcasted_iota(jnp.int32, arrays[0].shape, 1)
    result = arrays[-1]
    for index in range(len(arrays) - 2, -1, -1):
        result = jnp.where(lane < (index + 1) * size, arrays[index], result)
    return result


def widen_to_second(array):
    r32, r64, r96 = [pltpu.roll(array, shift, 1) for shift in (32, 64, 96)]
    return [by_lane_group([array, r32, r32, r64], 32), by_lane_group([r64, r96, r96, array], 32)]


def widen_to_units(arrays):
    units = []
    for array in arrays:
        turned = pltpu.roll(array, 64, 1)
        units += [by_lane_group([array, turned], 64), by_lane_group([turned, array], 64)]
    return units


def far_kernel(levels, plan, flags_ref, *refs):
    crossing = range(FIRST, levels + 1)
    bundles = 1 + max(bundle for _, bundle, _ in plan)
    kv_refs = refs[:bundles]
    refs = refs[bundles:]
    slices = len(SLICES)
    far_refs, num_refs, stat_refs = refs[:slices], refs[slices : 2 * slices], refs[2 * slices : 3 * slices]
    turn_ref, w_ref, out_ref = refs[3 * slices : 3 * slices + 3]
    kv, queries, num, stat, turn, weights, scores, probs = refs[3 * slices + 3 : 3 * slices + 11]
    mixed, natural, stage, kv_sems, near_sems, out_sems = refs[3 * slices + 11 :]
    pair = 2 * HEAD
    model = w_ref.shape[1]
    step = 512
    offsets, far_rows = far_offsets(levels)

    def kv_copies(index):
        cols = slice(index * pair, (index + 1) * pair)
        made = []
        for number, (level, bundle, spans) in enumerate(plan):
            source_start, target_start, rows = spans
            made.append(
                pltpu.make_async_copy(
                    kv_refs[bundle].at[:, source_start : source_start + rows, cols],
                    kv.at[level - FIRST, :, target_start : target_start + rows, cols],
                    kv_sems.at[index, number],
                )
            )
        return made

    far_copies, near_copies = [], []
    for index, (first, heads) in enumerate(SLICES):
        cols = slice(first * HEAD, (first + heads) * HEAD)
        group = slice(first, first + heads)
        sems = [near_sems.at[place * slices + index] for place in range(3)]
        far_copies.append(pltpu.make_async_copy(far_refs[index], queries.at[:, cols], sems[0]))
        near_copies.append(
            [
                pltpu.make_async_copy(num_refs[index], num.at[cols, :], sems[1]),
                pltpu.make_async_copy(stat_refs[index], stat.at[group], sems[2]),
            ]
        )
    last_copies = [
        pltpu.make_async_copy(turn_ref, turn, near_sems.at[3 * slices]),
        pltpu.make_async_copy(w_ref, weights, near_sems.at[3 * slices + 1]),
    ]
    for copy in far_copies + kv_copies(0) + kv_copies(1) + near_copies[0]:
        copy.start()
    for index in range(2, HEADS // 2):
        for copy in kv_copies(index):
            copy.start()
    for copies in near_copies[1:]:
        for copy in copies:
            copy.start()
    for copy in last_copies:
        copy.start()

    def score(head, level):
        own = lane_block(head)
        span = slice(offsets[level], offsets[level] + UNITS * count_of(level))
        scores[head % 2, :, span] = dot_t(kv[level - FIRST, 0, :, own], queries[span, own])

    def soft(head, level):
        blocks = range(offsets[level] // HEAD, (offsets[level] + UNITS * count_of(level)) // HEAD)
        return [
            soft_columns(
                [lambda span, block=block: scores[head % 2, span, lane_block(block)]], [probs.at[head % 2, :, lane_block(block)]]
            )
            for block in blocks
        ]

    def weigh(head, level, stats):
        own = lane_block(head)
        span = slice(offsets[level], offsets[level] + UNITS * count_of(level))
        live = flags_ref[level - FIRST] == 1
        factor = jnp.where(live, 2.0**level, 0.0)
        weighted = factor * dot_first(kv[level - FIRST, 1, :, own], probs[head % 2, :, span])
        return [
            (weighted[:, lane_block(block)], jnp.where(live, peak, NEG), factor * total)
            for block, (peak, total) in enumerate(stats)
        ]

    def join(state, terms):
        if state is None:
            return terms
        if len(terms) > len(state):
            wide = [widen_to_second(item) for item in state[0]]
            state = [tuple(item[side] for item in wide) for side in range(2)]
        return [merge(old, new) for old, new in zip(state, terms)]

    def mix(head, state):
        own = lane_block(head)
        wide = [widen_to_units([half[place] for half in state]) for place in range(3)]
        for unit in range(UNITS):
            far_num, far_peak, far_total = [item[unit] for item in wide]
            for block in range(2 * unit, 2 * unit + 2):
                peak = stat[head, 0:1, lane_block(block)]
                total = stat[head, 1:2, lane_block(block)]
                top = jnp.maximum(peak, far_peak)
                a = jnp.exp(peak - top)
                b = jnp.exp(far_peak - top)
                inverse = 1.0 / (a * total + b * far_total)
                both = (a * inverse) * num[own, lane_block(block)] + (b * inverse) * far_num
                mixed[own, lane_block(block)] = both.astype(jnp.bfloat16)

    order = list(range(levels, FIRST - 1, -1))
    for copy in far_copies + kv_copies(0):
        copy.wait()
    for level in order:
        score(0, level)
    for copy in near_copies[0]:
        copy.wait()
    pending = None
    for head in range(HEADS):
        if head % 2 == 1 and head + 1 < HEADS:
            for copy in kv_copies((head + 1) // 2):
                copy.wait()
        for index, (first, _) in enumerate(SLICES):
            if index and first == head:
                for copy in near_copies[index]:
                    copy.wait()
        terms = []
        for level in order:
            stats = soft(head, level)
            if head + 1 < HEADS:
                score(head + 1, level)
            if level == order[0] and pending is not None:
                pending()
            terms.append(weigh(head, level, stats))

        def pending(head=head, terms=terms):
            mix(head, functools.reduce(join, terms, None))

    pending()

    for copy in last_copies:
        copy.wait()
    for unit in range(UNITS):
        rows = slice(unit * BLOCK, (unit + 1) * BLOCK)
        natural[rows, :] = dot_t(turn[...], mixed[:, rows]).astype(jnp.bfloat16)
    sends = []
    for index in range(model // step):
        cols = slice(index * step, (index + 1) * step)
        stage[:, cols] = dot(natural[...], weights[:, cols]).astype(jnp.bfloat16)
        sends.append(pltpu.make_async_copy(stage.at[:, cols], out_ref.at[:, cols], out_sems.at[index]))
        sends[-1].start()
    for send in sends:
        send.wait()


def far_call(flags, bundles, plan, near, w_out, levels):
    turn = np.zeros((BLOCK, BLOCK))
    turn[token_of(np.arange(BLOCK)), np.arange(BLOCK)] = 1.0
    nums, stats, fars = [[item[place] for item in near] for place in range(3)]
    model = w_out.shape[1]
    _, far_rows = far_offsets(levels)
    count = levels - FIRST + 1
    bf16, f32 = jnp.bfloat16, jnp.float32
    return pl.pallas_call(
        functools.partial(far_kernel, levels, plan),
        in_specs=[pl.BlockSpec(memory_space=pltpu.SMEM)] + [HBM] * (len(bundles) + 3 * len(SLICES) + 2),
        out_specs=HBM,
        out_shape=jax.ShapeDtypeStruct((TOK, model), bf16),
        scratch_shapes=[
            pltpu.VMEM((count, 2, BLOCK, WIDTH), bf16),
            pltpu.VMEM((far_rows, WIDTH), bf16),
            pltpu.VMEM((WIDTH, TOK), f32),
            pltpu.VMEM((HEADS, 8, TOK), f32),
            pltpu.VMEM((BLOCK, BLOCK), bf16),
            pltpu.VMEM((WIDTH, model), bf16),
            pltpu.VMEM((2, BLOCK, far_rows), f32),
            pltpu.VMEM((2, BLOCK, far_rows), bf16),
            pltpu.VMEM((WIDTH, TOK), bf16),
            pltpu.VMEM((TOK, WIDTH), bf16),
            pltpu.VMEM((TOK, model), bf16),
            pltpu.SemaphoreType.DMA((HEADS // 2, len(plan))),
            pltpu.SemaphoreType.DMA((3 * len(SLICES) + 2,)),
            pltpu.SemaphoreType.DMA((model // 512,)),
        ],
        compiler_params=pltpu.CompilerParams(vmem_limit_bytes=VMEM_CLAIM),
        cost_estimate=pl.CostEstimate(flops=6_500_000_000, bytes_accessed=18 * MIB, transcendentals=3_000_000),
        name="far_levels_projection",
    )(flags, *bundles, *fars, *nums, *stats, as_bf16(turn), w_out)


def moved(array, distance, upper_of=0):
    size = lax.axis_size("seq")
    pairs = [(i ^ distance, i) for i in range(size) if not upper_of or i & upper_of]
    return lax.ppermute(array, "seq", pairs)


def gathered(blocks, distance):
    sent = jnp.concatenate(blocks, axis=1) if len(blocks) > 1 else blocks[0]
    got = moved(sent, distance)
    joined, start = [], 0
    for block in blocks:
        rows = block.shape[1]
        joined.append(jnp.concatenate([block, got[:, start : start + rows]], axis=1))
        start += rows
    return joined


def after(arrays, others):
    return lax.optimization_barrier((arrays, others))[0]


def on_device(queries, keys, values, w_out):
    size = lax.axis_size("seq")
    levels = (TOK * size // (2 * BLOCK)).bit_length() - 1
    position = lax.axis_index("seq")
    flags = jnp.stack([(position >> (level - FIRST)) & 1 for level in range(FIRST, levels + 1)]).astype(jnp.int32)
    pooled = pool_call(keys, values, levels)

    places, _ = packed(levels)
    blocks = {level: pooled[level - FIRST] for level in range(FIRST, TOP)}
    for level in range(TOP, levels + 1):
        place, first = places[level]
        blocks[level] = pooled[place][:, first : first + (TOK >> level)]
    high = list(range(TOP, levels + 1))

    for distance in [1 << (level - FIRST) for level in high]:
        members = [level for level in high if 1 << (level - FIRST) >= distance]
        sent = pooled[-1] if distance == GROUP else jnp.concatenate([blocks[level] for level in members], axis=1)
        got = moved(sent, distance, distance if len(members) == 1 else 0)
        start = 0
        for level in members:
            rows = blocks[level].shape[1]
            piece = got[:, start : start + rows]
            start += rows
            if 1 << (level - FIRST) == distance:
                blocks[level] = piece
            else:
                blocks[level] = jnp.concatenate([blocks[level], piece], axis=1)
        if distance == GROUP:
            fourth = moved(blocks[4], 4, 4)
            third = moved(blocks[3], 2, 2)
            second = moved(blocks[2], 1, 1)
            arrived = blocks[TOP]

    upper = [blocks[level] for level in high[1:]]
    five = gathered([arrived], 2)
    near = [near_call(after(queries, arrived), keys, values, levels, 0)]
    upper = gathered(after(upper, near[0]), 4)
    five_y = gathered(after(five, near[0]), 4)
    fourth = gathered([after(fourth, near[0])], 2)[0]
    near.append(near_call(after(queries, (near[0], five)), keys, values, levels, 1))
    upper_x = gathered(after(upper, near[1]), 2)
    low = jnp.concatenate([after(third, near[1]), fourth], axis=1)
    low_got = moved(low, 1)
    near.append(near_call(after(queries, (near[1], upper, five_y)), keys, values, levels, 2))
    top = jnp.concatenate(after(five_y + upper_x, near[2]), axis=1)
    top_got = moved(top, 1)
    plan = [(2, 4, (0, 0, BLOCK))]
    for level in (3, 4):
        plan += [(level, bundle, ((level - 3) * 128, bundle * 128, 128)) for bundle in (0, 1)]
    for level in high:
        plan += [(level, bundle, ((level - TOP) * 128, (bundle - 2) * 128, 128)) for bundle in (2, 3)]
    return far_call(flags, [low, low_got, top, top_got, second], plan, near, w_out, levels)


def solution(mesh):
    return jax.shard_map(
        on_device,
        mesh=mesh,
        in_specs=(P("seq", None), P("seq", None), P("seq", None), P()),
        out_specs=P("seq", None),
        check_vma=False,
    )
```

```python
import functools

import jax
import jax.numpy as jnp
import numpy as np
from jax import lax
from jax.experimental import pallas as pl
from jax.experimental.pallas import tpu as pltpu
from jax.sharding import PartitionSpec as P

HEADS = 8
HEAD = 128
BLOCK = 256
TOK = 1024
UNITS = TOK // BLOCK
WIDTH = HEADS * HEAD
NEG = -1e30
FIRST = 2
TOP = 5
GROUP = 8
SCALE = HEAD**-0.5
LOG2E = 1.4426950408889634
MIB = 1 << 20
SLICES = ((0, 3), (3, 3), (6, 2))
VMEM_CLAIM = 60 * MIB
HBM = pl.BlockSpec(memory_space=pltpu.HBM)


def token_of(position):
    return ((position & 31) << 3) | (((position >> 5) & 1) << 2) | (((position >> 6) & 1) << 1) | (position >> 7)


def count_of(level):
    return max(BLOCK >> level, 32)


def pool_rows(level):
    rows = token_of(np.arange(count_of(level))) >> level
    columns = np.arange(BLOCK) >> level
    return (rows[:, None] == columns[None, :]) * 2.0**-level


def natural_pool(level, span):
    rows = np.arange(span >> level)
    return (rows[:, None] == (np.arange(span) >> level)[None, :]) * 2.0**-level


def padded(array, multiple):
    return np.pad(array, ((0, -len(array) % multiple), (0, 0)))


def as_bf16(array):
    return jnp.asarray(array.astype(np.float32)).astype(jnp.bfloat16)


def dot(a, b):
    return jnp.dot(a, b, preferred_element_type=jnp.float32)


def dot_t(a, b):
    return lax.dot_general(a, b, (((1,), (1,)), ((), ())), preferred_element_type=jnp.float32)


def dot_first(a, b):
    return lax.dot_general(a, b, (((0,), (0,)), ((), ())), preferred_element_type=jnp.float32)


def merge(first, second):
    top = jnp.maximum(first[1], second[1])
    a = jnp.exp(first[1] - top)
    b = jnp.exp(second[1] - top)
    return (a * first[0] + b * second[0], top, a * first[2] + b * second[2])


ROWS = 64


def soft_columns(loads, targets):
    spans = [slice(start, start + ROWS) for start in range(0, BLOCK, ROWS)]
    peak = None
    for load in loads:
        for span in spans:
            rows = jnp.max(load(span).reshape(ROWS // 8, 8, HEAD), axis=0)
            peak = rows if peak is None else jnp.maximum(peak, rows)
    peak = jnp.max(peak, axis=0, keepdims=True)
    total = jnp.zeros((8, HEAD), jnp.float32)
    for load, target in zip(loads, targets):
        for span in spans:
            probs = jnp.exp2((load(span) - peak) * (SCALE * LOG2E))
            total = total + jnp.sum(probs.reshape(ROWS // 8, 8, HEAD), axis=0)
            target[span, :] = probs.astype(jnp.bfloat16)
    return peak * SCALE, jnp.sum(total, axis=0, keepdims=True)


def packed(levels):
    places, rows = {level: (level - FIRST, 0) for level in range(FIRST, TOP)}, 0
    for level in range(TOP, levels + 1):
        places[level] = (TOP - FIRST, rows)
        rows += TOK >> level
    return places, [TOK >> level for level in range(FIRST, TOP)] + [rows]


def pool_kernel(levels, small_ref, large_ref, keys_ref, values_ref, *refs):
    places, sizes = packed(levels)
    count = len(sizes)
    targets, (small, large, buffers, *outs, sems, out_sems) = refs[:count], refs[count:]
    step = WIDTH // 4
    fixed = [pltpu.make_async_copy(small_ref, small, sems.at[8]), pltpu.make_async_copy(large_ref, large, sems.at[9])]
    copies = []
    for index, source in enumerate((keys_ref, values_ref)):
        for part in range(4):
            cols = slice(part * step, (part + 1) * step)
            copies.append(pltpu.make_async_copy(source.at[:, cols], buffers.at[index, :, cols], sems.at[index * 4 + part]))
    for copy in fixed + copies:
        copy.start()
    for copy in fixed:
        copy.wait()
    sends = []
    for index in range(2):
        for part in range(4):
            cols = slice(part * step, (part + 1) * step)
            copies[index * 4 + part].wait()
            tiles = [
                dot(small[...], buffers[index, i * 2 * BLOCK : (i + 1) * 2 * BLOCK, cols]) for i in range(UNITS // 2)
            ]
            offset = 0
            for level in range(FIRST, min(levels, 6) + 1):
                rows = 2 * BLOCK >> level
                both = jnp.concatenate([tile[offset : offset + rows] for tile in tiles], axis=0)
                place, first = places[level]
                outs[place][index, first : first + 2 * rows, cols] = both.astype(jnp.bfloat16)
                offset += rows
            if levels > 6:
                rest = dot(large[...], buffers[index, :, cols])
                for level in range(7, levels + 1):
                    start = (level - 7) * 8
                    place, first = places[level]
                    outs[place][index, first : first + (TOK >> level), cols] = rest[start : start + (TOK >> level)].astype(jnp.bfloat16)
        for place, (out, target) in enumerate(zip(outs, targets)):
            sends.append(pltpu.make_async_copy(out.at[index], target.at[index], out_sems.at[index, place]))
            sends[-1].start()
    for send in sends:
        send.wait()


def pool_call(keys, values, levels):
    small = as_bf16(padded(np.concatenate([natural_pool(level, 2 * BLOCK) for level in range(FIRST, min(levels, 6) + 1)]), 16))
    parts = [padded(natural_pool(level, TOK), 8) for level in range(7, levels + 1)] + [np.zeros((8, TOK))]
    large = as_bf16(padded(np.concatenate(parts), 16))
    _, sizes = packed(levels)
    return pl.pallas_call(
        functools.partial(pool_kernel, levels),
        in_specs=[HBM] * 4,
        out_specs=[HBM] * len(sizes),
        out_shape=[jax.ShapeDtypeStruct((2, rows, WIDTH), jnp.bfloat16) for rows in sizes],
        scratch_shapes=[
            pltpu.VMEM(small.shape, jnp.bfloat16),
            pltpu.VMEM(large.shape, jnp.bfloat16),
            pltpu.VMEM((2, TOK, WIDTH), jnp.bfloat16),
        ]
        + [pltpu.VMEM((2, rows, WIDTH), jnp.bfloat16) for rows in sizes]
        + [
            pltpu.SemaphoreType.DMA((10,)),
            pltpu.SemaphoreType.DMA((2, len(sizes))),
        ],
        compiler_params=pltpu.CompilerParams(vmem_limit_bytes=VMEM_CLAIM),
        cost_estimate=pl.CostEstimate(flops=2 * 256 * 512 * 4096, bytes_accessed=6 * MIB, transcendentals=0),
        name="pool_keys_values",
    )(small, large, keys, values)


def far_offsets(levels):
    offsets, total = {}, 0
    for level in range(FIRST, levels + 1):
        offsets[level] = total
        total += UNITS * count_of(level)
    return offsets, total


def lane_block(index):
    return slice(index * HEAD, (index + 1) * HEAD)


def near_kernel(levels, first, heads, pool_ref, q_ref, k_ref, v_ref, num_out, stat_out, far_out, *scratch):
    (pool, q, k, v, num, stat, far, ordered, coarse_q, coarse_k, coarse_v, bias, scores_a, scores_b, scores_c) = scratch[:15]
    probs_a, probs_b, probs_c, sems, head_sems = scratch[15:]
    width = heads * HEAD
    cols = slice(first * HEAD, first * HEAD + width)
    copies = [
        pltpu.make_async_copy(pool_ref, pool, sems.at[0]),
        pltpu.make_async_copy(q_ref.at[:, cols], q, sems.at[1]),
        pltpu.make_async_copy(k_ref.at[:, cols], k, sems.at[2]),
        pltpu.make_async_copy(v_ref.at[:, cols], v, sems.at[3]),
    ]
    for copy in copies:
        copy.start()
    row = lax.broadcasted_iota(jnp.int32, (BLOCK, BLOCK), 0)
    position = lax.broadcasted_iota(jnp.int32, (BLOCK, BLOCK), 1)
    bias[...] = jnp.where(row <= token_of(position), 0.0, NEG)
    copies[0].wait()
    copies[1].wait()

    offsets, _ = far_offsets(levels)
    for unit in range(UNITS):
        pooled = dot(pool[...], q[unit * BLOCK : (unit + 1) * BLOCK, :])
        ordered[unit * BLOCK : (unit + 1) * BLOCK, :] = pooled[:BLOCK].astype(jnp.bfloat16)
        if unit >= 2:
            coarse_q[(unit - 2) * 128 : (unit - 1) * 128, :] = pooled[BLOCK : BLOCK + 128].astype(jnp.bfloat16)
        start = BLOCK + 128
        for level in range(FIRST, levels + 1):
            count = count_of(level)
            place = offsets[level] + unit * count
            far[place : place + count, :] = pooled[start : start + count].astype(jnp.bfloat16)
            start += count
    sends = [pltpu.make_async_copy(far, far_out, sems.at[4])]
    sends[0].start()
    copies[2].wait()
    copies[3].wait()
    for unit in range(2):
        rows = slice(unit * BLOCK, (unit + 1) * BLOCK)
        half = slice(unit * 128, (unit + 1) * 128)
        coarse_k[half, :] = dot(pool[BLOCK : BLOCK + 128, :], k[rows, :]).astype(jnp.bfloat16)
        coarse_v[half, :] = dot(pool[BLOCK : BLOCK + 128, :], v[rows, :]).astype(jnp.bfloat16)

    def num_copy(head, tile):
        rows = lane_block(head)
        lanes = slice(tile * 2 * BLOCK, (tile + 1) * 2 * BLOCK)
        return pltpu.make_async_copy(num.at[rows, lanes], num_out.at[rows, lanes], head_sems.at[head, tile])

    def dot_pieces(head):
        slot, own = head % 2, lane_block(head)

        def coarse():
            scores_c[slot] = dot_t(coarse_k[:, own], coarse_q[:, own])

        def part(tile, piece):
            base = 2 * tile * BLOCK
            if piece < 2:
                rows = slice(base + piece * BLOCK, base + (piece + 1) * BLOCK)
                scores_a[slot, tile, :, piece * BLOCK : (piece + 1) * BLOCK] = dot_t(
                    k[base : base + BLOCK, own], ordered[rows, own]
                )
            else:
                rows = slice(base + BLOCK, base + 2 * BLOCK)
                scores_b[slot, tile] = dot_t(k[rows, own], ordered[rows, own])

        return [coarse] + [functools.partial(part, tile, piece) for tile in (1, 0) for piece in range(3)]

    def soft_a(head, tile, block):
        slot, lanes = head % 2, lane_block(block)
        return soft_columns(
            [lambda span: scores_a[slot, tile, span, lanes] + bias[span, lanes]], [probs_a.at[slot, tile, :, lanes]]
        )

    def soft_b(head, tile, block):
        slot, lanes, late = head % 2, lane_block(block), lane_block(2 + block)
        return soft_columns(
            [
                lambda span: scores_a[slot, tile, span, late],
                lambda span: scores_b[slot, tile, span, lanes] + bias[span, lanes],
            ],
            [probs_a.at[slot, tile, :, late], probs_b.at[slot, tile, :, lanes]],
        )

    def soft_c(head, block):
        slot, lanes = head % 2, lane_block(block)
        return soft_columns([lambda span: scores_c[slot, span, lanes]], [probs_c.at[slot, :, lanes]])

    def weigh(head, tile):
        slot, own, base = head % 2, lane_block(head), 2 * tile * BLOCK
        both = dot_first(v[base : base + BLOCK, own], probs_a[slot, tile])
        more = dot_first(v[base + BLOCK : base + 2 * BLOCK, own], probs_b[slot, tile])
        nums = [both[:, lane_block(0)], both[:, lane_block(1)]]
        return nums + [both[:, lane_block(2 + block)] + more[:, lane_block(block)] for block in range(2)]

    def keep(head, tile, states):
        for index, state in enumerate(states):
            lanes = lane_block(4 * tile + index)
            num[lane_block(head), lanes] = state[0]
            stat[head, 0:1, lanes] = state[1]
            stat[head, 1:2, lanes] = state[2]
        num_copy(head, tile).start()

    def finish_late(head, nums, stats, coarse_num, coarse_stats):
        states = []
        for block in range(4):
            unit = block // 2
            coarse = (2.0 * coarse_num[:, lane_block(unit)], coarse_stats[unit][0], 2.0 * coarse_stats[unit][1])
            states.append(merge((nums[block],) + stats[block], coarse))
        keep(head, 1, states)

    for piece in dot_pieces(0):
        piece()
    pending = None
    for head in range(heads):
        pieces = dot_pieces(head + 1) if head + 1 < heads else []

        def more():
            if pieces:
                pieces.pop(0)()

        coarse_stats = [soft_c(head, 0)]
        more()
        if pending is not None:
            pending()
        coarse_stats.append(soft_c(head, 1))
        more()
        coarse_num = dot_first(coarse_v[:, lane_block(head)], probs_c[head % 2])
        late_stats = []
        for block in range(2):
            late_stats.append(soft_a(head, 1, block))
            more()
        for block in range(2):
            late_stats.append(soft_b(head, 1, block))
            more()
        nums = weigh(head, 1)
        stats = [soft_a(head, 0, 0)]
        more()
        stats.append(soft_a(head, 0, 1))
        finish_late(head, nums, late_stats, coarse_num, coarse_stats)
        for block in range(2):
            stats.append(soft_b(head, 0, block))

        def pending(head=head, stats=stats):
            keep(head, 0, [(item,) + pair for item, pair in zip(weigh(head, 0), stats)])

    pending()
    sends.append(pltpu.make_async_copy(stat, stat_out, sems.at[5]))
    sends[-1].start()
    for send in sends:
        send.wait()
    for head in range(heads):
        for tile in range(2):
            num_copy(head, tile).wait()


def near_call(queries, keys, values, levels, index):
    pool = as_bf16(padded(np.concatenate([pool_rows(level) for level in range(levels + 1)]), 16))
    first, heads = SLICES[index]
    width = heads * HEAD
    _, far_rows = far_offsets(levels)
    bf16, f32 = jnp.bfloat16, jnp.float32
    return pl.pallas_call(
        functools.partial(near_kernel, levels, first, heads),
        in_specs=[HBM] * 4,
        out_specs=[HBM] * 3,
        out_shape=[
            jax.ShapeDtypeStruct((width, TOK), f32),
            jax.ShapeDtypeStruct((heads, 8, TOK), f32),
            jax.ShapeDtypeStruct((far_rows, width), bf16),
        ],
        scratch_shapes=[
            pltpu.VMEM(pool.shape, bf16),
            pltpu.VMEM((TOK, width), bf16),
            pltpu.VMEM((TOK, width), bf16),
            pltpu.VMEM((TOK, width), bf16),
            pltpu.VMEM((width, TOK), f32),
            pltpu.VMEM((heads, 8, TOK), f32),
            pltpu.VMEM((far_rows, width), bf16),
            pltpu.VMEM((TOK, width), bf16),
            pltpu.VMEM((BLOCK, width), bf16),
            pltpu.VMEM((BLOCK, width), bf16),
            pltpu.VMEM((BLOCK, width), bf16),
            pltpu.VMEM((BLOCK, BLOCK), f32),
            pltpu.VMEM((2, 2, BLOCK, 2 * BLOCK), f32),
            pltpu.VMEM((2, 2, BLOCK, BLOCK), f32),
            pltpu.VMEM((2, BLOCK, BLOCK), f32),
            pltpu.VMEM((2, 2, BLOCK, 2 * BLOCK), bf16),
            pltpu.VMEM((2, 2, BLOCK, BLOCK), bf16),
            pltpu.VMEM((2, BLOCK, BLOCK), bf16),
            pltpu.SemaphoreType.DMA((6,)),
            pltpu.SemaphoreType.DMA((heads, 2)),
        ],
        compiler_params=pltpu.CompilerParams(vmem_limit_bytes=VMEM_CLAIM),
        cost_estimate=pl.CostEstimate(flops=8_000_000_000, bytes_accessed=4 * MIB, transcendentals=0),
        name="near_levels",
    )(pool, queries, keys, values)


def by_lane_group(arrays, size):
    lane = lax.broadcasted_iota(jnp.int32, arrays[0].shape, 1)
    result = arrays[-1]
    for index in range(len(arrays) - 2, -1, -1):
        result = jnp.where(lane < (index + 1) * size, arrays[index], result)
    return result


def widen_to_second(array):
    r32, r64, r96 = [pltpu.roll(array, shift, 1) for shift in (32, 64, 96)]
    return [by_lane_group([array, r32, r32, r64], 32), by_lane_group([r64, r96, r96, array], 32)]


def widen_to_units(arrays):
    units = []
    for array in arrays:
        turned = pltpu.roll(array, 64, 1)
        units += [by_lane_group([array, turned], 64), by_lane_group([turned, array], 64)]
    return units


def far_kernel(levels, plan, flags_ref, *refs):
    crossing = range(FIRST, levels + 1)
    bundles = 1 + max(bundle for _, bundle, _ in plan)
    kv_refs = refs[:bundles]
    refs = refs[bundles:]
    slices = len(SLICES)
    far_refs, num_refs, stat_refs = refs[:slices], refs[slices : 2 * slices], refs[2 * slices : 3 * slices]
    turn_ref, w_ref, out_ref = refs[3 * slices : 3 * slices + 3]
    kv, queries, num, stat, turn, weights, scores, probs = refs[3 * slices + 3 : 3 * slices + 11]
    mixed, natural, stage, kv_sems, near_sems, out_sems = refs[3 * slices + 11 :]
    pair = 2 * HEAD
    model = w_ref.shape[1]
    step = 512
    offsets, far_rows = far_offsets(levels)

    def kv_copies(index):
        cols = slice(index * pair, (index + 1) * pair)
        made = []
        for number, (level, bundle, spans) in enumerate(plan):
            source_start, target_start, rows = spans
            made.append(
                pltpu.make_async_copy(
                    kv_refs[bundle].at[:, source_start : source_start + rows, cols],
                    kv.at[level - FIRST, :, target_start : target_start + rows, cols],
                    kv_sems.at[index, number],
                )
            )
        return made

    far_copies, near_copies = [], []
    for index, (first, heads) in enumerate(SLICES):
        cols = slice(first * HEAD, (first + heads) * HEAD)
        group = slice(first, first + heads)
        sems = [near_sems.at[place * slices + index] for place in range(3)]
        far_copies.append(pltpu.make_async_copy(far_refs[index], queries.at[:, cols], sems[0]))
        near_copies.append(
            [
                pltpu.make_async_copy(num_refs[index], num.at[cols, :], sems[1]),
                pltpu.make_async_copy(stat_refs[index], stat.at[group], sems[2]),
            ]
        )
    last_copies = [
        pltpu.make_async_copy(turn_ref, turn, near_sems.at[3 * slices]),
        pltpu.make_async_copy(w_ref, weights, near_sems.at[3 * slices + 1]),
    ]
    for copy in far_copies + kv_copies(0) + kv_copies(1) + near_copies[0]:
        copy.start()
    for index in range(2, HEADS // 2):
        for copy in kv_copies(index):
            copy.start()
    for copies in near_copies[1:]:
        for copy in copies:
            copy.start()
    for copy in last_copies:
        copy.start()

    def score(head, level):
        own = lane_block(head)
        span = slice(offsets[level], offsets[level] + UNITS * count_of(level))
        scores[head % 2, :, span] = dot_t(kv[level - FIRST, 0, :, own], queries[span, own])

    def soft(head, level):
        blocks = range(offsets[level] // HEAD, (offsets[level] + UNITS * count_of(level)) // HEAD)
        return [
            soft_columns(
                [lambda span, block=block: scores[head % 2, span, lane_block(block)]], [probs.at[head % 2, :, lane_block(block)]]
            )
            for block in blocks
        ]

    def weigh(head, level, stats):
        own = lane_block(head)
        span = slice(offsets[level], offsets[level] + UNITS * count_of(level))
        live = flags_ref[level - FIRST] == 1
        factor = jnp.where(live, 2.0**level, 0.0)
        weighted = factor * dot_first(kv[level - FIRST, 1, :, own], probs[head % 2, :, span])
        return [
            (weighted[:, lane_block(block)], jnp.where(live, peak, NEG), factor * total)
            for block, (peak, total) in enumerate(stats)
        ]

    def join(state, terms):
        if state is None:
            return terms
        if len(terms) > len(state):
            wide = [widen_to_second(item) for item in state[0]]
            state = [tuple(item[side] for item in wide) for side in range(2)]
        return [merge(old, new) for old, new in zip(state, terms)]

    def mix(head, state):
        own = lane_block(head)
        wide = [widen_to_units([half[place] for half in state]) for place in range(3)]
        for unit in range(UNITS):
            far_num, far_peak, far_total = [item[unit] for item in wide]
            for block in range(2 * unit, 2 * unit + 2):
                peak = stat[head, 0:1, lane_block(block)]
                total = stat[head, 1:2, lane_block(block)]
                top = jnp.maximum(peak, far_peak)
                a = jnp.exp(peak - top)
                b = jnp.exp(far_peak - top)
                inverse = 1.0 / (a * total + b * far_total)
                both = (a * inverse) * num[own, lane_block(block)] + (b * inverse) * far_num
                mixed[own, lane_block(block)] = both.astype(jnp.bfloat16)

    order = list(range(levels, FIRST - 1, -1))
    for copy in far_copies + kv_copies(0):
        copy.wait()
    for level in order:
        score(0, level)
    for copy in near_copies[0]:
        copy.wait()
    pending = None
    for head in range(HEADS):
        if head % 2 == 1 and head + 1 < HEADS:
            for copy in kv_copies((head + 1) // 2):
                copy.wait()
        for index, (first, _) in enumerate(SLICES):
            if index and first == head:
                for copy in near_copies[index]:
                    copy.wait()
        terms = []
        for level in order:
            stats = soft(head, level)
            if head + 1 < HEADS:
                score(head + 1, level)
            if level == order[0] and pending is not None:
                pending()
            terms.append(weigh(head, level, stats))

        def pending(head=head, terms=terms):
            mix(head, functools.reduce(join, terms, None))

    pending()

    for copy in last_copies:
        copy.wait()
    for unit in range(UNITS):
        rows = slice(unit * BLOCK, (unit + 1) * BLOCK)
        natural[rows, :] = dot_t(turn[...], mixed[:, rows]).astype(jnp.bfloat16)
    sends = []
    for index in range(model // step):
        cols = slice(index * step, (index + 1) * step)
        stage[:, cols] = dot(natural[...], weights[:, cols]).astype(jnp.bfloat16)
        sends.append(pltpu.make_async_copy(stage.at[:, cols], out_ref.at[:, cols], out_sems.at[index]))
        sends[-1].start()
    for send in sends:
        send.wait()


def far_call(flags, bundles, plan, near, w_out, levels):
    turn = np.zeros((BLOCK, BLOCK))
    turn[token_of(np.arange(BLOCK)), np.arange(BLOCK)] = 1.0
    nums, stats, fars = [[item[place] for item in near] for place in range(3)]
    model = w_out.shape[1]
    _, far_rows = far_offsets(levels)
    count = levels - FIRST + 1
    bf16, f32 = jnp.bfloat16, jnp.float32
    return pl.pallas_call(
        functools.partial(far_kernel, levels, plan),
        in_specs=[pl.BlockSpec(memory_space=pltpu.SMEM)] + [HBM] * (len(bundles) + 3 * len(SLICES) + 2),
        out_specs=HBM,
        out_shape=jax.ShapeDtypeStruct((TOK, model), bf16),
        scratch_shapes=[
            pltpu.VMEM((count, 2, BLOCK, WIDTH), bf16),
            pltpu.VMEM((far_rows, WIDTH), bf16),
            pltpu.VMEM((WIDTH, TOK), f32),
            pltpu.VMEM((HEADS, 8, TOK), f32),
            pltpu.VMEM((BLOCK, BLOCK), bf16),
            pltpu.VMEM((WIDTH, model), bf16),
            pltpu.VMEM((2, BLOCK, far_rows), f32),
            pltpu.VMEM((2, BLOCK, far_rows), bf16),
            pltpu.VMEM((WIDTH, TOK), bf16),
            pltpu.VMEM((TOK, WIDTH), bf16),
            pltpu.VMEM((TOK, model), bf16),
            pltpu.SemaphoreType.DMA((HEADS // 2, len(plan))),
            pltpu.SemaphoreType.DMA((3 * len(SLICES) + 2,)),
            pltpu.SemaphoreType.DMA((model // 512,)),
        ],
        compiler_params=pltpu.CompilerParams(vmem_limit_bytes=VMEM_CLAIM),
        cost_estimate=pl.CostEstimate(flops=6_500_000_000, bytes_accessed=18 * MIB, transcendentals=3_000_000),
        name="far_levels_projection",
    )(flags, *bundles, *fars, *nums, *stats, as_bf16(turn), w_out)


def moved(array, distance):
    return lax.ppermute(array, "seq", [(i ^ distance, i) for i in range(lax.axis_size("seq"))])


def gathered(blocks, distance):
    sent = jnp.concatenate(blocks, axis=1) if len(blocks) > 1 else blocks[0]
    got = moved(sent, distance)
    joined, start = [], 0
    for block in blocks:
        rows = block.shape[1]
        joined.append(jnp.concatenate([block, got[:, start : start + rows]], axis=1))
        start += rows
    return joined


def after(arrays, others):
    return lax.optimization_barrier((arrays, others))[0]


def on_device(queries, keys, values, w_out):
    size = lax.axis_size("seq")
    levels = (TOK * size // (2 * BLOCK)).bit_length() - 1
    position = lax.axis_index("seq")
    flags = jnp.stack([(position >> (level - FIRST)) & 1 for level in range(FIRST, levels + 1)]).astype(jnp.int32)
    pooled = pool_call(keys, values, levels)

    places, _ = packed(levels)
    blocks = {level: pooled[level - FIRST] for level in range(FIRST, TOP)}
    for level in range(TOP, levels + 1):
        place, first = places[level]
        blocks[level] = pooled[place][:, first : first + (TOK >> level)]
    high = list(range(TOP, levels + 1))

    for distance in [1 << (level - FIRST) for level in high]:
        members = [level for level in high if 1 << (level - FIRST) >= distance]
        sent = pooled[-1] if distance == GROUP else jnp.concatenate([blocks[level] for level in members], axis=1)
        got = moved(sent, distance)
        start = 0
        for level in members:
            rows = blocks[level].shape[1]
            piece = got[:, start : start + rows]
            start += rows
            if 1 << (level - FIRST) == distance:
                blocks[level] = piece
            else:
                blocks[level] = jnp.concatenate([blocks[level], piece], axis=1)
        if distance == GROUP:
            fourth = moved(blocks[4], 4)
            third = moved(blocks[3], 2)
            second = moved(blocks[2], 1)
            arrived = blocks[TOP]

    upper = [blocks[level] for level in high[1:]]
    five = gathered([arrived], 2)
    near = [near_call(after(queries, arrived), keys, values, levels, 0)]
    upper = gathered(after(upper, near[0]), 4)
    five_y = gathered(after(five, near[0]), 4)
    fourth = gathered([after(fourth, near[0])], 2)[0]
    near.append(near_call(after(queries, (near[0], five)), keys, values, levels, 1))
    upper_x = gathered(after(upper, near[1]), 2)
    low = jnp.concatenate([after(third, near[1]), fourth], axis=1)
    low_got = moved(low, 1)
    near.append(near_call(after(queries, (near[1], upper, five_y)), keys, values, levels, 2))
    top = jnp.concatenate(after(five_y + upper_x, near[2]), axis=1)
    top_got = moved(top, 1)
    plan = [(2, 4, (0, 0, BLOCK))]
    for level in (3, 4):
        plan += [(level, bundle, ((level - 3) * 128, bundle * 128, 128)) for bundle in (0, 1)]
    for level in high:
        plan += [(level, bundle, ((level - TOP) * 128, (bundle - 2) * 128, 128)) for bundle in (2, 3)]
    return far_call(flags, [low, low_got, top, top_got, second], plan, near, w_out, levels)


def solution(mesh):
    return jax.shard_map(
        on_device,
        mesh=mesh,
        in_specs=(P("seq", None), P("seq", None), P("seq", None), P()),
        out_specs=P("seq", None),
        check_vma=False,
    )
```

```python
import functools

import jax
import jax.numpy as jnp
import numpy as np
from jax import lax
from jax.experimental import pallas as pl
from jax.experimental.pallas import tpu as pltpu
from jax.sharding import PartitionSpec as P

HEADS = 8
HEAD = 128
BLOCK = 256
TOK = 1024
UNITS = TOK // BLOCK
WIDTH = HEADS * HEAD
NEG = -1e30
FIRST = 2
TOP = 5
GROUP = 8
SCALE = HEAD**-0.5
LOG2E = 1.4426950408889634
MIB = 1 << 20
SLICES = ((0, 3), (3, 3), (6, 2))
VMEM_CLAIM = 60 * MIB
HBM = pl.BlockSpec(memory_space=pltpu.HBM)


def token_of(position):
    return ((position & 31) << 3) | (((position >> 5) & 1) << 2) | (((position >> 6) & 1) << 1) | (position >> 7)


def count_of(level):
    return max(BLOCK >> level, 32)


def pool_rows(level):
    rows = token_of(np.arange(count_of(level))) >> level
    columns = np.arange(BLOCK) >> level
    return (rows[:, None] == columns[None, :]) * 2.0**-level


def natural_pool(level, span):
    rows = np.arange(span >> level)
    return (rows[:, None] == (np.arange(span) >> level)[None, :]) * 2.0**-level


def padded(array, multiple):
    return np.pad(array, ((0, -len(array) % multiple), (0, 0)))


def as_bf16(array):
    return jnp.asarray(array.astype(np.float32)).astype(jnp.bfloat16)


def dot(a, b):
    return jnp.dot(a, b, preferred_element_type=jnp.float32)


def dot_t(a, b):
    return lax.dot_general(a, b, (((1,), (1,)), ((), ())), preferred_element_type=jnp.float32)


def dot_first(a, b):
    return lax.dot_general(a, b, (((0,), (0,)), ((), ())), preferred_element_type=jnp.float32)


def merge(first, second):
    top = jnp.maximum(first[1], second[1])
    a = jnp.exp(first[1] - top)
    b = jnp.exp(second[1] - top)
    return (a * first[0] + b * second[0], top, a * first[2] + b * second[2])


ROWS = 64


def soft_columns(loads, targets):
    spans = [slice(start, start + ROWS) for start in range(0, BLOCK, ROWS)]
    peak = None
    for load in loads:
        for span in spans:
            rows = jnp.max(load(span).reshape(ROWS // 8, 8, HEAD), axis=0)
            peak = rows if peak is None else jnp.maximum(peak, rows)
    peak = jnp.max(peak, axis=0, keepdims=True)
    total = jnp.zeros((8, HEAD), jnp.float32)
    for load, target in zip(loads, targets):
        for span in spans:
            probs = jnp.exp2((load(span) - peak) * (SCALE * LOG2E))
            total = total + jnp.sum(probs.reshape(ROWS // 8, 8, HEAD), axis=0)
            target[span, :] = probs.astype(jnp.bfloat16)
    return peak * SCALE, jnp.sum(total, axis=0, keepdims=True)


def packed(levels):
    places, rows = {level: (level - FIRST, 0) for level in range(FIRST, TOP)}, 0
    for level in range(TOP, levels + 1):
        places[level] = (TOP - FIRST, rows)
        rows += TOK >> level
    return places, [TOK >> level for level in range(FIRST, TOP)] + [rows]


def pool_kernel(levels, small_ref, large_ref, keys_ref, values_ref, *refs):
    places, sizes = packed(levels)
    count = len(sizes)
    targets, (small, large, buffers, *outs, sems, out_sems) = refs[:count], refs[count:]
    step = WIDTH // 4
    fixed = [pltpu.make_async_copy(small_ref, small, sems.at[8]), pltpu.make_async_copy(large_ref, large, sems.at[9])]
    copies = []
    for index, source in enumerate((keys_ref, values_ref)):
        for part in range(4):
            cols = slice(part * step, (part + 1) * step)
            copies.append(pltpu.make_async_copy(source.at[:, cols], buffers.at[index, :, cols], sems.at[index * 4 + part]))
    for copy in fixed + copies:
        copy.start()
    for copy in fixed:
        copy.wait()
    sends = []
    for index in range(2):
        for part in range(4):
            cols = slice(part * step, (part + 1) * step)
            copies[index * 4 + part].wait()
            tiles = [
                dot(small[...], buffers[index, i * 2 * BLOCK : (i + 1) * 2 * BLOCK, cols]) for i in range(UNITS // 2)
            ]
            offset = 0
            for level in range(FIRST, min(levels, 6) + 1):
                rows = 2 * BLOCK >> level
                both = jnp.concatenate([tile[offset : offset + rows] for tile in tiles], axis=0)
                place, first = places[level]
                outs[place][index, first : first + 2 * rows, cols] = both.astype(jnp.bfloat16)
                offset += rows
            if levels > 6:
                rest = dot(large[...], buffers[index, :, cols])
                for level in range(7, levels + 1):
                    start = (level - 7) * 8
                    place, first = places[level]
                    outs[place][index, first : first + (TOK >> level), cols] = rest[start : start + (TOK >> level)].astype(jnp.bfloat16)
        for place, (out, target) in enumerate(zip(outs, targets)):
            sends.append(pltpu.make_async_copy(out.at[index], target.at[index], out_sems.at[index, place]))
            sends[-1].start()
    for send in sends:
        send.wait()


def pool_call(keys, values, levels):
    small = as_bf16(padded(np.concatenate([natural_pool(level, 2 * BLOCK) for level in range(FIRST, min(levels, 6) + 1)]), 16))
    parts = [padded(natural_pool(level, TOK), 8) for level in range(7, levels + 1)] + [np.zeros((8, TOK))]
    large = as_bf16(padded(np.concatenate(parts), 16))
    _, sizes = packed(levels)
    return pl.pallas_call(
        functools.partial(pool_kernel, levels),
        in_specs=[HBM] * 4,
        out_specs=[HBM] * len(sizes),
        out_shape=[jax.ShapeDtypeStruct((2, rows, WIDTH), jnp.bfloat16) for rows in sizes],
        scratch_shapes=[
            pltpu.VMEM(small.shape, jnp.bfloat16),
            pltpu.VMEM(large.shape, jnp.bfloat16),
            pltpu.VMEM((2, TOK, WIDTH), jnp.bfloat16),
        ]
        + [pltpu.VMEM((2, rows, WIDTH), jnp.bfloat16) for rows in sizes]
        + [
            pltpu.SemaphoreType.DMA((10,)),
            pltpu.SemaphoreType.DMA((2, len(sizes))),
        ],
        compiler_params=pltpu.CompilerParams(vmem_limit_bytes=VMEM_CLAIM),
        cost_estimate=pl.CostEstimate(flops=2 * 256 * 512 * 4096, bytes_accessed=6 * MIB, transcendentals=0),
        name="pool_keys_values",
    )(small, large, keys, values)


def far_offsets(levels):
    offsets, total = {}, 0
    for level in range(FIRST, levels + 1):
        offsets[level] = total
        total += UNITS * count_of(level)
    return offsets, total


def lane_block(index):
    return slice(index * HEAD, (index + 1) * HEAD)


def near_kernel(levels, first, heads, pool_ref, q_ref, k_ref, v_ref, num_out, stat_out, far_out, *scratch):
    (pool, q, k, v, num, stat, far, ordered, coarse_q, coarse_k, coarse_v, bias, scores_a, scores_b, scores_c) = scratch[:15]
    probs_a, probs_b, probs_c, sems, head_sems = scratch[15:]
    width = heads * HEAD
    cols = slice(first * HEAD, first * HEAD + width)
    copies = [
        pltpu.make_async_copy(pool_ref, pool, sems.at[0]),
        pltpu.make_async_copy(q_ref.at[:, cols], q, sems.at[1]),
        pltpu.make_async_copy(k_ref.at[:, cols], k, sems.at[2]),
        pltpu.make_async_copy(v_ref.at[:, cols], v, sems.at[3]),
    ]
    for copy in copies:
        copy.start()
    row = lax.broadcasted_iota(jnp.int32, (BLOCK, BLOCK), 0)
    position = lax.broadcasted_iota(jnp.int32, (BLOCK, BLOCK), 1)
    bias[...] = jnp.where(row <= token_of(position), 0.0, NEG)
    copies[0].wait()
    copies[1].wait()

    offsets, _ = far_offsets(levels)
    for unit in range(UNITS):
        pooled = dot(pool[...], q[unit * BLOCK : (unit + 1) * BLOCK, :])
        ordered[unit * BLOCK : (unit + 1) * BLOCK, :] = pooled[:BLOCK].astype(jnp.bfloat16)
        if unit >= 2:
            coarse_q[(unit - 2) * 128 : (unit - 1) * 128, :] = pooled[BLOCK : BLOCK + 128].astype(jnp.bfloat16)
        start = BLOCK + 128
        for level in range(FIRST, levels + 1):
            count = count_of(level)
            place = offsets[level] + unit * count
            far[place : place + count, :] = pooled[start : start + count].astype(jnp.bfloat16)
            start += count
    sends = [pltpu.make_async_copy(far, far_out, sems.at[4])]
    sends[0].start()
    copies[2].wait()
    copies[3].wait()
    for unit in range(2):
        rows = slice(unit * BLOCK, (unit + 1) * BLOCK)
        half = slice(unit * 128, (unit + 1) * 128)
        coarse_k[half, :] = dot(pool[BLOCK : BLOCK + 128, :], k[rows, :]).astype(jnp.bfloat16)
        coarse_v[half, :] = dot(pool[BLOCK : BLOCK + 128, :], v[rows, :]).astype(jnp.bfloat16)

    def num_copy(head, tile):
        rows = lane_block(head)
        lanes = slice(tile * 2 * BLOCK, (tile + 1) * 2 * BLOCK)
        return pltpu.make_async_copy(num.at[rows, lanes], num_out.at[rows, lanes], head_sems.at[head, tile])

    def dot_pieces(head):
        slot, own = head % 2, lane_block(head)

        def coarse():
            scores_c[slot] = dot_t(coarse_k[:, own], coarse_q[:, own])

        def part(tile, piece):
            base = 2 * tile * BLOCK
            if piece < 2:
                rows = slice(base + piece * BLOCK, base + (piece + 1) * BLOCK)
                scores_a[slot, tile, :, piece * BLOCK : (piece + 1) * BLOCK] = dot_t(
                    k[base : base + BLOCK, own], ordered[rows, own]
                )
            else:
                rows = slice(base + BLOCK, base + 2 * BLOCK)
                scores_b[slot, tile] = dot_t(k[rows, own], ordered[rows, own])

        return [coarse] + [functools.partial(part, tile, piece) for tile in (1, 0) for piece in range(3)]

    def soft_a(head, tile, block):
        slot, lanes = head % 2, lane_block(block)
        return soft_columns(
            [lambda span: scores_a[slot, tile, span, lanes] + bias[span, lanes]], [probs_a.at[slot, tile, :, lanes]]
        )

    def soft_b(head, tile, block):
        slot, lanes, late = head % 2, lane_block(block), lane_block(2 + block)
        return soft_columns(
            [
                lambda span: scores_a[slot, tile, span, late],
                lambda span: scores_b[slot, tile, span, lanes] + bias[span, lanes],
            ],
            [probs_a.at[slot, tile, :, late], probs_b.at[slot, tile, :, lanes]],
        )

    def soft_c(head, block):
        slot, lanes = head % 2, lane_block(block)
        return soft_columns([lambda span: scores_c[slot, span, lanes]], [probs_c.at[slot, :, lanes]])

    def weigh(head, tile):
        slot, own, base = head % 2, lane_block(head), 2 * tile * BLOCK
        both = dot_first(v[base : base + BLOCK, own], probs_a[slot, tile])
        more = dot_first(v[base + BLOCK : base + 2 * BLOCK, own], probs_b[slot, tile])
        nums = [both[:, lane_block(0)], both[:, lane_block(1)]]
        return nums + [both[:, lane_block(2 + block)] + more[:, lane_block(block)] for block in range(2)]

    def keep(head, tile, states):
        for index, state in enumerate(states):
            lanes = lane_block(4 * tile + index)
            num[lane_block(head), lanes] = state[0]
            stat[head, 0:1, lanes] = state[1]
            stat[head, 1:2, lanes] = state[2]
        num_copy(head, tile).start()

    def finish_late(head, nums, stats, coarse_num, coarse_stats):
        states = []
        for block in range(4):
            unit = block // 2
            coarse = (2.0 * coarse_num[:, lane_block(unit)], coarse_stats[unit][0], 2.0 * coarse_stats[unit][1])
            states.append(merge((nums[block],) + stats[block], coarse))
        keep(head, 1, states)

    for piece in dot_pieces(0):
        piece()
    pending = None
    for head in range(heads):
        pieces = dot_pieces(head + 1) if head + 1 < heads else []

        def more():
            if pieces:
                pieces.pop(0)()

        coarse_stats = [soft_c(head, 0)]
        more()
        if pending is not None:
            pending()
        coarse_stats.append(soft_c(head, 1))
        more()
        coarse_num = dot_first(coarse_v[:, lane_block(head)], probs_c[head % 2])
        late_stats = []
        for block in range(2):
            late_stats.append(soft_a(head, 1, block))
            more()
        for block in range(2):
            late_stats.append(soft_b(head, 1, block))
            more()
        nums = weigh(head, 1)
        stats = [soft_a(head, 0, 0)]
        more()
        stats.append(soft_a(head, 0, 1))
        finish_late(head, nums, late_stats, coarse_num, coarse_stats)
        for block in range(2):
            stats.append(soft_b(head, 0, block))

        def pending(head=head, stats=stats):
            keep(head, 0, [(item,) + pair for item, pair in zip(weigh(head, 0), stats)])

    pending()
    sends.append(pltpu.make_async_copy(stat, stat_out, sems.at[5]))
    sends[-1].start()
    for send in sends:
        send.wait()
    for head in range(heads):
        for tile in range(2):
            num_copy(head, tile).wait()


def near_call(queries, keys, values, levels, index):
    pool = as_bf16(padded(np.concatenate([pool_rows(level) for level in range(levels + 1)]), 16))
    first, heads = SLICES[index]
    width = heads * HEAD
    _, far_rows = far_offsets(levels)
    bf16, f32 = jnp.bfloat16, jnp.float32
    return pl.pallas_call(
        functools.partial(near_kernel, levels, first, heads),
        in_specs=[HBM] * 4,
        out_specs=[HBM] * 3,
        out_shape=[
            jax.ShapeDtypeStruct((width, TOK), f32),
            jax.ShapeDtypeStruct((heads, 8, TOK), f32),
            jax.ShapeDtypeStruct((far_rows, width), bf16),
        ],
        scratch_shapes=[
            pltpu.VMEM(pool.shape, bf16),
            pltpu.VMEM((TOK, width), bf16),
            pltpu.VMEM((TOK, width), bf16),
            pltpu.VMEM((TOK, width), bf16),
            pltpu.VMEM((width, TOK), f32),
            pltpu.VMEM((heads, 8, TOK), f32),
            pltpu.VMEM((far_rows, width), bf16),
            pltpu.VMEM((TOK, width), bf16),
            pltpu.VMEM((BLOCK, width), bf16),
            pltpu.VMEM((BLOCK, width), bf16),
            pltpu.VMEM((BLOCK, width), bf16),
            pltpu.VMEM((BLOCK, BLOCK), f32),
            pltpu.VMEM((2, 2, BLOCK, 2 * BLOCK), f32),
            pltpu.VMEM((2, 2, BLOCK, BLOCK), f32),
            pltpu.VMEM((2, BLOCK, BLOCK), f32),
            pltpu.VMEM((2, 2, BLOCK, 2 * BLOCK), bf16),
            pltpu.VMEM((2, 2, BLOCK, BLOCK), bf16),
            pltpu.VMEM((2, BLOCK, BLOCK), bf16),
            pltpu.SemaphoreType.DMA((6,)),
            pltpu.SemaphoreType.DMA((heads, 2)),
        ],
        compiler_params=pltpu.CompilerParams(vmem_limit_bytes=VMEM_CLAIM),
        cost_estimate=pl.CostEstimate(flops=8_000_000_000, bytes_accessed=4 * MIB, transcendentals=0),
        name="near_levels",
    )(pool, queries, keys, values)


def by_lane_group(arrays, size):
    lane = lax.broadcasted_iota(jnp.int32, arrays[0].shape, 1)
    result = arrays[-1]
    for index in range(len(arrays) - 2, -1, -1):
        result = jnp.where(lane < (index + 1) * size, arrays[index], result)
    return result


def widen_to_second(array):
    r32, r64, r96 = [pltpu.roll(array, shift, 1) for shift in (32, 64, 96)]
    return [by_lane_group([array, r32, r32, r64], 32), by_lane_group([r64, r96, r96, array], 32)]


def widen_to_units(arrays):
    units = []
    for array in arrays:
        turned = pltpu.roll(array, 64, 1)
        units += [by_lane_group([array, turned], 64), by_lane_group([turned, array], 64)]
    return units


def far_kernel(levels, plan, flags_ref, *refs):
    crossing = range(FIRST, levels + 1)
    bundles = 1 + max(bundle for _, bundle, _ in plan)
    kv_refs = refs[:bundles]
    refs = refs[bundles:]
    slices = len(SLICES)
    far_refs, num_refs, stat_refs = refs[:slices], refs[slices : 2 * slices], refs[2 * slices : 3 * slices]
    turn_ref, w_ref, out_ref = refs[3 * slices : 3 * slices + 3]
    kv, queries, num, stat, turn, weights, scores, probs = refs[3 * slices + 3 : 3 * slices + 11]
    mixed, natural, stage, kv_sems, near_sems, out_sems = refs[3 * slices + 11 :]
    pair = 2 * HEAD
    model = w_ref.shape[1]
    step = 512
    offsets, far_rows = far_offsets(levels)

    def kv_copies(index):
        cols = slice(index * pair, (index + 1) * pair)
        made = []
        for number, (level, bundle, spans) in enumerate(plan):
            source_start, target_start, rows = spans
            made.append(
                pltpu.make_async_copy(
                    kv_refs[bundle].at[:, source_start : source_start + rows, cols],
                    kv.at[level - FIRST, :, target_start : target_start + rows, cols],
                    kv_sems.at[index, number],
                )
            )
        return made

    far_copies, near_copies = [], []
    for index, (first, heads) in enumerate(SLICES):
        cols = slice(first * HEAD, (first + heads) * HEAD)
        group = slice(first, first + heads)
        sems = [near_sems.at[place * slices + index] for place in range(3)]
        far_copies.append(pltpu.make_async_copy(far_refs[index], queries.at[:, cols], sems[0]))
        near_copies.append(
            [
                pltpu.make_async_copy(num_refs[index], num.at[cols, :], sems[1]),
                pltpu.make_async_copy(stat_refs[index], stat.at[group], sems[2]),
            ]
        )
    last_copies = [
        pltpu.make_async_copy(turn_ref, turn, near_sems.at[3 * slices]),
        pltpu.make_async_copy(w_ref, weights, near_sems.at[3 * slices + 1]),
    ]
    for copy in far_copies + kv_copies(0) + kv_copies(1) + near_copies[0]:
        copy.start()
    for index in range(2, HEADS // 2):
        for copy in kv_copies(index):
            copy.start()
    for copies in near_copies[1:]:
        for copy in copies:
            copy.start()
    for copy in last_copies:
        copy.start()

    def score(head, level):
        own = lane_block(head)
        span = slice(offsets[level], offsets[level] + UNITS * count_of(level))
        scores[head % 2, :, span] = dot_t(kv[level - FIRST, 0, :, own], queries[span, own])

    def soft(head, level):
        blocks = range(offsets[level] // HEAD, (offsets[level] + UNITS * count_of(level)) // HEAD)
        return [
            soft_columns(
                [lambda span, block=block: scores[head % 2, span, lane_block(block)]], [probs.at[head % 2, :, lane_block(block)]]
            )
            for block in blocks
        ]

    def weigh(head, level, stats):
        own = lane_block(head)
        span = slice(offsets[level], offsets[level] + UNITS * count_of(level))
        live = flags_ref[level - FIRST] == 1
        factor = jnp.where(live, 2.0**level, 0.0)
        weighted = factor * dot_first(kv[level - FIRST, 1, :, own], probs[head % 2, :, span])
        return [
            (weighted[:, lane_block(block)], jnp.where(live, peak, NEG), factor * total)
            for block, (peak, total) in enumerate(stats)
        ]

    def join(state, terms):
        if state is None:
            return terms
        if len(terms) > len(state):
            wide = [widen_to_second(item) for item in state[0]]
            state = [tuple(item[side] for item in wide) for side in range(2)]
        return [merge(old, new) for old, new in zip(state, terms)]

    def mix(head, state):
        own = lane_block(head)
        wide = [widen_to_units([half[place] for half in state]) for place in range(3)]
        for unit in range(UNITS):
            far_num, far_peak, far_total = [item[unit] for item in wide]
            for block in range(2 * unit, 2 * unit + 2):
                peak = stat[head, 0:1, lane_block(block)]
                total = stat[head, 1:2, lane_block(block)]
                top = jnp.maximum(peak, far_peak)
                a = jnp.exp(peak - top)
                b = jnp.exp(far_peak - top)
                inverse = 1.0 / (a * total + b * far_total)
                both = (a * inverse) * num[own, lane_block(block)] + (b * inverse) * far_num
                mixed[own, lane_block(block)] = both.astype(jnp.bfloat16)

    order = list(range(levels, FIRST - 1, -1))
    for copy in far_copies + kv_copies(0):
        copy.wait()
    for level in order:
        score(0, level)
    for copy in near_copies[0]:
        copy.wait()
    pending = None
    for head in range(HEADS):
        if head % 2 == 1 and head + 1 < HEADS:
            for copy in kv_copies((head + 1) // 2):
                copy.wait()
        for index, (first, _) in enumerate(SLICES):
            if index and first == head:
                for copy in near_copies[index]:
                    copy.wait()
        terms = []
        for level in order:
            stats = soft(head, level)
            if head + 1 < HEADS:
                score(head + 1, level)
            if level == order[0] and pending is not None:
                pending()
            terms.append(weigh(head, level, stats))

        def pending(head=head, terms=terms):
            mix(head, functools.reduce(join, terms, None))

    pending()

    for copy in last_copies:
        copy.wait()
    for unit in range(UNITS):
        rows = slice(unit * BLOCK, (unit + 1) * BLOCK)
        natural[rows, :] = dot_t(turn[...], mixed[:, rows]).astype(jnp.bfloat16)
    sends = []
    for index in range(model // step):
        cols = slice(index * step, (index + 1) * step)
        stage[:, cols] = dot(natural[...], weights[:, cols]).astype(jnp.bfloat16)
        sends.append(pltpu.make_async_copy(stage.at[:, cols], out_ref.at[:, cols], out_sems.at[index]))
        sends[-1].start()
    for send in sends:
        send.wait()


def far_call(flags, bundles, plan, near, w_out, levels):
    turn = np.zeros((BLOCK, BLOCK))
    turn[token_of(np.arange(BLOCK)), np.arange(BLOCK)] = 1.0
    nums, stats, fars = [[item[place] for item in near] for place in range(3)]
    model = w_out.shape[1]
    _, far_rows = far_offsets(levels)
    count = levels - FIRST + 1
    bf16, f32 = jnp.bfloat16, jnp.float32
    return pl.pallas_call(
        functools.partial(far_kernel, levels, plan),
        in_specs=[pl.BlockSpec(memory_space=pltpu.SMEM)] + [HBM] * (len(bundles) + 3 * len(SLICES) + 2),
        out_specs=HBM,
        out_shape=jax.ShapeDtypeStruct((TOK, model), bf16),
        scratch_shapes=[
            pltpu.VMEM((count, 2, BLOCK, WIDTH), bf16),
            pltpu.VMEM((far_rows, WIDTH), bf16),
            pltpu.VMEM((WIDTH, TOK), f32),
            pltpu.VMEM((HEADS, 8, TOK), f32),
            pltpu.VMEM((BLOCK, BLOCK), bf16),
            pltpu.VMEM((WIDTH, model), bf16),
            pltpu.VMEM((2, BLOCK, far_rows), f32),
            pltpu.VMEM((2, BLOCK, far_rows), bf16),
            pltpu.VMEM((WIDTH, TOK), bf16),
            pltpu.VMEM((TOK, WIDTH), bf16),
            pltpu.VMEM((TOK, model), bf16),
            pltpu.SemaphoreType.DMA((HEADS // 2, len(plan))),
            pltpu.SemaphoreType.DMA((3 * len(SLICES) + 2,)),
            pltpu.SemaphoreType.DMA((model // 512,)),
        ],
        compiler_params=pltpu.CompilerParams(vmem_limit_bytes=VMEM_CLAIM),
        cost_estimate=pl.CostEstimate(flops=6_500_000_000, bytes_accessed=18 * MIB, transcendentals=3_000_000),
        name="far_levels_projection",
    )(flags, *bundles, *fars, *nums, *stats, as_bf16(turn), w_out)


def moved(array, distance):
    return lax.ppermute(array, "seq", [(i ^ distance, i) for i in range(lax.axis_size("seq"))])


def gathered(array, distances):
    size = lax.axis_size("seq")
    got = lax.ppermute(array, "seq", [(i ^ distances[i % 2], i) for i in range(size)])
    return jnp.concatenate([array, got], axis=1)


def after(arrays, others):
    return lax.optimization_barrier((arrays, others))[0]


def on_device(queries, keys, values, w_out):
    size = lax.axis_size("seq")
    levels = (TOK * size // (2 * BLOCK)).bit_length() - 1
    position = lax.axis_index("seq")
    flags = jnp.stack([(position >> (level - FIRST)) & 1 for level in range(FIRST, levels + 1)]).astype(jnp.int32)
    pooled = pool_call(keys, values, levels)

    places, _ = packed(levels)
    blocks = {level: pooled[level - FIRST] for level in range(FIRST, TOP)}
    for level in range(TOP, levels + 1):
        place, first = places[level]
        blocks[level] = pooled[place][:, first : first + (TOK >> level)]
    high = list(range(TOP, levels + 1))

    for distance in [1 << (level - FIRST) for level in high]:
        members = [level for level in high if 1 << (level - FIRST) >= distance]
        sent = pooled[-1] if distance == GROUP else jnp.concatenate([blocks[level] for level in members], axis=1)
        got = moved(sent, distance)
        start = 0
        for level in members:
            rows = blocks[level].shape[1]
            piece = got[:, start : start + rows]
            start += rows
            if 1 << (level - FIRST) == distance:
                blocks[level] = piece
            else:
                blocks[level] = jnp.concatenate([blocks[level], piece], axis=1)
        if distance == GROUP:
            fourth = moved(blocks[4], 4)
            arrived = blocks[TOP]

    upper = jnp.concatenate([blocks[level] for level in high], axis=1)
    near = [near_call(after(queries, arrived), keys, values, levels, 0)]
    once = gathered(after(upper, near[0]), (2, 4))
    third = moved(after(blocks[3], (near[0], upper)), 2)
    near.append(near_call(after(queries, (near[0], upper)), keys, values, levels, 1))
    joined = gathered(after(once, near[1]), (4, 2))
    fourth = gathered(after(fourth, near[1]), (2, 2))
    second = moved(after(blocks[2], arrived), 1)
    near.append(near_call(after(queries, (near[1], once)), keys, values, levels, 2))
    low = jnp.concatenate([after(third, near[2]), fourth], axis=1)
    low_got = moved(low, 1)
    top = after(joined, near[2])
    top_got = moved(top, 1)
    plan = [(2, 4, (0, 0, BLOCK))]
    for level in (3, 4):
        plan += [(level, bundle, ((level - 3) * 128, bundle * 128, 128)) for bundle in (0, 1)]
    for level in high:
        for piece in range(4):
            start = (piece * len(high) + level - TOP) * 32
            plan += [(level, bundle, (start, (bundle - 2) * 128 + piece * 32, 32)) for bundle in (2, 3)]
    return far_call(flags, [low, low_got, top, top_got, second], plan, near, w_out, levels)


def solution(mesh):
    return jax.shard_map(
        on_device,
        mesh=mesh,
        in_specs=(P("seq", None), P("seq", None), P("seq", None), P()),
        out_specs=P("seq", None),
        check_vma=False,
    )
```

```python
import functools

import jax
import jax.numpy as jnp
import numpy as np
from jax import lax
from jax.experimental import pallas as pl
from jax.experimental.pallas import tpu as pltpu
from jax.sharding import PartitionSpec as P

HEADS = 8
HEAD = 128
BLOCK = 256
TOK = 1024
UNITS = TOK // BLOCK
WIDTH = HEADS * HEAD
NEG = -1e30
FIRST = 2
TOP = 5
GROUP = 8
SCALE = HEAD**-0.5
LOG2E = 1.4426950408889634
MIB = 1 << 20
SLICES = ((0, 3), (3, 3), (6, 2))
VMEM_CLAIM = 60 * MIB
HBM = pl.BlockSpec(memory_space=pltpu.HBM)


def token_of(position):
    return ((position & 31) << 3) | (((position >> 5) & 1) << 2) | (((position >> 6) & 1) << 1) | (position >> 7)


def count_of(level):
    return max(BLOCK >> level, 32)


def pool_rows(level):
    rows = token_of(np.arange(count_of(level))) >> level
    columns = np.arange(BLOCK) >> level
    return (rows[:, None] == columns[None, :]) * 2.0**-level


def natural_pool(level, span):
    rows = np.arange(span >> level)
    return (rows[:, None] == (np.arange(span) >> level)[None, :]) * 2.0**-level


def padded(array, multiple):
    return np.pad(array, ((0, -len(array) % multiple), (0, 0)))


def as_bf16(array):
    return jnp.asarray(array.astype(np.float32)).astype(jnp.bfloat16)


def dot(a, b):
    return jnp.dot(a, b, preferred_element_type=jnp.float32)


def dot_t(a, b):
    return lax.dot_general(a, b, (((1,), (1,)), ((), ())), preferred_element_type=jnp.float32)


def dot_first(a, b):
    return lax.dot_general(a, b, (((0,), (0,)), ((), ())), preferred_element_type=jnp.float32)


def merge(first, second):
    top = jnp.maximum(first[1], second[1])
    a = jnp.exp(first[1] - top)
    b = jnp.exp(second[1] - top)
    return (a * first[0] + b * second[0], top, a * first[2] + b * second[2])


ROWS = 64


def soft_columns(loads, targets):
    spans = [slice(start, start + ROWS) for start in range(0, BLOCK, ROWS)]
    peak = None
    for load in loads:
        for span in spans:
            rows = jnp.max(load(span).reshape(ROWS // 8, 8, HEAD), axis=0)
            peak = rows if peak is None else jnp.maximum(peak, rows)
    peak = jnp.max(peak, axis=0, keepdims=True)
    total = jnp.zeros((8, HEAD), jnp.float32)
    for load, target in zip(loads, targets):
        for span in spans:
            probs = jnp.exp2((load(span) - peak) * (SCALE * LOG2E))
            total = total + jnp.sum(probs.reshape(ROWS // 8, 8, HEAD), axis=0)
            target[span, :] = probs.astype(jnp.bfloat16)
    return peak * SCALE, jnp.sum(total, axis=0, keepdims=True)


def packed(levels):
    places, rows = {level: (level - FIRST, 0) for level in range(FIRST, TOP)}, 0
    for level in range(TOP, levels + 1):
        places[level] = (TOP - FIRST, rows)
        rows += TOK >> level
    return places, [TOK >> level for level in range(FIRST, TOP)] + [rows]


def pool_kernel(levels, small_ref, large_ref, keys_ref, values_ref, *refs):
    places, sizes = packed(levels)
    count = len(sizes)
    targets, (small, large, buffers, *outs, sems, out_sems) = refs[:count], refs[count:]
    step = WIDTH // 4
    fixed = [pltpu.make_async_copy(small_ref, small, sems.at[8]), pltpu.make_async_copy(large_ref, large, sems.at[9])]
    copies = []
    for index, source in enumerate((keys_ref, values_ref)):
        for part in range(4):
            cols = slice(part * step, (part + 1) * step)
            copies.append(pltpu.make_async_copy(source.at[:, cols], buffers.at[index, :, cols], sems.at[index * 4 + part]))
    for copy in fixed + copies:
        copy.start()
    for copy in fixed:
        copy.wait()
    sends = []
    for index in range(2):
        for part in range(4):
            cols = slice(part * step, (part + 1) * step)
            copies[index * 4 + part].wait()
            tiles = [
                dot(small[...], buffers[index, i * 2 * BLOCK : (i + 1) * 2 * BLOCK, cols]) for i in range(UNITS // 2)
            ]
            offset = 0
            for level in range(FIRST, min(levels, 6) + 1):
                rows = 2 * BLOCK >> level
                both = jnp.concatenate([tile[offset : offset + rows] for tile in tiles], axis=0)
                place, first = places[level]
                outs[place][index, first : first + 2 * rows, cols] = both.astype(jnp.bfloat16)
                offset += rows
            if levels > 6:
                rest = dot(large[...], buffers[index, :, cols])
                for level in range(7, levels + 1):
                    start = (level - 7) * 8
                    place, first = places[level]
                    outs[place][index, first : first + (TOK >> level), cols] = rest[start : start + (TOK >> level)].astype(jnp.bfloat16)
            for place, (out, target) in enumerate(zip(outs, targets)):
                span = (index, slice(None), cols)
                sends.append(pltpu.make_async_copy(out.at[span], target.at[span], out_sems.at[index * 4 + part, place]))
                sends[-1].start()
    for send in sends:
        send.wait()


def pool_call(keys, values, levels):
    small = as_bf16(padded(np.concatenate([natural_pool(level, 2 * BLOCK) for level in range(FIRST, min(levels, 6) + 1)]), 16))
    parts = [padded(natural_pool(level, TOK), 8) for level in range(7, levels + 1)] + [np.zeros((8, TOK))]
    large = as_bf16(padded(np.concatenate(parts), 16))
    _, sizes = packed(levels)
    return pl.pallas_call(
        functools.partial(pool_kernel, levels),
        in_specs=[HBM] * 4,
        out_specs=[HBM] * len(sizes),
        out_shape=[jax.ShapeDtypeStruct((2, rows, WIDTH), jnp.bfloat16) for rows in sizes],
        scratch_shapes=[
            pltpu.VMEM(small.shape, jnp.bfloat16),
            pltpu.VMEM(large.shape, jnp.bfloat16),
            pltpu.VMEM((2, TOK, WIDTH), jnp.bfloat16),
        ]
        + [pltpu.VMEM((2, rows, WIDTH), jnp.bfloat16) for rows in sizes]
        + [
            pltpu.SemaphoreType.DMA((10,)),
            pltpu.SemaphoreType.DMA((8, len(sizes))),
        ],
        compiler_params=pltpu.CompilerParams(vmem_limit_bytes=VMEM_CLAIM),
        cost_estimate=pl.CostEstimate(flops=2 * 256 * 512 * 4096, bytes_accessed=6 * MIB, transcendentals=0),
        name="pool_keys_values",
    )(small, large, keys, values)


def far_offsets(levels):
    offsets, total = {}, 0
    for level in range(FIRST, levels + 1):
        offsets[level] = total
        total += UNITS * count_of(level)
    return offsets, total


def lane_block(index):
    return slice(index * HEAD, (index + 1) * HEAD)


def near_kernel(levels, first, heads, pool_ref, q_ref, k_ref, v_ref, num_out, stat_out, far_out, *scratch):
    (pool, q, k, v, num, stat, far, ordered, coarse_q, coarse_k, coarse_v, bias, scores_a, scores_b, scores_c) = scratch[:15]
    probs_a, probs_b, probs_c, sems, head_sems = scratch[15:]
    width = heads * HEAD
    cols = slice(first * HEAD, first * HEAD + width)
    copies = [
        pltpu.make_async_copy(pool_ref, pool, sems.at[0]),
        pltpu.make_async_copy(q_ref.at[:, cols], q, sems.at[1]),
        pltpu.make_async_copy(k_ref.at[:, cols], k, sems.at[2]),
        pltpu.make_async_copy(v_ref.at[:, cols], v, sems.at[3]),
    ]
    for copy in copies:
        copy.start()
    row = lax.broadcasted_iota(jnp.int32, (BLOCK, BLOCK), 0)
    position = lax.broadcasted_iota(jnp.int32, (BLOCK, BLOCK), 1)
    bias[...] = jnp.where(row <= token_of(position), 0.0, NEG)
    copies[0].wait()
    copies[1].wait()

    offsets, _ = far_offsets(levels)
    for unit in range(UNITS):
        pooled = dot(pool[...], q[unit * BLOCK : (unit + 1) * BLOCK, :])
        ordered[unit * BLOCK : (unit + 1) * BLOCK, :] = pooled[:BLOCK].astype(jnp.bfloat16)
        if unit >= 2:
            coarse_q[(unit - 2) * 128 : (unit - 1) * 128, :] = pooled[BLOCK : BLOCK + 128].astype(jnp.bfloat16)
        start = BLOCK + 128
        for level in range(FIRST, levels + 1):
            count = count_of(level)
            place = offsets[level] + unit * count
            far[place : place + count, :] = pooled[start : start + count].astype(jnp.bfloat16)
            start += count
    sends = [pltpu.make_async_copy(far, far_out, sems.at[4])]
    sends[0].start()
    copies[2].wait()
    copies[3].wait()
    for unit in range(2):
        rows = slice(unit * BLOCK, (unit + 1) * BLOCK)
        half = slice(unit * 128, (unit + 1) * 128)
        coarse_k[half, :] = dot(pool[BLOCK : BLOCK + 128, :], k[rows, :]).astype(jnp.bfloat16)
        coarse_v[half, :] = dot(pool[BLOCK : BLOCK + 128, :], v[rows, :]).astype(jnp.bfloat16)

    def num_copy(head, tile):
        rows = lane_block(head)
        lanes = slice(tile * 2 * BLOCK, (tile + 1) * 2 * BLOCK)
        return pltpu.make_async_copy(num.at[rows, lanes], num_out.at[rows, lanes], head_sems.at[head, tile])

    def dot_pieces(head):
        slot, own = head % 2, lane_block(head)

        def coarse():
            scores_c[slot] = dot_t(coarse_k[:, own], coarse_q[:, own])

        def part(tile, piece):
            base = 2 * tile * BLOCK
            if piece < 2:
                rows = slice(base + piece * BLOCK, base + (piece + 1) * BLOCK)
                scores_a[slot, tile, :, piece * BLOCK : (piece + 1) * BLOCK] = dot_t(
                    k[base : base + BLOCK, own], ordered[rows, own]
                )
            else:
                rows = slice(base + BLOCK, base + 2 * BLOCK)
                scores_b[slot, tile] = dot_t(k[rows, own], ordered[rows, own])

        return [coarse] + [functools.partial(part, tile, piece) for tile in (1, 0) for piece in range(3)]

    def soft_a(head, tile, block):
        slot, lanes = head % 2, lane_block(block)
        return soft_columns(
            [lambda span: scores_a[slot, tile, span, lanes] + bias[span, lanes]], [probs_a.at[slot, tile, :, lanes]]
        )

    def soft_b(head, tile, block):
        slot, lanes, late = head % 2, lane_block(block), lane_block(2 + block)
        return soft_columns(
            [
                lambda span: scores_a[slot, tile, span, late],
                lambda span: scores_b[slot, tile, span, lanes] + bias[span, lanes],
            ],
            [probs_a.at[slot, tile, :, late], probs_b.at[slot, tile, :, lanes]],
        )

    def soft_c(head, block):
        slot, lanes = head % 2, lane_block(block)
        return soft_columns([lambda span: scores_c[slot, span, lanes]], [probs_c.at[slot, :, lanes]])

    def weigh(head, tile):
        slot, own, base = head % 2, lane_block(head), 2 * tile * BLOCK
        both = dot_first(v[base : base + BLOCK, own], probs_a[slot, tile])
        more = dot_first(v[base + BLOCK : base + 2 * BLOCK, own], probs_b[slot, tile])
        nums = [both[:, lane_block(0)], both[:, lane_block(1)]]
        return nums + [both[:, lane_block(2 + block)] + more[:, lane_block(block)] for block in range(2)]

    def keep(head, tile, states):
        for index, state in enumerate(states):
            lanes = lane_block(4 * tile + index)
            num[lane_block(head), lanes] = state[0]
            stat[head, 0:1, lanes] = state[1]
            stat[head, 1:2, lanes] = state[2]
        num_copy(head, tile).start()

    def finish_late(head, nums, stats, coarse_num, coarse_stats):
        states = []
        for block in range(4):
            unit = block // 2
            coarse = (2.0 * coarse_num[:, lane_block(unit)], coarse_stats[unit][0], 2.0 * coarse_stats[unit][1])
            states.append(merge((nums[block],) + stats[block], coarse))
        keep(head, 1, states)

    for piece in dot_pieces(0):
        piece()
    pending = None
    for head in range(heads):
        pieces = dot_pieces(head + 1) if head + 1 < heads else []

        def more():
            if pieces:
                pieces.pop(0)()

        coarse_stats = [soft_c(head, 0)]
        more()
        if pending is not None:
            pending()
        coarse_stats.append(soft_c(head, 1))
        more()
        coarse_num = dot_first(coarse_v[:, lane_block(head)], probs_c[head % 2])
        late_stats = []
        for block in range(2):
            late_stats.append(soft_a(head, 1, block))
            more()
        for block in range(2):
            late_stats.append(soft_b(head, 1, block))
            more()
        nums = weigh(head, 1)
        stats = [soft_a(head, 0, 0)]
        more()
        stats.append(soft_a(head, 0, 1))
        finish_late(head, nums, late_stats, coarse_num, coarse_stats)
        for block in range(2):
            stats.append(soft_b(head, 0, block))

        def pending(head=head, stats=stats):
            keep(head, 0, [(item,) + pair for item, pair in zip(weigh(head, 0), stats)])

    pending()
    sends.append(pltpu.make_async_copy(stat, stat_out, sems.at[5]))
    sends[-1].start()
    for send in sends:
        send.wait()
    for head in range(heads):
        for tile in range(2):
            num_copy(head, tile).wait()


def near_call(queries, keys, values, levels, index):
    pool = as_bf16(padded(np.concatenate([pool_rows(level) for level in range(levels + 1)]), 16))
    first, heads = SLICES[index]
    width = heads * HEAD
    _, far_rows = far_offsets(levels)
    bf16, f32 = jnp.bfloat16, jnp.float32
    return pl.pallas_call(
        functools.partial(near_kernel, levels, first, heads),
        in_specs=[HBM] * 4,
        out_specs=[HBM] * 3,
        out_shape=[
            jax.ShapeDtypeStruct((width, TOK), f32),
            jax.ShapeDtypeStruct((heads, 8, TOK), f32),
            jax.ShapeDtypeStruct((far_rows, width), bf16),
        ],
        scratch_shapes=[
            pltpu.VMEM(pool.shape, bf16),
            pltpu.VMEM((TOK, width), bf16),
            pltpu.VMEM((TOK, width), bf16),
            pltpu.VMEM((TOK, width), bf16),
            pltpu.VMEM((width, TOK), f32),
            pltpu.VMEM((heads, 8, TOK), f32),
            pltpu.VMEM((far_rows, width), bf16),
            pltpu.VMEM((TOK, width), bf16),
            pltpu.VMEM((BLOCK, width), bf16),
            pltpu.VMEM((BLOCK, width), bf16),
            pltpu.VMEM((BLOCK, width), bf16),
            pltpu.VMEM((BLOCK, BLOCK), f32),
            pltpu.VMEM((2, 2, BLOCK, 2 * BLOCK), f32),
            pltpu.VMEM((2, 2, BLOCK, BLOCK), f32),
            pltpu.VMEM((2, BLOCK, BLOCK), f32),
            pltpu.VMEM((2, 2, BLOCK, 2 * BLOCK), bf16),
            pltpu.VMEM((2, 2, BLOCK, BLOCK), bf16),
            pltpu.VMEM((2, BLOCK, BLOCK), bf16),
            pltpu.SemaphoreType.DMA((6,)),
            pltpu.SemaphoreType.DMA((heads, 2)),
        ],
        compiler_params=pltpu.CompilerParams(vmem_limit_bytes=VMEM_CLAIM),
        cost_estimate=pl.CostEstimate(flops=8_000_000_000, bytes_accessed=4 * MIB, transcendentals=0),
        name="near_levels",
    )(pool, queries, keys, values)


def by_lane_group(arrays, size):
    lane = lax.broadcasted_iota(jnp.int32, arrays[0].shape, 1)
    result = arrays[-1]
    for index in range(len(arrays) - 2, -1, -1):
        result = jnp.where(lane < (index + 1) * size, arrays[index], result)
    return result


def widen_to_second(array):
    r32, r64, r96 = [pltpu.roll(array, shift, 1) for shift in (32, 64, 96)]
    return [by_lane_group([array, r32, r32, r64], 32), by_lane_group([r64, r96, r96, array], 32)]


def widen_to_units(arrays):
    units = []
    for array in arrays:
        turned = pltpu.roll(array, 64, 1)
        units += [by_lane_group([array, turned], 64), by_lane_group([turned, array], 64)]
    return units


def far_kernel(levels, plan, *refs):
    crossing = range(FIRST, levels + 1)
    bundles = 1 + max(bundle for _, bundle, _ in plan)
    kv_refs = refs[:bundles]
    refs = refs[bundles:]
    slices = len(SLICES)
    far_refs, num_refs, stat_refs = refs[:slices], refs[slices : 2 * slices], refs[2 * slices : 3 * slices]
    turn_ref, w_ref, out_ref = refs[3 * slices : 3 * slices + 3]
    kv, queries, num, stat, turn, weights, scores, probs = refs[3 * slices + 3 : 3 * slices + 11]
    mixed, natural, stage, partial, kv_sems, near_sems, out_sems = refs[3 * slices + 11 :]
    pair = 2 * HEAD
    model = w_ref.shape[1]
    step = 256
    offsets, far_rows = far_offsets(levels)

    def kv_copies(index):
        cols = slice(index * pair, (index + 1) * pair)
        made = []
        for number, (level, bundle, spans) in enumerate(plan):
            source_start, target_start, rows = spans
            made.append(
                pltpu.make_async_copy(
                    kv_refs[bundle].at[:, source_start : source_start + rows, cols],
                    kv.at[level - FIRST, :, target_start : target_start + rows, cols],
                    kv_sems.at[index, number],
                )
            )
        return made

    far_copies, near_copies = [], []
    for index, (first, heads) in enumerate(SLICES):
        cols = slice(first * HEAD, (first + heads) * HEAD)
        group = slice(first, first + heads)
        sems = [near_sems.at[place * slices + index] for place in range(3)]
        far_copies.append(pltpu.make_async_copy(far_refs[index], queries.at[:, cols], sems[0]))
        near_copies.append(
            [
                pltpu.make_async_copy(num_refs[index], num.at[cols, :], sems[1]),
                pltpu.make_async_copy(stat_refs[index], stat.at[group], sems[2]),
            ]
        )
    turn_copy = pltpu.make_async_copy(turn_ref, turn, near_sems.at[3 * slices])
    half = WIDTH // 2
    w_copies = [
        pltpu.make_async_copy(w_ref.at[rows], weights.at[rows], near_sems.at[3 * slices + 1 + index])
        for index, rows in enumerate((slice(0, half), slice(half, WIDTH)))
    ]
    started = far_copies + kv_copies(0) + near_copies[0] + kv_copies(1) + [turn_copy] + near_copies[1]
    started += [w_copies[0]] + kv_copies(2) + kv_copies(3)
    for copies in near_copies[2:]:
        started += copies
    for copy in started + [w_copies[1]]:
        copy.start()

    def turned(part):
        cols = slice(part * half, (part + 1) * half)
        for unit in range(UNITS):
            rows = slice(unit * BLOCK, (unit + 1) * BLOCK)
            natural[rows, cols] = dot_t(turn[...], mixed[cols, rows]).astype(jnp.bfloat16)

    def first_product(index):
        cols = slice(index * step, (index + 1) * step)
        partial[:, cols] = dot(natural[:, :half], weights[:half, cols])

    def score(head, level):
        own = lane_block(head)
        span = slice(offsets[level], offsets[level] + UNITS * count_of(level))
        scores[head % 2, :, span] = dot_t(kv[level - FIRST, 0, :, own], queries[span, own])

    def soft(head, level):
        blocks = range(offsets[level] // HEAD, (offsets[level] + UNITS * count_of(level)) // HEAD)
        return [
            soft_columns(
                [lambda span, block=block: scores[head % 2, span, lane_block(block)]], [probs.at[head % 2, :, lane_block(block)]]
            )
            for block in blocks
        ]

    def weigh(head, level, stats):
        own = lane_block(head)
        span = slice(offsets[level], offsets[level] + UNITS * count_of(level))
        live = ((position >> (level - FIRST)) & 1) == 1
        factor = jnp.where(live, 2.0**level, 0.0)
        weighted = factor * dot_first(kv[level - FIRST, 1, :, own], probs[head % 2, :, span])
        return [
            (weighted[:, lane_block(block)], jnp.where(live, peak, NEG), factor * total)
            for block, (peak, total) in enumerate(stats)
        ]

    def join(state, terms):
        if state is None:
            return terms
        if len(terms) > len(state):
            wide = [widen_to_second(item) for item in state[0]]
            state = [tuple(item[side] for item in wide) for side in range(2)]
        return [merge(old, new) for old, new in zip(state, terms)]

    def mix(head, state):
        own = lane_block(head)
        wide = [widen_to_units([half[place] for half in state]) for place in range(3)]
        for unit in range(UNITS):
            far_num, far_peak, far_total = [item[unit] for item in wide]
            for block in range(2 * unit, 2 * unit + 2):
                peak = stat[head, 0:1, lane_block(block)]
                total = stat[head, 1:2, lane_block(block)]
                top = jnp.maximum(peak, far_peak)
                a = jnp.exp(peak - top)
                b = jnp.exp(far_peak - top)
                inverse = 1.0 / (a * total + b * far_total)
                both = (a * inverse) * num[own, lane_block(block)] + (b * inverse) * far_num
                mixed[own, lane_block(block)] = both.astype(jnp.bfloat16)

    position = lax.axis_index("seq")
    order = list(range(levels, FIRST - 1, -1))
    for copy in far_copies + kv_copies(0):
        copy.wait()
    for level in order:
        score(0, level)
    for copy in near_copies[0]:
        copy.wait()
    pending = None
    products = [functools.partial(first_product, index) for index in range(model // step)]
    for head in range(HEADS):
        if head % 2 == 1 and head + 1 < HEADS:
            for copy in kv_copies((head + 1) // 2):
                copy.wait()
        for index, (first, _) in enumerate(SLICES):
            if index and first == head:
                for copy in near_copies[index]:
                    copy.wait()
        terms = []
        for level in order:
            stats = soft(head, level)
            if head + 1 < HEADS:
                score(head + 1, level)
            if level == order[0] and pending is not None:
                pending()
                if head == HEADS // 2:
                    turn_copy.wait()
                    w_copies[0].wait()
                    turned(0)
            elif head >= HEADS // 2 and products:
                products.pop(0)()
            terms.append(weigh(head, level, stats))

        def pending(head=head, terms=terms):
            mix(head, functools.reduce(join, terms, None))

    pending()

    for product in products:
        product()
    turned(1)
    w_copies[1].wait()
    sends = []
    for index in range(model // step):
        cols = slice(index * step, (index + 1) * step)
        stage[:, cols] = (partial[:, cols] + dot(natural[:, half:], weights[half:, cols])).astype(jnp.bfloat16)
        sends.append(pltpu.make_async_copy(stage.at[:, cols], out_ref.at[:, cols], out_sems.at[index]))
        sends[-1].start()
    for send in sends:
        send.wait()


def far_call(bundles, plan, near, w_out, levels):
    turn = np.zeros((BLOCK, BLOCK))
    turn[token_of(np.arange(BLOCK)), np.arange(BLOCK)] = 1.0
    nums, stats, fars = [[item[place] for item in near] for place in range(3)]
    model = w_out.shape[1]
    _, far_rows = far_offsets(levels)
    count = levels - FIRST + 1
    bf16, f32 = jnp.bfloat16, jnp.float32
    return pl.pallas_call(
        functools.partial(far_kernel, levels, plan),
        in_specs=[HBM] * (len(bundles) + 3 * len(SLICES) + 2),
        out_specs=HBM,
        out_shape=jax.ShapeDtypeStruct((TOK, model), bf16),
        scratch_shapes=[
            pltpu.VMEM((count, 2, BLOCK, WIDTH), bf16),
            pltpu.VMEM((far_rows, WIDTH), bf16),
            pltpu.VMEM((WIDTH, TOK), f32),
            pltpu.VMEM((HEADS, 8, TOK), f32),
            pltpu.VMEM((BLOCK, BLOCK), bf16),
            pltpu.VMEM((WIDTH, model), bf16),
            pltpu.VMEM((2, BLOCK, far_rows), f32),
            pltpu.VMEM((2, BLOCK, far_rows), bf16),
            pltpu.VMEM((WIDTH, TOK), bf16),
            pltpu.VMEM((TOK, WIDTH), bf16),
            pltpu.VMEM((TOK, model), bf16),
            pltpu.VMEM((TOK, model), f32),
            pltpu.SemaphoreType.DMA((HEADS // 2, len(plan))),
            pltpu.SemaphoreType.DMA((3 * len(SLICES) + 3,)),
            pltpu.SemaphoreType.DMA((model // 256,)),
        ],
        compiler_params=pltpu.CompilerParams(vmem_limit_bytes=VMEM_CLAIM),
        cost_estimate=pl.CostEstimate(flops=6_500_000_000, bytes_accessed=18 * MIB, transcendentals=3_000_000),
        name="far_levels_projection",
    )(*bundles, *fars, *nums, *stats, as_bf16(turn), w_out)


def moved(array, distance):
    return lax.ppermute(array, "seq", [(i ^ distance, i) for i in range(lax.axis_size("seq"))])


def gathered(blocks, distance):
    sent = jnp.concatenate(blocks, axis=1) if len(blocks) > 1 else blocks[0]
    got = moved(sent, distance)
    joined, start = [], 0
    for block in blocks:
        rows = block.shape[1]
        joined.append(jnp.concatenate([block, got[:, start : start + rows]], axis=1))
        start += rows
    return joined


def after(arrays, others):
    return lax.optimization_barrier((arrays, others))[0]


def on_device(queries, keys, values, w_out):
    size = lax.axis_size("seq")
    levels = (TOK * size // (2 * BLOCK)).bit_length() - 1
    pooled = pool_call(keys, values, levels)

    places, _ = packed(levels)
    blocks = {level: pooled[level - FIRST] for level in range(FIRST, TOP)}
    for level in range(TOP, levels + 1):
        place, first = places[level]
        blocks[level] = pooled[place][:, first : first + (TOK >> level)]
    high = list(range(TOP, levels + 1))

    for distance in [1 << (level - FIRST) for level in high]:
        members = [level for level in high if 1 << (level - FIRST) >= distance]
        sent = pooled[-1] if distance == GROUP else jnp.concatenate([blocks[level] for level in members], axis=1)
        got = moved(sent, distance)
        start = 0
        for level in members:
            rows = blocks[level].shape[1]
            piece = got[:, start : start + rows]
            start += rows
            if 1 << (level - FIRST) == distance:
                blocks[level] = piece
            else:
                blocks[level] = jnp.concatenate([blocks[level], piece], axis=1)
        if distance == GROUP:
            fourth = moved(blocks[4], 4)
            third = moved(blocks[3], 2)
            second = moved(blocks[2], 1)
            arrived = blocks[TOP]

    upper = [blocks[level] for level in high[1:]]
    five = gathered([arrived], 2)
    near = [near_call(after(queries, arrived), keys, values, levels, 0)]
    upper = gathered(after(upper, near[0]), 4)
    five_y = gathered(after(five, near[0]), 4)
    fourth = gathered([after(fourth, near[0])], 2)[0]
    near.append(near_call(after(queries, (near[0], five)), keys, values, levels, 1))
    upper_x = gathered(after(upper, near[1]), 2)
    low = jnp.concatenate([after(third, near[1]), fourth], axis=1)
    low_got = moved(low, 1)
    near.append(near_call(after(queries, (near[1], upper, five_y)), keys, values, levels, 2))
    top = jnp.concatenate(after(five_y + upper_x, near[2]), axis=1)
    top_got = moved(top, 1)
    plan = [(2, 4, (0, 0, BLOCK))]
    for level in (3, 4):
        plan += [(level, bundle, ((level - 3) * 128, bundle * 128, 128)) for bundle in (0, 1)]
    for level in high:
        plan += [(level, bundle, ((level - TOP) * 128, (bundle - 2) * 128, 128)) for bundle in (2, 3)]
    return far_call([low, low_got, top, top_got, second], plan, near, w_out, levels)


def solution(mesh):
    return jax.shard_map(
        on_device,
        mesh=mesh,
        in_specs=(P("seq", None), P("seq", None), P("seq", None), P()),
        out_specs=P("seq", None),
        check_vma=False,
    )
```

```python
import functools

import jax
import jax.numpy as jnp
import numpy as np
from jax import lax
from jax.experimental import pallas as pl
from jax.experimental.pallas import tpu as pltpu
from jax.sharding import PartitionSpec as P

HEADS = 8
HEAD = 128
BLOCK = 256
TOK = 1024
UNITS = TOK // BLOCK
WIDTH = HEADS * HEAD
NEG = -1e30
FIRST = 2
TOP = 5
GROUP = 8
SCALE = HEAD**-0.5
LOG2E = 1.4426950408889634
MIB = 1 << 20
SLICES = ((0, 3), (3, 3), (6, 2))
VMEM_CLAIM = 60 * MIB
HBM = pl.BlockSpec(memory_space=pltpu.HBM)


def token_of(position):
    return ((position & 31) << 3) | (((position >> 5) & 1) << 2) | (((position >> 6) & 1) << 1) | (position >> 7)


def count_of(level):
    return max(BLOCK >> level, 32)


def pool_rows(level):
    rows = token_of(np.arange(count_of(level))) >> level
    columns = np.arange(BLOCK) >> level
    return (rows[:, None] == columns[None, :]) * 2.0**-level


def natural_pool(level, span):
    rows = np.arange(span >> level)
    return (rows[:, None] == (np.arange(span) >> level)[None, :]) * 2.0**-level


def padded(array, multiple):
    return np.pad(array, ((0, -len(array) % multiple), (0, 0)))


def as_bf16(array):
    return jnp.asarray(array.astype(np.float32)).astype(jnp.bfloat16)


def dot(a, b):
    return jnp.dot(a, b, preferred_element_type=jnp.float32)


def dot_t(a, b):
    return lax.dot_general(a, b, (((1,), (1,)), ((), ())), preferred_element_type=jnp.float32)


def dot_first(a, b):
    return lax.dot_general(a, b, (((0,), (0,)), ((), ())), preferred_element_type=jnp.float32)


def merge(first, second):
    top = jnp.maximum(first[1], second[1])
    a = jnp.exp(first[1] - top)
    b = jnp.exp(second[1] - top)
    return (a * first[0] + b * second[0], top, a * first[2] + b * second[2])


ROWS = 64


def soft_columns(loads, targets):
    spans = [slice(start, start + ROWS) for start in range(0, BLOCK, ROWS)]
    peak = None
    for load in loads:
        for span in spans:
            rows = jnp.max(load(span).reshape(ROWS // 8, 8, HEAD), axis=0)
            peak = rows if peak is None else jnp.maximum(peak, rows)
    peak = jnp.max(peak, axis=0, keepdims=True)
    total = jnp.zeros((8, HEAD), jnp.float32)
    for load, target in zip(loads, targets):
        for span in spans:
            probs = jnp.exp2((load(span) - peak) * (SCALE * LOG2E))
            total = total + jnp.sum(probs.reshape(ROWS // 8, 8, HEAD), axis=0)
            target[span, :] = probs.astype(jnp.bfloat16)
    return peak * SCALE, jnp.sum(total, axis=0, keepdims=True)


def packed(levels):
    places, rows = {2: (0, 0), 3: (1, 0), 4: (3, 0)}, 0
    for level in range(TOP, levels + 1):
        places[level] = (4, rows)
        rows += TOK >> level
    return places, [TOK >> 2, TOK >> 4, TOK >> 4, TOK >> 4, rows]


def pool_kernel(levels, small_ref, large_ref, keys_ref, values_ref, *refs):
    places, sizes = packed(levels)
    count = len(sizes)
    targets, (small, large, buffers, *outs, sems, out_sems) = refs[:count], refs[count:]
    step = WIDTH // 4
    fixed = [pltpu.make_async_copy(small_ref, small, sems.at[8]), pltpu.make_async_copy(large_ref, large, sems.at[9])]
    copies = []
    for index, source in enumerate((keys_ref, values_ref)):
        for part in range(4):
            cols = slice(part * step, (part + 1) * step)
            copies.append(pltpu.make_async_copy(source.at[:, cols], buffers.at[index, :, cols], sems.at[index * 4 + part]))
    for copy in fixed + copies:
        copy.start()
    for copy in fixed:
        copy.wait()
    sends = []
    for index in range(2):
        for part in range(4):
            cols = slice(part * step, (part + 1) * step)
            copies[index * 4 + part].wait()
            tiles = [
                dot(small[...], buffers[index, i * 2 * BLOCK : (i + 1) * 2 * BLOCK, cols]) for i in range(UNITS // 2)
            ]
            offset = 0
            for level in range(FIRST, min(levels, 6) + 1):
                rows = 2 * BLOCK >> level
                if level == 3:
                    for place, tile in enumerate(tiles):
                        outs[1 + place][index, :, cols] = tile[offset : offset + rows].astype(jnp.bfloat16)
                    offset += rows
                    continue
                both = jnp.concatenate([tile[offset : offset + rows] for tile in tiles], axis=0)
                place, first = places[level]
                outs[place][index, first : first + 2 * rows, cols] = both.astype(jnp.bfloat16)
                offset += rows
            if levels > 6:
                rest = dot(large[...], buffers[index, :, cols])
                for level in range(7, levels + 1):
                    start = (level - 7) * 8
                    place, first = places[level]
                    outs[place][index, first : first + (TOK >> level), cols] = rest[start : start + (TOK >> level)].astype(jnp.bfloat16)
            for place, (out, target) in enumerate(zip(outs, targets)):
                span = (index, slice(None), cols)
                sends.append(pltpu.make_async_copy(out.at[span], target.at[span], out_sems.at[index * 4 + part, place]))
                sends[-1].start()
    for send in sends:
        send.wait()


def pool_call(keys, values, levels):
    small = as_bf16(padded(np.concatenate([natural_pool(level, 2 * BLOCK) for level in range(FIRST, min(levels, 6) + 1)]), 16))
    parts = [padded(natural_pool(level, TOK), 8) for level in range(7, levels + 1)] + [np.zeros((8, TOK))]
    large = as_bf16(padded(np.concatenate(parts), 16))
    _, sizes = packed(levels)
    return pl.pallas_call(
        functools.partial(pool_kernel, levels),
        in_specs=[HBM] * 4,
        out_specs=[HBM] * len(sizes),
        out_shape=[jax.ShapeDtypeStruct((2, rows, WIDTH), jnp.bfloat16) for rows in sizes],
        scratch_shapes=[
            pltpu.VMEM(small.shape, jnp.bfloat16),
            pltpu.VMEM(large.shape, jnp.bfloat16),
            pltpu.VMEM((2, TOK, WIDTH), jnp.bfloat16),
        ]
        + [pltpu.VMEM((2, rows, WIDTH), jnp.bfloat16) for rows in sizes]
        + [
            pltpu.SemaphoreType.DMA((10,)),
            pltpu.SemaphoreType.DMA((8, len(sizes))),
        ],
        compiler_params=pltpu.CompilerParams(vmem_limit_bytes=VMEM_CLAIM),
        cost_estimate=pl.CostEstimate(flops=2 * 256 * 512 * 4096, bytes_accessed=6 * MIB, transcendentals=0),
        name="pool_keys_values",
    )(small, large, keys, values)


def far_offsets(levels):
    offsets, total = {}, 0
    for level in range(FIRST, levels + 1):
        offsets[level] = total
        total += UNITS * count_of(level)
    return offsets, total


def lane_block(index):
    return slice(index * HEAD, (index + 1) * HEAD)


def near_kernel(levels, first, heads, pool_ref, q_ref, k_ref, v_ref, num_out, stat_out, far_out, *scratch):
    (pool, q, k, v, num, stat, far, ordered, coarse_q, coarse_k, coarse_v, bias, scores_a, scores_b, scores_c) = scratch[:15]
    probs_a, probs_b, probs_c, sems, head_sems = scratch[15:]
    width = heads * HEAD
    cols = slice(first * HEAD, first * HEAD + width)
    copies = [
        pltpu.make_async_copy(pool_ref, pool, sems.at[0]),
        pltpu.make_async_copy(q_ref.at[:, cols], q, sems.at[1]),
        pltpu.make_async_copy(k_ref.at[:, cols], k, sems.at[2]),
        pltpu.make_async_copy(v_ref.at[:, cols], v, sems.at[3]),
    ]
    for copy in copies:
        copy.start()
    row = lax.broadcasted_iota(jnp.int32, (BLOCK, BLOCK), 0)
    position = lax.broadcasted_iota(jnp.int32, (BLOCK, BLOCK), 1)
    bias[...] = jnp.where(row <= token_of(position), 0.0, NEG)
    copies[0].wait()
    copies[1].wait()

    offsets, _ = far_offsets(levels)
    for unit in range(UNITS):
        pooled = dot(pool[...], q[unit * BLOCK : (unit + 1) * BLOCK, :])
        ordered[unit * BLOCK : (unit + 1) * BLOCK, :] = pooled[:BLOCK].astype(jnp.bfloat16)
        if unit >= 2:
            coarse_q[(unit - 2) * 128 : (unit - 1) * 128, :] = pooled[BLOCK : BLOCK + 128].astype(jnp.bfloat16)
        start = BLOCK + 128
        for level in range(FIRST, levels + 1):
            count = count_of(level)
            place = offsets[level] + unit * count
            far[place : place + count, :] = pooled[start : start + count].astype(jnp.bfloat16)
            start += count
    sends = [pltpu.make_async_copy(far, far_out, sems.at[4])]
    sends[0].start()
    copies[2].wait()
    copies[3].wait()
    for unit in range(2):
        rows = slice(unit * BLOCK, (unit + 1) * BLOCK)
        half = slice(unit * 128, (unit + 1) * 128)
        coarse_k[half, :] = dot(pool[BLOCK : BLOCK + 128, :], k[rows, :]).astype(jnp.bfloat16)
        coarse_v[half, :] = dot(pool[BLOCK : BLOCK + 128, :], v[rows, :]).astype(jnp.bfloat16)

    def num_copy(head, tile):
        rows = lane_block(head)
        lanes = slice(tile * 2 * BLOCK, (tile + 1) * 2 * BLOCK)
        return pltpu.make_async_copy(num.at[rows, lanes], num_out.at[rows, lanes], head_sems.at[head, tile])

    def dot_pieces(head):
        slot, own = head % 2, lane_block(head)

        def coarse():
            scores_c[slot] = dot_t(coarse_k[:, own], coarse_q[:, own])

        def part(tile, piece):
            base = 2 * tile * BLOCK
            if piece < 2:
                rows = slice(base + piece * BLOCK, base + (piece + 1) * BLOCK)
                scores_a[slot, tile, :, piece * BLOCK : (piece + 1) * BLOCK] = dot_t(
                    k[base : base + BLOCK, own], ordered[rows, own]
                )
            else:
                rows = slice(base + BLOCK, base + 2 * BLOCK)
                scores_b[slot, tile] = dot_t(k[rows, own], ordered[rows, own])

        return [coarse] + [functools.partial(part, tile, piece) for tile in (1, 0) for piece in range(3)]

    def soft_a(head, tile, block):
        slot, lanes = head % 2, lane_block(block)
        return soft_columns(
            [lambda span: scores_a[slot, tile, span, lanes] + bias[span, lanes]], [probs_a.at[slot, tile, :, lanes]]
        )

    def soft_b(head, tile, block):
        slot, lanes, late = head % 2, lane_block(block), lane_block(2 + block)
        return soft_columns(
            [
                lambda span: scores_a[slot, tile, span, late],
                lambda span: scores_b[slot, tile, span, lanes] + bias[span, lanes],
            ],
            [probs_a.at[slot, tile, :, late], probs_b.at[slot, tile, :, lanes]],
        )

    def soft_c(head, block):
        slot, lanes = head % 2, lane_block(block)
        return soft_columns([lambda span: scores_c[slot, span, lanes]], [probs_c.at[slot, :, lanes]])

    def weigh(head, tile):
        slot, own, base = head % 2, lane_block(head), 2 * tile * BLOCK
        both = dot_first(v[base : base + BLOCK, own], probs_a[slot, tile])
        more = dot_first(v[base + BLOCK : base + 2 * BLOCK, own], probs_b[slot, tile])
        nums = [both[:, lane_block(0)], both[:, lane_block(1)]]
        return nums + [both[:, lane_block(2 + block)] + more[:, lane_block(block)] for block in range(2)]

    def keep(head, tile, states):
        for index, state in enumerate(states):
            lanes = lane_block(4 * tile + index)
            num[lane_block(head), lanes] = state[0]
            stat[head, 0:1, lanes] = state[1]
            stat[head, 1:2, lanes] = state[2]
        num_copy(head, tile).start()

    def finish_late(head, nums, stats, coarse_num, coarse_stats):
        states = []
        for block in range(4):
            unit = block // 2
            coarse = (2.0 * coarse_num[:, lane_block(unit)], coarse_stats[unit][0], 2.0 * coarse_stats[unit][1])
            states.append(merge((nums[block],) + stats[block], coarse))
        keep(head, 1, states)

    for piece in dot_pieces(0):
        piece()
    pending = None
    for head in range(heads):
        pieces = dot_pieces(head + 1) if head + 1 < heads else []

        def more():
            if pieces:
                pieces.pop(0)()

        coarse_stats = [soft_c(head, 0)]
        more()
        if pending is not None:
            pending()
        coarse_stats.append(soft_c(head, 1))
        more()
        coarse_num = dot_first(coarse_v[:, lane_block(head)], probs_c[head % 2])
        late_stats = []
        for block in range(2):
            late_stats.append(soft_a(head, 1, block))
            more()
        for block in range(2):
            late_stats.append(soft_b(head, 1, block))
            more()
        nums = weigh(head, 1)
        stats = [soft_a(head, 0, 0)]
        more()
        stats.append(soft_a(head, 0, 1))
        finish_late(head, nums, late_stats, coarse_num, coarse_stats)
        for block in range(2):
            stats.append(soft_b(head, 0, block))

        def pending(head=head, stats=stats):
            keep(head, 0, [(item,) + pair for item, pair in zip(weigh(head, 0), stats)])

    pending()
    sends.append(pltpu.make_async_copy(stat, stat_out, sems.at[5]))
    sends[-1].start()
    for send in sends:
        send.wait()
    for head in range(heads):
        for tile in range(2):
            num_copy(head, tile).wait()


def near_call(queries, keys, values, levels, index):
    pool = as_bf16(padded(np.concatenate([pool_rows(level) for level in range(levels + 1)]), 16))
    first, heads = SLICES[index]
    width = heads * HEAD
    _, far_rows = far_offsets(levels)
    bf16, f32 = jnp.bfloat16, jnp.float32
    return pl.pallas_call(
        functools.partial(near_kernel, levels, first, heads),
        in_specs=[HBM] * 4,
        out_specs=[HBM] * 3,
        out_shape=[
            jax.ShapeDtypeStruct((width, TOK), f32),
            jax.ShapeDtypeStruct((heads, 8, TOK), f32),
            jax.ShapeDtypeStruct((far_rows, width), bf16),
        ],
        scratch_shapes=[
            pltpu.VMEM(pool.shape, bf16),
            pltpu.VMEM((TOK, width), bf16),
            pltpu.VMEM((TOK, width), bf16),
            pltpu.VMEM((TOK, width), bf16),
            pltpu.VMEM((width, TOK), f32),
            pltpu.VMEM((heads, 8, TOK), f32),
            pltpu.VMEM((far_rows, width), bf16),
            pltpu.VMEM((TOK, width), bf16),
            pltpu.VMEM((BLOCK, width), bf16),
            pltpu.VMEM((BLOCK, width), bf16),
            pltpu.VMEM((BLOCK, width), bf16),
            pltpu.VMEM((BLOCK, BLOCK), f32),
            pltpu.VMEM((2, 2, BLOCK, 2 * BLOCK), f32),
            pltpu.VMEM((2, 2, BLOCK, BLOCK), f32),
            pltpu.VMEM((2, BLOCK, BLOCK), f32),
            pltpu.VMEM((2, 2, BLOCK, 2 * BLOCK), bf16),
            pltpu.VMEM((2, 2, BLOCK, BLOCK), bf16),
            pltpu.VMEM((2, BLOCK, BLOCK), bf16),
            pltpu.SemaphoreType.DMA((6,)),
            pltpu.SemaphoreType.DMA((heads, 2)),
        ],
        compiler_params=pltpu.CompilerParams(vmem_limit_bytes=VMEM_CLAIM),
        cost_estimate=pl.CostEstimate(flops=8_000_000_000, bytes_accessed=4 * MIB, transcendentals=0),
        name="near_levels",
    )(pool, queries, keys, values)


def by_lane_group(arrays, size):
    lane = lax.broadcasted_iota(jnp.int32, arrays[0].shape, 1)
    result = arrays[-1]
    for index in range(len(arrays) - 2, -1, -1):
        result = jnp.where(lane < (index + 1) * size, arrays[index], result)
    return result


def widen_to_second(array):
    r32, r64, r96 = [pltpu.roll(array, shift, 1) for shift in (32, 64, 96)]
    return [by_lane_group([array, r32, r32, r64], 32), by_lane_group([r64, r96, r96, array], 32)]


def widen_to_units(arrays):
    units = []
    for array in arrays:
        turned = pltpu.roll(array, 64, 1)
        units += [by_lane_group([array, turned], 64), by_lane_group([turned, array], 64)]
    return units


def far_kernel(levels, plan, *refs):
    crossing = range(FIRST, levels + 1)
    bundles = 1 + max(bundle for _, bundle, _ in plan)
    kv_refs = refs[:bundles]
    refs = refs[bundles:]
    slices = len(SLICES)
    far_refs, num_refs, stat_refs = refs[:slices], refs[slices : 2 * slices], refs[2 * slices : 3 * slices]
    turn_ref, w_ref, out_ref = refs[3 * slices : 3 * slices + 3]
    kv, queries, num, stat, turn, weights, scores, probs = refs[3 * slices + 3 : 3 * slices + 11]
    mixed, natural, stage, partial, kv_sems, near_sems, out_sems = refs[3 * slices + 11 :]
    pair = 2 * HEAD
    model = w_ref.shape[1]
    step = 256
    offsets, far_rows = far_offsets(levels)

    def kv_copies(index):
        cols = slice(index * pair, (index + 1) * pair)
        made = []
        for number, (level, bundle, spans) in enumerate(plan):
            source_start, target_start, rows = spans
            made.append(
                pltpu.make_async_copy(
                    kv_refs[bundle].at[:, source_start : source_start + rows, cols],
                    kv.at[level - FIRST, :, target_start : target_start + rows, cols],
                    kv_sems.at[index, number],
                )
            )
        return made

    far_copies, near_copies = [], []
    for index, (first, heads) in enumerate(SLICES):
        cols = slice(first * HEAD, (first + heads) * HEAD)
        group = slice(first, first + heads)
        sems = [near_sems.at[place * slices + index] for place in range(3)]
        far_copies.append(pltpu.make_async_copy(far_refs[index], queries.at[:, cols], sems[0]))
        near_copies.append(
            [
                pltpu.make_async_copy(num_refs[index], num.at[cols, :], sems[1]),
                pltpu.make_async_copy(stat_refs[index], stat.at[group], sems[2]),
            ]
        )
    turn_copy = pltpu.make_async_copy(turn_ref, turn, near_sems.at[3 * slices])
    half = WIDTH // 2
    w_copies = [
        pltpu.make_async_copy(w_ref.at[rows], weights.at[rows], near_sems.at[3 * slices + 1 + index])
        for index, rows in enumerate((slice(0, half), slice(half, WIDTH)))
    ]
    stages = [
        far_copies[:1] + kv_copies(0) + near_copies[0],
        far_copies[1:2] + kv_copies(1) + [turn_copy],
        far_copies[2:] + kv_copies(2) + near_copies[1] + w_copies[:1],
        kv_copies(3) + near_copies[2] + w_copies[1:],
    ]

    def start_stage(number):
        for copy in stages[number]:
            copy.start()

    start_stage(0)
    start_stage(1)

    def turned(part):
        cols = slice(part * half, (part + 1) * half)
        for unit in range(UNITS):
            rows = slice(unit * BLOCK, (unit + 1) * BLOCK)
            natural[rows, cols] = dot_t(turn[...], mixed[cols, rows]).astype(jnp.bfloat16)

    def first_product(index):
        cols = slice(index * step, (index + 1) * step)
        partial[:, cols] = dot(natural[:, :half], weights[:half, cols])

    def score(head, level):
        own = lane_block(head)
        span = slice(offsets[level], offsets[level] + UNITS * count_of(level))
        scores[head % 2, :, span] = dot_t(kv[level - FIRST, 0, :, own], queries[span, own])

    def soft(head, level):
        blocks = range(offsets[level] // HEAD, (offsets[level] + UNITS * count_of(level)) // HEAD)
        return [
            soft_columns(
                [lambda span, block=block: scores[head % 2, span, lane_block(block)]], [probs.at[head % 2, :, lane_block(block)]]
            )
            for block in blocks
        ]

    def weigh(head, level, stats):
        own = lane_block(head)
        span = slice(offsets[level], offsets[level] + UNITS * count_of(level))
        live = ((position >> (level - FIRST)) & 1) == 1
        factor = jnp.where(live, 2.0**level, 0.0)
        weighted = factor * dot_first(kv[level - FIRST, 1, :, own], probs[head % 2, :, span])
        return [
            (weighted[:, lane_block(block)], jnp.where(live, peak, NEG), factor * total)
            for block, (peak, total) in enumerate(stats)
        ]

    def join(state, terms):
        if state is None:
            return terms
        if len(terms) > len(state):
            wide = [widen_to_second(item) for item in state[0]]
            state = [tuple(item[side] for item in wide) for side in range(2)]
        return [merge(old, new) for old, new in zip(state, terms)]

    def mix(head, state):
        own = lane_block(head)
        wide = [widen_to_units([half[place] for half in state]) for place in range(3)]
        for unit in range(UNITS):
            far_num, far_peak, far_total = [item[unit] for item in wide]
            for block in range(2 * unit, 2 * unit + 2):
                peak = stat[head, 0:1, lane_block(block)]
                total = stat[head, 1:2, lane_block(block)]
                top = jnp.maximum(peak, far_peak)
                a = jnp.exp(peak - top)
                b = jnp.exp(far_peak - top)
                inverse = 1.0 / (a * total + b * far_total)
                both = (a * inverse) * num[own, lane_block(block)] + (b * inverse) * far_num
                mixed[own, lane_block(block)] = both.astype(jnp.bfloat16)

    position = lax.axis_index("seq")
    order = list(range(levels, FIRST - 1, -1))
    for copy in far_copies[:1] + kv_copies(0):
        copy.wait()
    start_stage(2)
    for level in order:
        score(0, level)
    for copy in near_copies[0]:
        copy.wait()
    pending = None
    products = [functools.partial(first_product, index) for index in range(model // step)]
    for head in range(HEADS):
        if head % 2 == 1 and head + 1 < HEADS:
            for copy in kv_copies((head + 1) // 2):
                copy.wait()
        for index, (first, _) in enumerate(SLICES):
            if index and first == head + 1:
                far_copies[index].wait()
        if head == 1:
            start_stage(3)
        for index, (first, _) in enumerate(SLICES):
            if index and first == head:
                for copy in near_copies[index]:
                    copy.wait()
        terms = []
        for level in order:
            stats = soft(head, level)
            if head + 1 < HEADS:
                score(head + 1, level)
            if level == order[0] and pending is not None:
                pending()
                if head == HEADS // 2:
                    turn_copy.wait()
                    w_copies[0].wait()
                    turned(0)
            elif head >= HEADS // 2 and products:
                products.pop(0)()
            terms.append(weigh(head, level, stats))

        def pending(head=head, terms=terms):
            mix(head, functools.reduce(join, terms, None))

    pending()

    for product in products:
        product()
    turned(1)
    w_copies[1].wait()
    sends = []
    for index in range(model // step):
        cols = slice(index * step, (index + 1) * step)
        stage[:, cols] = (partial[:, cols] + dot(natural[:, half:], weights[half:, cols])).astype(jnp.bfloat16)
        sends.append(pltpu.make_async_copy(stage.at[:, cols], out_ref.at[:, cols], out_sems.at[index]))
        sends[-1].start()
    for send in sends:
        send.wait()


def far_call(bundles, plan, near, w_out, levels):
    turn = np.zeros((BLOCK, BLOCK))
    turn[token_of(np.arange(BLOCK)), np.arange(BLOCK)] = 1.0
    nums, stats, fars = [[item[place] for item in near] for place in range(3)]
    model = w_out.shape[1]
    _, far_rows = far_offsets(levels)
    count = levels - FIRST + 1
    bf16, f32 = jnp.bfloat16, jnp.float32
    return pl.pallas_call(
        functools.partial(far_kernel, levels, plan),
        in_specs=[HBM] * (len(bundles) + 3 * len(SLICES) + 2),
        out_specs=HBM,
        out_shape=jax.ShapeDtypeStruct((TOK, model), bf16),
        scratch_shapes=[
            pltpu.VMEM((count, 2, BLOCK, WIDTH), bf16),
            pltpu.VMEM((far_rows, WIDTH), bf16),
            pltpu.VMEM((WIDTH, TOK), f32),
            pltpu.VMEM((HEADS, 8, TOK), f32),
            pltpu.VMEM((BLOCK, BLOCK), bf16),
            pltpu.VMEM((WIDTH, model), bf16),
            pltpu.VMEM((2, BLOCK, far_rows), f32),
            pltpu.VMEM((2, BLOCK, far_rows), bf16),
            pltpu.VMEM((WIDTH, TOK), bf16),
            pltpu.VMEM((TOK, WIDTH), bf16),
            pltpu.VMEM((TOK, model), bf16),
            pltpu.VMEM((TOK, model), f32),
            pltpu.SemaphoreType.DMA((HEADS // 2, len(plan))),
            pltpu.SemaphoreType.DMA((3 * len(SLICES) + 3,)),
            pltpu.SemaphoreType.DMA((model // 256,)),
        ],
        compiler_params=pltpu.CompilerParams(vmem_limit_bytes=VMEM_CLAIM),
        cost_estimate=pl.CostEstimate(flops=6_500_000_000, bytes_accessed=18 * MIB, transcendentals=3_000_000),
        name="far_levels_projection",
    )(*bundles, *fars, *nums, *stats, as_bf16(turn), w_out)


def moved(array, distance):
    return lax.ppermute(array, "seq", [(i ^ distance, i) for i in range(lax.axis_size("seq"))])


def gathered(blocks, distance):
    sent = jnp.concatenate(blocks, axis=1) if len(blocks) > 1 else blocks[0]
    got = moved(sent, distance)
    joined, start = [], 0
    for block in blocks:
        rows = block.shape[1]
        joined.append(jnp.concatenate([block, got[:, start : start + rows]], axis=1))
        start += rows
    return joined


def after(arrays, others):
    return lax.optimization_barrier((arrays, others))[0]


def on_device(queries, keys, values, w_out):
    size = lax.axis_size("seq")
    levels = (TOK * size // (2 * BLOCK)).bit_length() - 1
    pooled = pool_call(keys, values, levels)

    places, _ = packed(levels)
    blocks = {2: pooled[0], 4: pooled[3]}
    for level in range(TOP, levels + 1):
        place, first = places[level]
        blocks[level] = pooled[place][:, first : first + (TOK >> level)]
    high = list(range(TOP, levels + 1))

    for distance in [1 << (level - FIRST) for level in high]:
        members = [level for level in high if 1 << (level - FIRST) >= distance]
        sent = pooled[-1] if distance == GROUP else jnp.concatenate([blocks[level] for level in members], axis=1)
        got = moved(sent, distance)
        start = 0
        for level in members:
            rows = blocks[level].shape[1]
            piece = got[:, start : start + rows]
            start += rows
            if 1 << (level - FIRST) == distance:
                blocks[level] = piece
            else:
                blocks[level] = jnp.concatenate([blocks[level], piece], axis=1)
        if distance == GROUP:
            fourth = moved(blocks[4], 4)
            third = [moved(pooled[1], 2)]
            arrived = blocks[TOP]
            third.append(moved(after(pooled[2], arrived), 2))
            second = moved(after(blocks[2], arrived), 1)

    upper = [blocks[level] for level in high[1:]]
    five = gathered([arrived], 2)
    near = [near_call(after(queries, arrived), keys, values, levels, 0)]
    upper = gathered(after(upper, near[0]), 4)
    five_y = gathered(after(five, near[0]), 4)
    fourth = gathered([after(fourth, near[0])], 2)[0]
    near.append(near_call(after(queries, (near[0], five)), keys, values, levels, 1))
    upper_x = gathered(after(upper, near[1]), 2)
    low = jnp.concatenate([*after(third, near[1]), fourth], axis=1)
    low_got = moved(low, 1)
    near.append(near_call(after(queries, (near[1], upper, five_y)), keys, values, levels, 2))
    top = jnp.concatenate(after(five_y + upper_x, near[2]), axis=1)
    top_got = moved(top, 1)
    plan = [(2, 4, (0, 0, BLOCK))]
    for level in (3, 4):
        plan += [(level, bundle, ((level - 3) * 128, bundle * 128, 128)) for bundle in (0, 1)]
    for level in high:
        plan += [(level, bundle, ((level - TOP) * 128, (bundle - 2) * 128, 128)) for bundle in (2, 3)]
    return far_call([low, low_got, top, top_got, second], plan, near, w_out, levels)


def solution(mesh):
    return jax.shard_map(
        on_device,
        mesh=mesh,
        in_specs=(P("seq", None), P("seq", None), P("seq", None), P()),
        out_specs=P("seq", None),
        check_vma=False,
    )
```

```python
import functools

import jax
import jax.numpy as jnp
import numpy as np
from jax import lax
from jax.experimental import pallas as pl
from jax.experimental.pallas import tpu as pltpu
from jax.sharding import PartitionSpec as P

HEADS = 8
HEAD = 128
BLOCK = 256
TOK = 1024
UNITS = TOK // BLOCK
WIDTH = HEADS * HEAD
NEG = -1e30
FIRST = 2
TOP = 5
GROUP = 8
SCALE = HEAD**-0.5
LOG2E = 1.4426950408889634
MIB = 1 << 20
SLICES = ((0, 3), (3, 3), (6, 2))
VMEM_CLAIM = 60 * MIB
HBM = pl.BlockSpec(memory_space=pltpu.HBM)


def token_of(position):
    return ((position & 31) << 3) | (((position >> 5) & 1) << 2) | (((position >> 6) & 1) << 1) | (position >> 7)


def count_of(level):
    return max(BLOCK >> level, 32)


def pool_rows(level):
    rows = token_of(np.arange(count_of(level))) >> level
    columns = np.arange(BLOCK) >> level
    return (rows[:, None] == columns[None, :]) * 2.0**-level


def natural_pool(level, span):
    rows = np.arange(span >> level)
    return (rows[:, None] == (np.arange(span) >> level)[None, :]) * 2.0**-level


def padded(array, multiple):
    return np.pad(array, ((0, -len(array) % multiple), (0, 0)))


def as_bf16(array):
    return jnp.asarray(array.astype(np.float32)).astype(jnp.bfloat16)


def dot(a, b):
    return jnp.dot(a, b, preferred_element_type=jnp.float32)


def dot_t(a, b):
    return lax.dot_general(a, b, (((1,), (1,)), ((), ())), preferred_element_type=jnp.float32)


def dot_first(a, b):
    return lax.dot_general(a, b, (((0,), (0,)), ((), ())), preferred_element_type=jnp.float32)


def merge(first, second):
    top = jnp.maximum(first[1], second[1])
    a = jnp.exp(first[1] - top)
    b = jnp.exp(second[1] - top)
    return (a * first[0] + b * second[0], top, a * first[2] + b * second[2])


ROWS = 64


def soft_columns(loads, targets):
    spans = [slice(start, start + ROWS) for start in range(0, BLOCK, ROWS)]
    peak = None
    for load in loads:
        for span in spans:
            rows = jnp.max(load(span).reshape(ROWS // 8, 8, HEAD), axis=0)
            peak = rows if peak is None else jnp.maximum(peak, rows)
    peak = jnp.max(peak, axis=0, keepdims=True)
    total = jnp.zeros((8, HEAD), jnp.float32)
    for load, target in zip(loads, targets):
        for span in spans:
            probs = jnp.exp2((load(span) - peak) * (SCALE * LOG2E))
            total = total + jnp.sum(probs.reshape(ROWS // 8, 8, HEAD), axis=0)
            target[span, :] = probs.astype(jnp.bfloat16)
    return peak * SCALE, jnp.sum(total, axis=0, keepdims=True)


def packed(levels):
    places, rows = {2: (0, 0), 3: (1, 0), 4: (3, 0)}, 0
    for level in range(TOP, levels + 1):
        places[level] = (4, rows)
        rows += TOK >> level
    return places, [TOK >> 2, TOK >> 4, TOK >> 4, TOK >> 4, rows]


def pool_kernel(levels, small_ref, large_ref, keys_ref, values_ref, *refs):
    places, sizes = packed(levels)
    count = len(sizes)
    targets, (small, large, buffers, *outs, sems, out_sems) = refs[:count], refs[count:]
    step = WIDTH // 4
    fixed = [pltpu.make_async_copy(small_ref, small, sems.at[8]), pltpu.make_async_copy(large_ref, large, sems.at[9])]
    copies = []
    for index, source in enumerate((keys_ref, values_ref)):
        for part in range(4):
            cols = slice(part * step, (part + 1) * step)
            copies.append(pltpu.make_async_copy(source.at[:, cols], buffers.at[index, :, cols], sems.at[index * 4 + part]))
    for copy in fixed + copies:
        copy.start()
    for copy in fixed:
        copy.wait()
    sends = []
    for index in range(2):
        for part in range(4):
            cols = slice(part * step, (part + 1) * step)
            copies[index * 4 + part].wait()
            tiles = [
                dot(small[...], buffers[index, i * 2 * BLOCK : (i + 1) * 2 * BLOCK, cols]) for i in range(UNITS // 2)
            ]
            offset = 0
            for level in range(FIRST, min(levels, 6) + 1):
                rows = 2 * BLOCK >> level
                if level == 3:
                    for place, tile in enumerate(tiles):
                        outs[1 + place][index, :, cols] = tile[offset : offset + rows].astype(jnp.bfloat16)
                    offset += rows
                    continue
                both = jnp.concatenate([tile[offset : offset + rows] for tile in tiles], axis=0)
                place, first = places[level]
                outs[place][index, first : first + 2 * rows, cols] = both.astype(jnp.bfloat16)
                offset += rows
            if levels > 6:
                rest = dot(large[...], buffers[index, :, cols])
                for level in range(7, levels + 1):
                    start = (level - 7) * 8
                    place, first = places[level]
                    outs[place][index, first : first + (TOK >> level), cols] = rest[start : start + (TOK >> level)].astype(jnp.bfloat16)
            for place, (out, target) in enumerate(zip(outs, targets)):
                span = (index, slice(None), cols)
                sends.append(pltpu.make_async_copy(out.at[span], target.at[span], out_sems.at[index * 4 + part, place]))
                sends[-1].start()
    for send in sends:
        send.wait()


def pool_call(keys, values, levels):
    small = as_bf16(padded(np.concatenate([natural_pool(level, 2 * BLOCK) for level in range(FIRST, min(levels, 6) + 1)]), 16))
    parts = [padded(natural_pool(level, TOK), 8) for level in range(7, levels + 1)] + [np.zeros((8, TOK))]
    large = as_bf16(padded(np.concatenate(parts), 16))
    _, sizes = packed(levels)
    return pl.pallas_call(
        functools.partial(pool_kernel, levels),
        in_specs=[HBM] * 4,
        out_specs=[HBM] * len(sizes),
        out_shape=[jax.ShapeDtypeStruct((2, rows, WIDTH), jnp.bfloat16) for rows in sizes],
        scratch_shapes=[
            pltpu.VMEM(small.shape, jnp.bfloat16),
            pltpu.VMEM(large.shape, jnp.bfloat16),
            pltpu.VMEM((2, TOK, WIDTH), jnp.bfloat16),
        ]
        + [pltpu.VMEM((2, rows, WIDTH), jnp.bfloat16) for rows in sizes]
        + [
            pltpu.SemaphoreType.DMA((10,)),
            pltpu.SemaphoreType.DMA((8, len(sizes))),
        ],
        compiler_params=pltpu.CompilerParams(vmem_limit_bytes=VMEM_CLAIM),
        cost_estimate=pl.CostEstimate(flops=2 * 256 * 512 * 4096, bytes_accessed=6 * MIB, transcendentals=0),
        name="pool_keys_values",
    )(small, large, keys, values)


def far_offsets(levels):
    offsets, total = {}, 0
    for level in range(FIRST, levels + 1):
        offsets[level] = total
        total += UNITS * count_of(level)
    return offsets, total


def lane_block(index):
    return slice(index * HEAD, (index + 1) * HEAD)


def near_kernel(levels, first, heads, pool_ref, q_ref, k_ref, v_ref, num_out, stat_out, far_out, *scratch):
    (pool, q, k, v, num, stat, far, ordered, coarse_q, coarse_k, coarse_v, bias, scores_a, scores_b, scores_c) = scratch[:15]
    probs_a, probs_b, probs_c, sems, head_sems = scratch[15:]
    width = heads * HEAD
    cols = slice(first * HEAD, first * HEAD + width)
    copies = [
        pltpu.make_async_copy(pool_ref, pool, sems.at[0]),
        pltpu.make_async_copy(q_ref.at[:, cols], q, sems.at[1]),
        pltpu.make_async_copy(k_ref.at[:, cols], k, sems.at[2]),
        pltpu.make_async_copy(v_ref.at[:, cols], v, sems.at[3]),
    ]
    for copy in copies:
        copy.start()
    row = lax.broadcasted_iota(jnp.int32, (BLOCK, BLOCK), 0)
    position = lax.broadcasted_iota(jnp.int32, (BLOCK, BLOCK), 1)
    bias[...] = jnp.where(row <= token_of(position), 0.0, NEG)
    copies[0].wait()
    copies[1].wait()

    offsets, _ = far_offsets(levels)
    for unit in range(UNITS):
        pooled = dot(pool[...], q[unit * BLOCK : (unit + 1) * BLOCK, :])
        ordered[unit * BLOCK : (unit + 1) * BLOCK, :] = pooled[:BLOCK].astype(jnp.bfloat16)
        if unit >= 2:
            coarse_q[(unit - 2) * 128 : (unit - 1) * 128, :] = pooled[BLOCK : BLOCK + 128].astype(jnp.bfloat16)
        start = BLOCK + 128
        for level in range(FIRST, levels + 1):
            count = count_of(level)
            place = offsets[level] + unit * count
            far[place : place + count, :] = pooled[start : start + count].astype(jnp.bfloat16)
            start += count
    sends = [pltpu.make_async_copy(far, far_out, sems.at[4])]
    sends[0].start()
    copies[2].wait()
    copies[3].wait()
    for unit in range(2):
        rows = slice(unit * BLOCK, (unit + 1) * BLOCK)
        half = slice(unit * 128, (unit + 1) * 128)
        coarse_k[half, :] = dot(pool[BLOCK : BLOCK + 128, :], k[rows, :]).astype(jnp.bfloat16)
        coarse_v[half, :] = dot(pool[BLOCK : BLOCK + 128, :], v[rows, :]).astype(jnp.bfloat16)

    def num_copy(head, tile):
        rows = lane_block(head)
        lanes = slice(tile * 2 * BLOCK, (tile + 1) * 2 * BLOCK)
        return pltpu.make_async_copy(num.at[rows, lanes], num_out.at[rows, lanes], head_sems.at[head, tile])

    def dot_pieces(head):
        slot, own = head % 2, lane_block(head)

        def coarse():
            scores_c[slot] = dot_t(coarse_k[:, own], coarse_q[:, own])

        def part(tile, piece):
            base = 2 * tile * BLOCK
            if piece < 2:
                rows = slice(base + piece * BLOCK, base + (piece + 1) * BLOCK)
                scores_a[slot, tile, :, piece * BLOCK : (piece + 1) * BLOCK] = dot_t(
                    k[base : base + BLOCK, own], ordered[rows, own]
                )
            else:
                rows = slice(base + BLOCK, base + 2 * BLOCK)
                scores_b[slot, tile] = dot_t(k[rows, own], ordered[rows, own])

        return [coarse] + [functools.partial(part, tile, piece) for tile in (1, 0) for piece in range(3)]

    def soft_a(head, tile, block):
        slot, lanes = head % 2, lane_block(block)
        return soft_columns(
            [lambda span: scores_a[slot, tile, span, lanes] + bias[span, lanes]], [probs_a.at[slot, tile, :, lanes]]
        )

    def soft_b(head, tile, block):
        slot, lanes, late = head % 2, lane_block(block), lane_block(2 + block)
        return soft_columns(
            [
                lambda span: scores_a[slot, tile, span, late],
                lambda span: scores_b[slot, tile, span, lanes] + bias[span, lanes],
            ],
            [probs_a.at[slot, tile, :, late], probs_b.at[slot, tile, :, lanes]],
        )

    def soft_c(head, block):
        slot, lanes = head % 2, lane_block(block)
        return soft_columns([lambda span: scores_c[slot, span, lanes]], [probs_c.at[slot, :, lanes]])

    def weigh(head, tile):
        slot, own, base = head % 2, lane_block(head), 2 * tile * BLOCK
        both = dot_first(v[base : base + BLOCK, own], probs_a[slot, tile])
        more = dot_first(v[base + BLOCK : base + 2 * BLOCK, own], probs_b[slot, tile])
        nums = [both[:, lane_block(0)], both[:, lane_block(1)]]
        return nums + [both[:, lane_block(2 + block)] + more[:, lane_block(block)] for block in range(2)]

    def keep(head, tile, states):
        for index, state in enumerate(states):
            lanes = lane_block(4 * tile + index)
            num[lane_block(head), lanes] = state[0]
            stat[head, 0:1, lanes] = state[1]
            stat[head, 1:2, lanes] = state[2]
        num_copy(head, tile).start()

    def finish_late(head, nums, stats, coarse_num, coarse_stats):
        states = []
        for block in range(4):
            unit = block // 2
            coarse = (2.0 * coarse_num[:, lane_block(unit)], coarse_stats[unit][0], 2.0 * coarse_stats[unit][1])
            states.append(merge((nums[block],) + stats[block], coarse))
        keep(head, 1, states)

    for piece in dot_pieces(0):
        piece()
    pending = None
    for head in range(heads):
        pieces = dot_pieces(head + 1) if head + 1 < heads else []

        def more():
            if pieces:
                pieces.pop(0)()

        coarse_stats = [soft_c(head, 0)]
        more()
        if pending is not None:
            pending()
        coarse_stats.append(soft_c(head, 1))
        more()
        coarse_num = dot_first(coarse_v[:, lane_block(head)], probs_c[head % 2])
        late_stats = []
        for block in range(2):
            late_stats.append(soft_a(head, 1, block))
            more()
        for block in range(2):
            late_stats.append(soft_b(head, 1, block))
            more()
        nums = weigh(head, 1)
        stats = [soft_a(head, 0, 0)]
        more()
        stats.append(soft_a(head, 0, 1))
        finish_late(head, nums, late_stats, coarse_num, coarse_stats)
        for block in range(2):
            stats.append(soft_b(head, 0, block))

        def pending(head=head, stats=stats):
            keep(head, 0, [(item,) + pair for item, pair in zip(weigh(head, 0), stats)])

    pending()
    sends.append(pltpu.make_async_copy(stat, stat_out, sems.at[5]))
    sends[-1].start()
    for send in sends:
        send.wait()
    for head in range(heads):
        for tile in range(2):
            num_copy(head, tile).wait()


def near_call(queries, keys, values, levels, index):
    pool = as_bf16(padded(np.concatenate([pool_rows(level) for level in range(levels + 1)]), 16))
    first, heads = SLICES[index]
    width = heads * HEAD
    _, far_rows = far_offsets(levels)
    bf16, f32 = jnp.bfloat16, jnp.float32
    return pl.pallas_call(
        functools.partial(near_kernel, levels, first, heads),
        in_specs=[HBM] * 4,
        out_specs=[HBM] * 3,
        out_shape=[
            jax.ShapeDtypeStruct((width, TOK), f32),
            jax.ShapeDtypeStruct((heads, 8, TOK), f32),
            jax.ShapeDtypeStruct((far_rows, width), bf16),
        ],
        scratch_shapes=[
            pltpu.VMEM(pool.shape, bf16),
            pltpu.VMEM((TOK, width), bf16),
            pltpu.VMEM((TOK, width), bf16),
            pltpu.VMEM((TOK, width), bf16),
            pltpu.VMEM((width, TOK), f32),
            pltpu.VMEM((heads, 8, TOK), f32),
            pltpu.VMEM((far_rows, width), bf16),
            pltpu.VMEM((TOK, width), bf16),
            pltpu.VMEM((BLOCK, width), bf16),
            pltpu.VMEM((BLOCK, width), bf16),
            pltpu.VMEM((BLOCK, width), bf16),
            pltpu.VMEM((BLOCK, BLOCK), f32),
            pltpu.VMEM((2, 2, BLOCK, 2 * BLOCK), f32),
            pltpu.VMEM((2, 2, BLOCK, BLOCK), f32),
            pltpu.VMEM((2, BLOCK, BLOCK), f32),
            pltpu.VMEM((2, 2, BLOCK, 2 * BLOCK), bf16),
            pltpu.VMEM((2, 2, BLOCK, BLOCK), bf16),
            pltpu.VMEM((2, BLOCK, BLOCK), bf16),
            pltpu.SemaphoreType.DMA((6,)),
            pltpu.SemaphoreType.DMA((heads, 2)),
        ],
        compiler_params=pltpu.CompilerParams(vmem_limit_bytes=VMEM_CLAIM),
        cost_estimate=pl.CostEstimate(flops=8_000_000_000, bytes_accessed=4 * MIB, transcendentals=0),
        name="near_levels",
    )(pool, queries, keys, values)


def by_lane_group(arrays, size):
    lane = lax.broadcasted_iota(jnp.int32, arrays[0].shape, 1)
    result = arrays[-1]
    for index in range(len(arrays) - 2, -1, -1):
        result = jnp.where(lane < (index + 1) * size, arrays[index], result)
    return result


def widen_to_second(array):
    r32, r64, r96 = [pltpu.roll(array, shift, 1) for shift in (32, 64, 96)]
    return [by_lane_group([array, r32, r32, r64], 32), by_lane_group([r64, r96, r96, array], 32)]


def widen_to_units(arrays):
    units = []
    for array in arrays:
        turned = pltpu.roll(array, 64, 1)
        units += [by_lane_group([array, turned], 64), by_lane_group([turned, array], 64)]
    return units


def far_kernel(levels, plan, *refs):
    crossing = range(FIRST, levels + 1)
    bundles = 1 + max(bundle for _, bundle, _ in plan)
    kv_refs = refs[:bundles]
    refs = refs[bundles:]
    slices = len(SLICES)
    far_refs, num_refs, stat_refs = refs[:slices], refs[slices : 2 * slices], refs[2 * slices : 3 * slices]
    turn_ref, w_ref, out_ref = refs[3 * slices : 3 * slices + 3]
    kv, queries, num, stat, turn, weights, scores, probs = refs[3 * slices + 3 : 3 * slices + 11]
    mixed, natural, stage, partial, kv_sems, near_sems, out_sems = refs[3 * slices + 11 :]
    pair = 2 * HEAD
    model = w_ref.shape[1]
    step = 256
    offsets, far_rows = far_offsets(levels)

    def kv_copies(index):
        cols = slice(index * pair, (index + 1) * pair)
        made = []
        for number, (level, bundle, spans) in enumerate(plan):
            source_start, target_start, rows = spans
            made.append(
                pltpu.make_async_copy(
                    kv_refs[bundle].at[:, source_start : source_start + rows, cols],
                    kv.at[level - FIRST, :, target_start : target_start + rows, cols],
                    kv_sems.at[index, number],
                )
            )
        return made

    far_copies, near_copies = [], []
    for index, (first, heads) in enumerate(SLICES):
        cols = slice(first * HEAD, (first + heads) * HEAD)
        group = slice(first, first + heads)
        sems = [near_sems.at[place * slices + index] for place in range(3)]
        far_copies.append(pltpu.make_async_copy(far_refs[index], queries.at[:, cols], sems[0]))
        near_copies.append(
            [
                pltpu.make_async_copy(num_refs[index], num.at[cols, :], sems[1]),
                pltpu.make_async_copy(stat_refs[index], stat.at[group], sems[2]),
            ]
        )
    turn_copy = pltpu.make_async_copy(turn_ref, turn, near_sems.at[3 * slices])
    half = WIDTH // 2
    w_copies = [
        pltpu.make_async_copy(w_ref.at[rows], weights.at[rows], near_sems.at[3 * slices + 1 + index])
        for index, rows in enumerate((slice(0, half), slice(half, WIDTH)))
    ]
    stages = [
        far_copies[:1] + kv_copies(0) + near_copies[0],
        far_copies[1:2] + kv_copies(1) + [turn_copy],
        far_copies[2:] + kv_copies(2) + near_copies[1] + w_copies[:1],
        kv_copies(3) + near_copies[2] + w_copies[1:],
    ]

    def start_stage(number):
        for copy in stages[number]:
            copy.start()

    start_stage(0)
    start_stage(1)

    def turned(part):
        cols = slice(part * half, (part + 1) * half)
        for unit in range(UNITS):
            rows = slice(unit * BLOCK, (unit + 1) * BLOCK)
            natural[rows, cols] = dot_t(turn[...], mixed[cols, rows]).astype(jnp.bfloat16)

    def first_product(index):
        cols = slice(index * step, (index + 1) * step)
        partial[:, cols] = dot(natural[:, :half], weights[:half, cols])

    def score(head, level):
        own = lane_block(head)
        span = slice(offsets[level], offsets[level] + UNITS * count_of(level))
        scores[head % 2, :, span] = dot_t(kv[level - FIRST, 0, :, own], queries[span, own])

    def soft(head, level):
        blocks = range(offsets[level] // HEAD, (offsets[level] + UNITS * count_of(level)) // HEAD)
        return [
            soft_columns(
                [lambda span, block=block: scores[head % 2, span, lane_block(block)]], [probs.at[head % 2, :, lane_block(block)]]
            )
            for block in blocks
        ]

    def weigh(head, level, stats):
        own = lane_block(head)
        span = slice(offsets[level], offsets[level] + UNITS * count_of(level))
        live = ((position >> (level - FIRST)) & 1) == 1
        factor = jnp.where(live, 2.0**level, 0.0)
        weighted = factor * dot_first(kv[level - FIRST, 1, :, own], probs[head % 2, :, span])
        return [
            (weighted[:, lane_block(block)], jnp.where(live, peak, NEG), factor * total)
            for block, (peak, total) in enumerate(stats)
        ]

    def join(state, terms):
        if state is None:
            return terms
        if len(terms) > len(state):
            wide = [widen_to_second(item) for item in state[0]]
            state = [tuple(item[side] for item in wide) for side in range(2)]
        return [merge(old, new) for old, new in zip(state, terms)]

    def mix(head, state):
        own = lane_block(head)
        wide = [widen_to_units([half[place] for half in state]) for place in range(3)]
        for unit in range(UNITS):
            far_num, far_peak, far_total = [item[unit] for item in wide]
            for block in range(2 * unit, 2 * unit + 2):
                peak = stat[head, 0:1, lane_block(block)]
                total = stat[head, 1:2, lane_block(block)]
                top = jnp.maximum(peak, far_peak)
                a = jnp.exp(peak - top)
                b = jnp.exp(far_peak - top)
                inverse = 1.0 / (a * total + b * far_total)
                both = (a * inverse) * num[own, lane_block(block)] + (b * inverse) * far_num
                mixed[own, lane_block(block)] = both.astype(jnp.bfloat16)

    position = lax.axis_index("seq")
    order = list(range(levels, FIRST - 1, -1))
    for copy in far_copies[:1] + kv_copies(0):
        copy.wait()
    start_stage(2)
    for level in order:
        score(0, level)
    for copy in near_copies[0]:
        copy.wait()
    pending = None
    products = [functools.partial(first_product, index) for index in range(model // step)]
    for head in range(HEADS):
        if head % 2 == 1 and head + 1 < HEADS:
            for copy in kv_copies((head + 1) // 2):
                copy.wait()
        for index, (first, _) in enumerate(SLICES):
            if index and first == head + 1:
                far_copies[index].wait()
        if head == 1:
            start_stage(3)
        for index, (first, _) in enumerate(SLICES):
            if index and first == head:
                for copy in near_copies[index]:
                    copy.wait()
        terms = []
        for level in order:
            stats = soft(head, level)
            if head + 1 < HEADS:
                score(head + 1, level)
            if level == order[0] and pending is not None:
                pending()
                if head == HEADS // 2:
                    turn_copy.wait()
                    w_copies[0].wait()
                    turned(0)
            elif head >= HEADS // 2 and products:
                products.pop(0)()
            terms.append(weigh(head, level, stats))

        def pending(head=head, terms=terms):
            mix(head, functools.reduce(join, terms, None))

    pending()

    for product in products:
        product()
    turned(1)
    w_copies[1].wait()
    sends = []
    for index in range(model // step):
        cols = slice(index * step, (index + 1) * step)
        stage[:, cols] = (partial[:, cols] + dot(natural[:, half:], weights[half:, cols])).astype(jnp.bfloat16)
        sends.append(pltpu.make_async_copy(stage.at[:, cols], out_ref.at[:, cols], out_sems.at[index]))
        sends[-1].start()
    for send in sends:
        send.wait()


def far_call(bundles, plan, near, w_out, levels):
    turn = np.zeros((BLOCK, BLOCK))
    turn[token_of(np.arange(BLOCK)), np.arange(BLOCK)] = 1.0
    nums, stats, fars = [[item[place] for item in near] for place in range(3)]
    model = w_out.shape[1]
    _, far_rows = far_offsets(levels)
    count = levels - FIRST + 1
    bf16, f32 = jnp.bfloat16, jnp.float32
    return pl.pallas_call(
        functools.partial(far_kernel, levels, plan),
        in_specs=[HBM] * (len(bundles) + 3 * len(SLICES) + 2),
        out_specs=HBM,
        out_shape=jax.ShapeDtypeStruct((TOK, model), bf16),
        scratch_shapes=[
            pltpu.VMEM((count, 2, BLOCK, WIDTH), bf16),
            pltpu.VMEM((far_rows, WIDTH), bf16),
            pltpu.VMEM((WIDTH, TOK), f32),
            pltpu.VMEM((HEADS, 8, TOK), f32),
            pltpu.VMEM((BLOCK, BLOCK), bf16),
            pltpu.VMEM((WIDTH, model), bf16),
            pltpu.VMEM((2, BLOCK, far_rows), f32),
            pltpu.VMEM((2, BLOCK, far_rows), bf16),
            pltpu.VMEM((WIDTH, TOK), bf16),
            pltpu.VMEM((TOK, WIDTH), bf16),
            pltpu.VMEM((TOK, model), bf16),
            pltpu.VMEM((TOK, model), f32),
            pltpu.SemaphoreType.DMA((HEADS // 2, len(plan))),
            pltpu.SemaphoreType.DMA((3 * len(SLICES) + 3,)),
            pltpu.SemaphoreType.DMA((model // 256,)),
        ],
        compiler_params=pltpu.CompilerParams(vmem_limit_bytes=VMEM_CLAIM),
        cost_estimate=pl.CostEstimate(flops=6_500_000_000, bytes_accessed=18 * MIB, transcendentals=3_000_000),
        name="far_levels_projection",
    )(*bundles, *fars, *nums, *stats, as_bf16(turn), w_out)


def moved(array, distance):
    return lax.ppermute(array, "seq", [(i ^ distance, i) for i in range(lax.axis_size("seq"))])


def gathered(blocks, distance):
    sent = jnp.concatenate(blocks, axis=1) if len(blocks) > 1 else blocks[0]
    got = moved(sent, distance)
    joined, start = [], 0
    for block in blocks:
        rows = block.shape[1]
        joined.append(jnp.concatenate([block, got[:, start : start + rows]], axis=1))
        start += rows
    return joined


def after(arrays, others):
    return lax.optimization_barrier((arrays, others))[0]


def on_device(queries, keys, values, w_out):
    size = lax.axis_size("seq")
    levels = (TOK * size // (2 * BLOCK)).bit_length() - 1
    pooled = pool_call(keys, values, levels)

    places, _ = packed(levels)
    blocks = {2: pooled[0], 4: pooled[3]}
    for level in range(TOP, levels + 1):
        place, first = places[level]
        blocks[level] = pooled[place][:, first : first + (TOK >> level)]
    high = list(range(TOP, levels + 1))

    for distance in [1 << (level - FIRST) for level in high]:
        members = [level for level in high if 1 << (level - FIRST) >= distance]
        sent = pooled[-1] if distance == GROUP else jnp.concatenate([blocks[level] for level in members], axis=1)
        got = moved(sent, distance)
        start = 0
        for level in members:
            rows = blocks[level].shape[1]
            piece = got[:, start : start + rows]
            start += rows
            if 1 << (level - FIRST) == distance:
                blocks[level] = piece
            else:
                blocks[level] = jnp.concatenate([blocks[level], piece], axis=1)
        if distance == GROUP:
            fourth = moved(blocks[4], 4)
            third = [moved(pooled[1], 2)]
            arrived = blocks[TOP]
            third.append(moved(after(pooled[2], arrived), 2))
            second = moved(after(blocks[2], arrived), 1)

    upper = [blocks[level] for level in high[1:]]
    five = gathered([arrived], 2)
    near = [near_call(after(queries, arrived), keys, values, levels, 0)]
    five_y, *upper = gathered(after(five + upper, near[0]), 4)
    fourth = gathered([after(fourth, near[0])], 2)[0]
    near.append(near_call(after(queries, (near[0], five)), keys, values, levels, 1))
    upper_x = gathered(after(upper, near[1]), 2)
    low = jnp.concatenate([*after(third, near[1]), fourth], axis=1)
    low_got = moved(low, 1)
    near.append(near_call(after(queries, (near[1], upper)), keys, values, levels, 2))
    top = jnp.concatenate(after([five_y] + upper_x, near[2]), axis=1)
    top_got = moved(top, 1)
    plan = [(2, 4, (0, 0, BLOCK))]
    for level in (3, 4):
        plan += [(level, bundle, ((level - 3) * 128, bundle * 128, 128)) for bundle in (0, 1)]
    for level in high:
        plan += [(level, bundle, ((level - TOP) * 128, (bundle - 2) * 128, 128)) for bundle in (2, 3)]
    return far_call([low, low_got, top, top_got, second], plan, near, w_out, levels)


def solution(mesh):
    return jax.shard_map(
        on_device,
        mesh=mesh,
        in_specs=(P("seq", None), P("seq", None), P("seq", None), P()),
        out_specs=P("seq", None),
        check_vma=False,
    )
```

```python
import functools

import jax
import jax.numpy as jnp
import numpy as np
from jax import lax
from jax.experimental import pallas as pl
from jax.experimental.pallas import tpu as pltpu
from jax.sharding import PartitionSpec as P

HEADS = 8
HEAD = 128
BLOCK = 256
TOK = 1024
UNITS = TOK // BLOCK
WIDTH = HEADS * HEAD
NEG = -1e30
FIRST = 2
TOP = 5
GROUP = 8
SCALE = HEAD**-0.5
LOG2E = 1.4426950408889634
MIB = 1 << 20
SLICES = ((0, 3), (3, 3), (6, 2))
VMEM_CLAIM = 60 * MIB
HBM = pl.BlockSpec(memory_space=pltpu.HBM)


def token_of(position):
    return ((position & 31) << 3) | (((position >> 5) & 1) << 2) | (((position >> 6) & 1) << 1) | (position >> 7)


def count_of(level):
    return max(BLOCK >> level, 32)


def pool_rows(level):
    rows = token_of(np.arange(count_of(level))) >> level
    columns = np.arange(BLOCK) >> level
    return (rows[:, None] == columns[None, :]) * 2.0**-level


def natural_pool(level, span):
    rows = np.arange(span >> level)
    return (rows[:, None] == (np.arange(span) >> level)[None, :]) * 2.0**-level


def padded(array, multiple):
    return np.pad(array, ((0, -len(array) % multiple), (0, 0)))


def as_bf16(array):
    return jnp.asarray(array.astype(np.float32)).astype(jnp.bfloat16)


def dot(a, b):
    return jnp.dot(a, b, preferred_element_type=jnp.float32)


def dot_t(a, b):
    return lax.dot_general(a, b, (((1,), (1,)), ((), ())), preferred_element_type=jnp.float32)


def dot_first(a, b):
    return lax.dot_general(a, b, (((0,), (0,)), ((), ())), preferred_element_type=jnp.float32)


def merge(first, second):
    top = jnp.maximum(first[1], second[1])
    a = jnp.exp(first[1] - top)
    b = jnp.exp(second[1] - top)
    return (a * first[0] + b * second[0], top, a * first[2] + b * second[2])


ROWS = 64


def soft_columns(loads, targets):
    spans = [slice(start, start + ROWS) for start in range(0, BLOCK, ROWS)]
    peak = None
    for load in loads:
        for span in spans:
            rows = jnp.max(load(span).reshape(ROWS // 8, 8, HEAD), axis=0)
            peak = rows if peak is None else jnp.maximum(peak, rows)
    peak = jnp.max(peak, axis=0, keepdims=True)
    total = jnp.zeros((8, HEAD), jnp.float32)
    for load, target in zip(loads, targets):
        for span in spans:
            probs = jnp.exp2((load(span) - peak) * (SCALE * LOG2E))
            total = total + jnp.sum(probs.reshape(ROWS // 8, 8, HEAD), axis=0)
            target[span, :] = probs.astype(jnp.bfloat16)
    return peak * SCALE, jnp.sum(total, axis=0, keepdims=True)


def packed(levels):
    places, rows = {2: (0, 0), 3: (1, 0), 4: (3, 0)}, 0
    for level in range(TOP, levels + 1):
        places[level] = (4, rows)
        rows += TOK >> level
    return places, [TOK >> 2, TOK >> 4, TOK >> 4, TOK >> 4, rows]


def pool_kernel(levels, small_ref, large_ref, keys_ref, values_ref, *refs):
    places, sizes = packed(levels)
    count = len(sizes)
    targets, (small, large, buffers, *outs, sems, out_sems) = refs[:count], refs[count:]
    step = WIDTH // 4
    fixed = [pltpu.make_async_copy(small_ref, small, sems.at[8]), pltpu.make_async_copy(large_ref, large, sems.at[9])]
    copies = []
    for index, source in enumerate((keys_ref, values_ref)):
        for part in range(4):
            cols = slice(part * step, (part + 1) * step)
            copies.append(pltpu.make_async_copy(source.at[:, cols], buffers.at[index, :, cols], sems.at[index * 4 + part]))
    for copy in fixed + copies:
        copy.start()
    for copy in fixed:
        copy.wait()
    sends = []
    for index in range(2):
        for part in range(4):
            cols = slice(part * step, (part + 1) * step)
            copies[index * 4 + part].wait()
            tiles = [
                dot(small[...], buffers[index, i * 2 * BLOCK : (i + 1) * 2 * BLOCK, cols]) for i in range(UNITS // 2)
            ]
            offset = 0
            for level in range(FIRST, min(levels, 6) + 1):
                rows = 2 * BLOCK >> level
                if level == 3:
                    for place, tile in enumerate(tiles):
                        outs[1 + place][index, :, cols] = tile[offset : offset + rows].astype(jnp.bfloat16)
                    offset += rows
                    continue
                both = jnp.concatenate([tile[offset : offset + rows] for tile in tiles], axis=0)
                place, first = places[level]
                outs[place][index, first : first + 2 * rows, cols] = both.astype(jnp.bfloat16)
                offset += rows
            if levels > 6:
                rest = dot(large[...], buffers[index, :, cols])
                for level in range(7, levels + 1):
                    start = (level - 7) * 8
                    place, first = places[level]
                    outs[place][index, first : first + (TOK >> level), cols] = rest[start : start + (TOK >> level)].astype(jnp.bfloat16)
            for place, (out, target) in enumerate(zip(outs, targets)):
                span = (index, slice(None), cols)
                sends.append(pltpu.make_async_copy(out.at[span], target.at[span], out_sems.at[index * 4 + part, place]))
                sends[-1].start()
    for send in sends:
        send.wait()


def pool_call(keys, values, levels):
    small = as_bf16(padded(np.concatenate([natural_pool(level, 2 * BLOCK) for level in range(FIRST, min(levels, 6) + 1)]), 16))
    parts = [padded(natural_pool(level, TOK), 8) for level in range(7, levels + 1)] + [np.zeros((8, TOK))]
    large = as_bf16(padded(np.concatenate(parts), 16))
    _, sizes = packed(levels)
    return pl.pallas_call(
        functools.partial(pool_kernel, levels),
        in_specs=[HBM] * 4,
        out_specs=[HBM] * len(sizes),
        out_shape=[jax.ShapeDtypeStruct((2, rows, WIDTH), jnp.bfloat16) for rows in sizes],
        scratch_shapes=[
            pltpu.VMEM(small.shape, jnp.bfloat16),
            pltpu.VMEM(large.shape, jnp.bfloat16),
            pltpu.VMEM((2, TOK, WIDTH), jnp.bfloat16),
        ]
        + [pltpu.VMEM((2, rows, WIDTH), jnp.bfloat16) for rows in sizes]
        + [
            pltpu.SemaphoreType.DMA((10,)),
            pltpu.SemaphoreType.DMA((8, len(sizes))),
        ],
        compiler_params=pltpu.CompilerParams(vmem_limit_bytes=VMEM_CLAIM),
        cost_estimate=pl.CostEstimate(flops=2 * 256 * 512 * 4096, bytes_accessed=6 * MIB, transcendentals=0),
        name="pool_keys_values",
    )(small, large, keys, values)


def far_offsets(levels):
    offsets, total = {}, 0
    for level in range(FIRST, levels + 1):
        offsets[level] = total
        total += UNITS * count_of(level)
    return offsets, total


def lane_block(index):
    return slice(index * HEAD, (index + 1) * HEAD)


def near_kernel(levels, first, heads, pool_ref, q_ref, k_ref, v_ref, num_out, stat_out, far_out, *scratch):
    (pool, q, k, v, num, stat, far, ordered, coarse_q, coarse_k, coarse_v, bias, scores_a, scores_b, scores_c) = scratch[:15]
    probs_a, probs_b, probs_c, sems, head_sems = scratch[15:]
    width = heads * HEAD
    cols = slice(first * HEAD, first * HEAD + width)
    copies = [
        pltpu.make_async_copy(pool_ref, pool, sems.at[0]),
        pltpu.make_async_copy(q_ref.at[:, cols], q, sems.at[1]),
        pltpu.make_async_copy(k_ref.at[:, cols], k, sems.at[2]),
        pltpu.make_async_copy(v_ref.at[:, cols], v, sems.at[3]),
    ]
    for copy in copies:
        copy.start()
    row = lax.broadcasted_iota(jnp.int32, (BLOCK, BLOCK), 0)
    position = lax.broadcasted_iota(jnp.int32, (BLOCK, BLOCK), 1)
    bias[...] = jnp.where(row <= token_of(position), 0.0, NEG)
    copies[0].wait()
    copies[1].wait()

    offsets, _ = far_offsets(levels)
    for unit in range(UNITS):
        pooled = dot(pool[...], q[unit * BLOCK : (unit + 1) * BLOCK, :])
        ordered[unit * BLOCK : (unit + 1) * BLOCK, :] = pooled[:BLOCK].astype(jnp.bfloat16)
        if unit >= 2:
            coarse_q[(unit - 2) * 128 : (unit - 1) * 128, :] = pooled[BLOCK : BLOCK + 128].astype(jnp.bfloat16)
        start = BLOCK + 128
        for level in range(FIRST, levels + 1):
            count = count_of(level)
            place = offsets[level] + unit * count
            far[place : place + count, :] = pooled[start : start + count].astype(jnp.bfloat16)
            start += count
    sends = [pltpu.make_async_copy(far, far_out, sems.at[4])]
    sends[0].start()
    copies[2].wait()
    copies[3].wait()
    for unit in range(2):
        rows = slice(unit * BLOCK, (unit + 1) * BLOCK)
        half = slice(unit * 128, (unit + 1) * 128)
        coarse_k[half, :] = dot(pool[BLOCK : BLOCK + 128, :], k[rows, :]).astype(jnp.bfloat16)
        coarse_v[half, :] = dot(pool[BLOCK : BLOCK + 128, :], v[rows, :]).astype(jnp.bfloat16)

    def num_copy(head, tile):
        rows = lane_block(head)
        lanes = slice(tile * 2 * BLOCK, (tile + 1) * 2 * BLOCK)
        return pltpu.make_async_copy(num.at[rows, lanes], num_out.at[rows, lanes], head_sems.at[head, tile])

    def dot_pieces(head):
        slot, own = head % 2, lane_block(head)

        def coarse():
            scores_c[slot] = dot_t(coarse_k[:, own], coarse_q[:, own])

        def part(tile, piece):
            base = 2 * tile * BLOCK
            if piece < 2:
                rows = slice(base + piece * BLOCK, base + (piece + 1) * BLOCK)
                scores_a[slot, tile, :, piece * BLOCK : (piece + 1) * BLOCK] = dot_t(
                    k[base : base + BLOCK, own], ordered[rows, own]
                )
            else:
                rows = slice(base + BLOCK, base + 2 * BLOCK)
                scores_b[slot, tile] = dot_t(k[rows, own], ordered[rows, own])

        return [coarse] + [functools.partial(part, tile, piece) for tile in (1, 0) for piece in range(3)]

    def soft_a(head, tile, block):
        slot, lanes = head % 2, lane_block(block)
        return soft_columns(
            [lambda span: scores_a[slot, tile, span, lanes] + bias[span, lanes]], [probs_a.at[slot, tile, :, lanes]]
        )

    def soft_b(head, tile, block):
        slot, lanes, late = head % 2, lane_block(block), lane_block(2 + block)
        return soft_columns(
            [
                lambda span: scores_a[slot, tile, span, late],
                lambda span: scores_b[slot, tile, span, lanes] + bias[span, lanes],
            ],
            [probs_a.at[slot, tile, :, late], probs_b.at[slot, tile, :, lanes]],
        )

    def soft_c(head, block):
        slot, lanes = head % 2, lane_block(block)
        return soft_columns([lambda span: scores_c[slot, span, lanes]], [probs_c.at[slot, :, lanes]])

    def weigh(head, tile):
        slot, own, base = head % 2, lane_block(head), 2 * tile * BLOCK
        both = dot_first(v[base : base + BLOCK, own], probs_a[slot, tile])
        more = dot_first(v[base + BLOCK : base + 2 * BLOCK, own], probs_b[slot, tile])
        nums = [both[:, lane_block(0)], both[:, lane_block(1)]]
        return nums + [both[:, lane_block(2 + block)] + more[:, lane_block(block)] for block in range(2)]

    def keep(head, tile, states):
        for index, state in enumerate(states):
            lanes = lane_block(4 * tile + index)
            num[lane_block(head), lanes] = state[0]
            stat[head, 0:1, lanes] = state[1]
            stat[head, 1:2, lanes] = state[2]
        num_copy(head, tile).start()

    def finish_late(head, nums, stats, coarse_num, coarse_stats):
        states = []
        for block in range(4):
            unit = block // 2
            coarse = (2.0 * coarse_num[:, lane_block(unit)], coarse_stats[unit][0], 2.0 * coarse_stats[unit][1])
            states.append(merge((nums[block],) + stats[block], coarse))
        keep(head, 1, states)

    for piece in dot_pieces(0):
        piece()
    pending = None
    for head in range(heads):
        pieces = dot_pieces(head + 1) if head + 1 < heads else []

        def more():
            if pieces:
                pieces.pop(0)()

        coarse_stats = [soft_c(head, 0)]
        more()
        if pending is not None:
            pending()
        coarse_stats.append(soft_c(head, 1))
        more()
        coarse_num = dot_first(coarse_v[:, lane_block(head)], probs_c[head % 2])
        late_stats = []
        for block in range(2):
            late_stats.append(soft_a(head, 1, block))
            more()
        for block in range(2):
            late_stats.append(soft_b(head, 1, block))
            more()
        nums = weigh(head, 1)
        stats = [soft_a(head, 0, 0)]
        more()
        stats.append(soft_a(head, 0, 1))
        finish_late(head, nums, late_stats, coarse_num, coarse_stats)
        for block in range(2):
            stats.append(soft_b(head, 0, block))

        def pending(head=head, stats=stats):
            keep(head, 0, [(item,) + pair for item, pair in zip(weigh(head, 0), stats)])

    pending()
    sends.append(pltpu.make_async_copy(stat, stat_out, sems.at[5]))
    sends[-1].start()
    for send in sends:
        send.wait()
    for head in range(heads):
        for tile in range(2):
            num_copy(head, tile).wait()


def near_call(queries, keys, values, levels, index):
    pool = as_bf16(padded(np.concatenate([pool_rows(level) for level in range(levels + 1)]), 16))
    first, heads = SLICES[index]
    width = heads * HEAD
    _, far_rows = far_offsets(levels)
    bf16, f32 = jnp.bfloat16, jnp.float32
    return pl.pallas_call(
        functools.partial(near_kernel, levels, first, heads),
        in_specs=[HBM] * 4,
        out_specs=[HBM] * 3,
        out_shape=[
            jax.ShapeDtypeStruct((width, TOK), f32),
            jax.ShapeDtypeStruct((heads, 8, TOK), f32),
            jax.ShapeDtypeStruct((far_rows, width), bf16),
        ],
        scratch_shapes=[
            pltpu.VMEM(pool.shape, bf16),
            pltpu.VMEM((TOK, width), bf16),
            pltpu.VMEM((TOK, width), bf16),
            pltpu.VMEM((TOK, width), bf16),
            pltpu.VMEM((width, TOK), f32),
            pltpu.VMEM((heads, 8, TOK), f32),
            pltpu.VMEM((far_rows, width), bf16),
            pltpu.VMEM((TOK, width), bf16),
            pltpu.VMEM((BLOCK, width), bf16),
            pltpu.VMEM((BLOCK, width), bf16),
            pltpu.VMEM((BLOCK, width), bf16),
            pltpu.VMEM((BLOCK, BLOCK), f32),
            pltpu.VMEM((2, 2, BLOCK, 2 * BLOCK), f32),
            pltpu.VMEM((2, 2, BLOCK, BLOCK), f32),
            pltpu.VMEM((2, BLOCK, BLOCK), f32),
            pltpu.VMEM((2, 2, BLOCK, 2 * BLOCK), bf16),
            pltpu.VMEM((2, 2, BLOCK, BLOCK), bf16),
            pltpu.VMEM((2, BLOCK, BLOCK), bf16),
            pltpu.SemaphoreType.DMA((6,)),
            pltpu.SemaphoreType.DMA((heads, 2)),
        ],
        compiler_params=pltpu.CompilerParams(vmem_limit_bytes=VMEM_CLAIM),
        cost_estimate=pl.CostEstimate(flops=8_000_000_000, bytes_accessed=4 * MIB, transcendentals=0),
        name="near_levels",
    )(pool, queries, keys, values)


def by_lane_group(arrays, size):
    lane = lax.broadcasted_iota(jnp.int32, arrays[0].shape, 1)
    result = arrays[-1]
    for index in range(len(arrays) - 2, -1, -1):
        result = jnp.where(lane < (index + 1) * size, arrays[index], result)
    return result


def widen_to_second(array):
    r32, r64, r96 = [pltpu.roll(array, shift, 1) for shift in (32, 64, 96)]
    return [by_lane_group([array, r32, r32, r64], 32), by_lane_group([r64, r96, r96, array], 32)]


def widen_to_units(arrays):
    units = []
    for array in arrays:
        turned = pltpu.roll(array, 64, 1)
        units += [by_lane_group([array, turned], 64), by_lane_group([turned, array], 64)]
    return units


def far_kernel(levels, plan, *refs):
    crossing = range(FIRST, levels + 1)
    bundles = 1 + max(bundle for _, bundle, _ in plan)
    kv_refs = refs[:bundles]
    refs = refs[bundles:]
    slices = len(SLICES)
    far_refs, num_refs, stat_refs = refs[:slices], refs[slices : 2 * slices], refs[2 * slices : 3 * slices]
    turn_ref, w_ref, out_ref = refs[3 * slices : 3 * slices + 3]
    kv, queries, num, stat, turn, weights, scores, probs = refs[3 * slices + 3 : 3 * slices + 11]
    mixed, natural, stage, partial, kv_sems, near_sems, out_sems = refs[3 * slices + 11 :]
    pair = 2 * HEAD
    model = w_ref.shape[1]
    step = 256
    offsets, far_rows = far_offsets(levels)

    def kv_copies(index):
        cols = slice(index * pair, (index + 1) * pair)
        made = []
        for number, (level, bundle, spans) in enumerate(plan):
            source_start, target_start, rows = spans
            made.append(
                pltpu.make_async_copy(
                    kv_refs[bundle].at[:, source_start : source_start + rows, cols],
                    kv.at[level - FIRST, :, target_start : target_start + rows, cols],
                    kv_sems.at[index, number],
                )
            )
        return made

    far_copies, near_copies = [], []
    for index, (first, heads) in enumerate(SLICES):
        cols = slice(first * HEAD, (first + heads) * HEAD)
        group = slice(first, first + heads)
        sems = [near_sems.at[place * slices + index] for place in range(3)]
        far_copies.append(pltpu.make_async_copy(far_refs[index], queries.at[:, cols], sems[0]))
        near_copies.append(
            [
                pltpu.make_async_copy(num_refs[index], num.at[cols, :], sems[1]),
                pltpu.make_async_copy(stat_refs[index], stat.at[group], sems[2]),
            ]
        )
    turn_copy = pltpu.make_async_copy(turn_ref, turn, near_sems.at[3 * slices])
    half = WIDTH // 2
    w_copies = [
        pltpu.make_async_copy(w_ref.at[rows], weights.at[rows], near_sems.at[3 * slices + 1 + index])
        for index, rows in enumerate((slice(0, half), slice(half, WIDTH)))
    ]
    stages = [
        far_copies[:1] + kv_copies(0) + near_copies[0],
        far_copies[1:2] + kv_copies(1) + [turn_copy],
        far_copies[2:] + kv_copies(2) + near_copies[1] + w_copies[:1],
        kv_copies(3) + near_copies[2] + w_copies[1:],
    ]

    def start_stage(number):
        for copy in stages[number]:
            copy.start()

    start_stage(0)
    start_stage(1)

    def turned(part):
        cols = slice(part * half, (part + 1) * half)
        for unit in range(UNITS):
            rows = slice(unit * BLOCK, (unit + 1) * BLOCK)
            natural[rows, cols] = dot_t(turn[...], mixed[cols, rows]).astype(jnp.bfloat16)

    def first_product(index):
        cols = slice(index * step, (index + 1) * step)
        partial[:, cols] = dot(natural[:, :half], weights[:half, cols])

    def score(head, level):
        own = lane_block(head)
        span = slice(offsets[level], offsets[level] + UNITS * count_of(level))
        scores[head % 2, :, span] = dot_t(kv[level - FIRST, 0, :, own], queries[span, own])

    def soft(head, level):
        blocks = range(offsets[level] // HEAD, (offsets[level] + UNITS * count_of(level)) // HEAD)
        return [
            soft_columns(
                [lambda span, block=block: scores[head % 2, span, lane_block(block)]], [probs.at[head % 2, :, lane_block(block)]]
            )
            for block in blocks
        ]

    def weigh(head, level, stats):
        own = lane_block(head)
        span = slice(offsets[level], offsets[level] + UNITS * count_of(level))
        live = ((position >> (level - FIRST)) & 1) == 1
        factor = jnp.where(live, 2.0**level, 0.0)
        weighted = factor * dot_first(kv[level - FIRST, 1, :, own], probs[head % 2, :, span])
        return [
            (weighted[:, lane_block(block)], jnp.where(live, peak, NEG), factor * total)
            for block, (peak, total) in enumerate(stats)
        ]

    def join(state, terms):
        if state is None:
            return terms
        if len(terms) > len(state):
            wide = [widen_to_second(item) for item in state[0]]
            state = [tuple(item[side] for item in wide) for side in range(2)]
        return [merge(old, new) for old, new in zip(state, terms)]

    def mix(head, state):
        own = lane_block(head)
        wide = [widen_to_units([half[place] for half in state]) for place in range(3)]
        for unit in range(UNITS):
            far_num, far_peak, far_total = [item[unit] for item in wide]
            for block in range(2 * unit, 2 * unit + 2):
                peak = stat[head, 0:1, lane_block(block)]
                total = stat[head, 1:2, lane_block(block)]
                top = jnp.maximum(peak, far_peak)
                a = jnp.exp(peak - top)
                b = jnp.exp(far_peak - top)
                inverse = 1.0 / (a * total + b * far_total)
                both = (a * inverse) * num[own, lane_block(block)] + (b * inverse) * far_num
                mixed[own, lane_block(block)] = both.astype(jnp.bfloat16)

    position = lax.axis_index("seq")
    order = list(range(levels, FIRST - 1, -1))
    for copy in far_copies[:1] + kv_copies(0):
        copy.wait()
    start_stage(2)
    for level in order:
        score(0, level)
    for copy in near_copies[0]:
        copy.wait()
    pending = None
    products = [functools.partial(first_product, index) for index in range(model // step)]
    for head in range(HEADS):
        if head % 2 == 1 and head + 1 < HEADS:
            for copy in kv_copies((head + 1) // 2):
                copy.wait()
        for index, (first, _) in enumerate(SLICES):
            if index and first == head + 1:
                far_copies[index].wait()
        if head == 1:
            start_stage(3)
        for index, (first, _) in enumerate(SLICES):
            if index and first == head:
                for copy in near_copies[index]:
                    copy.wait()
        terms = []
        for level in order:
            stats = soft(head, level)
            if head + 1 < HEADS:
                score(head + 1, level)
            if level == order[0] and pending is not None:
                pending()
                if head == HEADS // 2:
                    turn_copy.wait()
                    w_copies[0].wait()
                    turned(0)
            elif head >= HEADS // 2 and products:
                products.pop(0)()
            terms.append(weigh(head, level, stats))

        def pending(head=head, terms=terms):
            mix(head, functools.reduce(join, terms, None))

    pending()

    for product in products:
        product()
    turned(1)
    w_copies[1].wait()
    sends = []
    for index in range(model // step):
        cols = slice(index * step, (index + 1) * step)
        stage[:, cols] = (partial[:, cols] + dot(natural[:, half:], weights[half:, cols])).astype(jnp.bfloat16)
        sends.append(pltpu.make_async_copy(stage.at[:, cols], out_ref.at[:, cols], out_sems.at[index]))
        sends[-1].start()
    for send in sends:
        send.wait()


def far_call(bundles, plan, near, w_out, levels):
    turn = np.zeros((BLOCK, BLOCK))
    turn[token_of(np.arange(BLOCK)), np.arange(BLOCK)] = 1.0
    nums, stats, fars = [[item[place] for item in near] for place in range(3)]
    model = w_out.shape[1]
    _, far_rows = far_offsets(levels)
    count = levels - FIRST + 1
    bf16, f32 = jnp.bfloat16, jnp.float32
    return pl.pallas_call(
        functools.partial(far_kernel, levels, plan),
        in_specs=[HBM] * (len(bundles) + 3 * len(SLICES) + 2),
        out_specs=HBM,
        out_shape=jax.ShapeDtypeStruct((TOK, model), bf16),
        scratch_shapes=[
            pltpu.VMEM((count, 2, BLOCK, WIDTH), bf16),
            pltpu.VMEM((far_rows, WIDTH), bf16),
            pltpu.VMEM((WIDTH, TOK), f32),
            pltpu.VMEM((HEADS, 8, TOK), f32),
            pltpu.VMEM((BLOCK, BLOCK), bf16),
            pltpu.VMEM((WIDTH, model), bf16),
            pltpu.VMEM((2, BLOCK, far_rows), f32),
            pltpu.VMEM((2, BLOCK, far_rows), bf16),
            pltpu.VMEM((WIDTH, TOK), bf16),
            pltpu.VMEM((TOK, WIDTH), bf16),
            pltpu.VMEM((TOK, model), bf16),
            pltpu.VMEM((TOK, model), f32),
            pltpu.SemaphoreType.DMA((HEADS // 2, len(plan))),
            pltpu.SemaphoreType.DMA((3 * len(SLICES) + 3,)),
            pltpu.SemaphoreType.DMA((model // 256,)),
        ],
        compiler_params=pltpu.CompilerParams(vmem_limit_bytes=VMEM_CLAIM),
        cost_estimate=pl.CostEstimate(flops=6_500_000_000, bytes_accessed=18 * MIB, transcendentals=3_000_000),
        name="far_levels_projection",
    )(*bundles, *fars, *nums, *stats, as_bf16(turn), w_out)


def moved(array, distance):
    return lax.ppermute(array, "seq", [(i ^ distance, i) for i in range(lax.axis_size("seq"))])


def gathered(array, distances):
    size = lax.axis_size("seq")
    got = lax.ppermute(array, "seq", [(i ^ distances[i % 2], i) for i in range(size)])
    return jnp.concatenate([array, got], axis=1)


def after(arrays, others):
    return lax.optimization_barrier((arrays, others))[0]


def on_device(queries, keys, values, w_out):
    size = lax.axis_size("seq")
    levels = (TOK * size // (2 * BLOCK)).bit_length() - 1
    pooled = pool_call(keys, values, levels)

    places, _ = packed(levels)
    blocks = {2: pooled[0], 4: pooled[3]}
    for level in range(TOP, levels + 1):
        place, first = places[level]
        blocks[level] = pooled[place][:, first : first + (TOK >> level)]
    high = list(range(TOP, levels + 1))

    for distance in [1 << (level - FIRST) for level in high]:
        members = [level for level in high if 1 << (level - FIRST) >= distance]
        sent = pooled[-1] if distance == GROUP else jnp.concatenate([blocks[level] for level in members], axis=1)
        got = moved(sent, distance)
        start = 0
        for level in members:
            rows = blocks[level].shape[1]
            piece = got[:, start : start + rows]
            start += rows
            if 1 << (level - FIRST) == distance:
                blocks[level] = piece
            else:
                blocks[level] = jnp.concatenate([blocks[level], piece], axis=1)
        if distance == GROUP:
            fourth = moved(blocks[4], 4)
            third = [moved(pooled[1], 2)]
            arrived = blocks[TOP]
            third.append(moved(after(pooled[2], arrived), 2))
            second = moved(after(blocks[2], arrived), 1)

    upper = jnp.concatenate([blocks[level] for level in high], axis=1)
    near = [near_call(after(queries, arrived), keys, values, levels, 0)]
    once = gathered(after(upper, near[0]), (2, 4))
    fourth = gathered(after(fourth, (near[0], upper)), (2, 2))
    near.append(near_call(after(queries, (near[0], upper)), keys, values, levels, 1))
    joined = gathered(after(once, near[1]), (4, 2))
    low = jnp.concatenate([*after(third, near[1]), fourth], axis=1)
    low_got = moved(low, 1)
    near.append(near_call(after(queries, (near[1], once)), keys, values, levels, 2))
    top = after(joined, near[2])
    top_got = moved(top, 1)
    plan = [(2, 4, (0, 0, BLOCK))]
    for level in (3, 4):
        plan += [(level, bundle, ((level - 3) * 128, bundle * 128, 128)) for bundle in (0, 1)]
    for level in high:
        for piece in range(4):
            start = (piece * len(high) + level - TOP) * 32
            plan += [(level, bundle, (start, (bundle - 2) * 128 + piece * 32, 32)) for bundle in (2, 3)]
    return far_call([low, low_got, top, top_got, second], plan, near, w_out, levels)


def solution(mesh):
    return jax.shard_map(
        on_device,
        mesh=mesh,
        in_specs=(P("seq", None), P("seq", None), P("seq", None), P()),
        out_specs=P("seq", None),
        check_vma=False,
    )
```

```python
import functools

import jax
import jax.numpy as jnp
import numpy as np
from jax import lax
from jax.experimental import pallas as pl
from jax.experimental.pallas import tpu as pltpu
from jax.sharding import PartitionSpec as P

HEADS = 8
HEAD = 128
BLOCK = 256
TOK = 1024
UNITS = TOK // BLOCK
WIDTH = HEADS * HEAD
NEG = -1e30
FIRST = 2
TOP = 5
GROUP = 8
SCALE = HEAD**-0.5
LOG2E = 1.4426950408889634
MIB = 1 << 20
SLICES = ((0, 3), (3, 3), (6, 2))
VMEM_CLAIM = 60 * MIB
HBM = pl.BlockSpec(memory_space=pltpu.HBM)


def token_of(position):
    return ((position & 31) << 3) | (((position >> 5) & 1) << 2) | (((position >> 6) & 1) << 1) | (position >> 7)


def count_of(level):
    return max(BLOCK >> level, 32)


def pool_rows(level):
    rows = token_of(np.arange(count_of(level))) >> level
    columns = np.arange(BLOCK) >> level
    return (rows[:, None] == columns[None, :]) * 2.0**-level


def natural_pool(level, span):
    rows = np.arange(span >> level)
    return (rows[:, None] == (np.arange(span) >> level)[None, :]) * 2.0**-level


def padded(array, multiple):
    return np.pad(array, ((0, -len(array) % multiple), (0, 0)))


def as_bf16(array):
    return jnp.asarray(array.astype(np.float32)).astype(jnp.bfloat16)


def dot(a, b):
    return jnp.dot(a, b, preferred_element_type=jnp.float32)


def dot_t(a, b):
    return lax.dot_general(a, b, (((1,), (1,)), ((), ())), preferred_element_type=jnp.float32)


def dot_first(a, b):
    return lax.dot_general(a, b, (((0,), (0,)), ((), ())), preferred_element_type=jnp.float32)


def merge(first, second):
    top = jnp.maximum(first[1], second[1])
    a = jnp.exp(first[1] - top)
    b = jnp.exp(second[1] - top)
    return (a * first[0] + b * second[0], top, a * first[2] + b * second[2])


ROWS = 64


def soft_columns(loads, targets):
    spans = [slice(start, start + ROWS) for start in range(0, BLOCK, ROWS)]
    peak = None
    for load in loads:
        for span in spans:
            rows = jnp.max(load(span).reshape(ROWS // 8, 8, HEAD), axis=0)
            peak = rows if peak is None else jnp.maximum(peak, rows)
    peak = jnp.max(peak, axis=0, keepdims=True)
    total = jnp.zeros((8, HEAD), jnp.float32)
    for load, target in zip(loads, targets):
        for span in spans:
            probs = jnp.exp2((load(span) - peak) * (SCALE * LOG2E))
            total = total + jnp.sum(probs.reshape(ROWS // 8, 8, HEAD), axis=0)
            target[span, :] = probs.astype(jnp.bfloat16)
    return peak * SCALE, jnp.sum(total, axis=0, keepdims=True)


def packed(levels):
    places, rows = {2: (0, 0), 3: (1, 0), 4: (3, 0)}, 0
    for level in range(TOP, levels + 1):
        places[level] = (4, rows)
        rows += TOK >> level
    return places, [TOK >> 2, TOK >> 4, TOK >> 4, TOK >> 4, rows]


def pool_kernel(levels, small_ref, large_ref, keys_ref, values_ref, *refs):
    places, sizes = packed(levels)
    count = len(sizes)
    targets, (small, large, buffers, *outs, sems, out_sems) = refs[:count], refs[count:]
    step = WIDTH // 4
    fixed = [pltpu.make_async_copy(small_ref, small, sems.at[8]), pltpu.make_async_copy(large_ref, large, sems.at[9])]
    copies = []
    for index, source in enumerate((keys_ref, values_ref)):
        for part in range(4):
            cols = slice(part * step, (part + 1) * step)
            copies.append(pltpu.make_async_copy(source.at[:, cols], buffers.at[index, :, cols], sems.at[index * 4 + part]))
    for copy in fixed + copies:
        copy.start()
    for copy in fixed:
        copy.wait()
    sends = []
    for index in range(2):
        for part in range(4):
            cols = slice(part * step, (part + 1) * step)
            copies[index * 4 + part].wait()
            tiles = [
                dot(small[...], buffers[index, i * 2 * BLOCK : (i + 1) * 2 * BLOCK, cols]) for i in range(UNITS // 2)
            ]
            offset = 0
            for level in range(FIRST, min(levels, 6) + 1):
                rows = 2 * BLOCK >> level
                if level == 3:
                    for place, tile in enumerate(tiles):
                        outs[1 + place][index, :, cols] = tile[offset : offset + rows].astype(jnp.bfloat16)
                    offset += rows
                    continue
                both = jnp.concatenate([tile[offset : offset + rows] for tile in tiles], axis=0)
                place, first = places[level]
                outs[place][index, first : first + 2 * rows, cols] = both.astype(jnp.bfloat16)
                offset += rows
            if levels > 6:
                rest = dot(large[...], buffers[index, :, cols])
                for level in range(7, levels + 1):
                    start = (level - 7) * 8
                    place, first = places[level]
                    outs[place][index, first : first + (TOK >> level), cols] = rest[start : start + (TOK >> level)].astype(jnp.bfloat16)
            for place, (out, target) in enumerate(zip(outs, targets)):
                span = (index, slice(None), cols)
                sends.append(pltpu.make_async_copy(out.at[span], target.at[span], out_sems.at[index * 4 + part, place]))
                sends[-1].start()
    for send in sends:
        send.wait()


def pool_call(keys, values, levels):
    small = as_bf16(padded(np.concatenate([natural_pool(level, 2 * BLOCK) for level in range(FIRST, min(levels, 6) + 1)]), 16))
    parts = [padded(natural_pool(level, TOK), 8) for level in range(7, levels + 1)] + [np.zeros((8, TOK))]
    large = as_bf16(padded(np.concatenate(parts), 16))
    _, sizes = packed(levels)
    return pl.pallas_call(
        functools.partial(pool_kernel, levels),
        in_specs=[HBM] * 4,
        out_specs=[HBM] * len(sizes),
        out_shape=[jax.ShapeDtypeStruct((2, rows, WIDTH), jnp.bfloat16) for rows in sizes],
        scratch_shapes=[
            pltpu.VMEM(small.shape, jnp.bfloat16),
            pltpu.VMEM(large.shape, jnp.bfloat16),
            pltpu.VMEM((2, TOK, WIDTH), jnp.bfloat16),
        ]
        + [pltpu.VMEM((2, rows, WIDTH), jnp.bfloat16) for rows in sizes]
        + [
            pltpu.SemaphoreType.DMA((10,)),
            pltpu.SemaphoreType.DMA((8, len(sizes))),
        ],
        compiler_params=pltpu.CompilerParams(vmem_limit_bytes=VMEM_CLAIM),
        cost_estimate=pl.CostEstimate(flops=2 * 256 * 512 * 4096, bytes_accessed=6 * MIB, transcendentals=0),
        name="pool_keys_values",
    )(small, large, keys, values)


def far_offsets(levels):
    offsets, total = {}, 0
    for level in range(FIRST, levels + 1):
        offsets[level] = total
        total += UNITS * count_of(level)
    return offsets, total


def lane_block(index):
    return slice(index * HEAD, (index + 1) * HEAD)


def near_kernel(levels, first, heads, pool_ref, q_ref, k_ref, v_ref, num_out, stat_out, far_out, *scratch):
    (pool, q, k, v, num, stat, far, ordered, coarse_q, coarse_k, coarse_v, bias, scores_a, scores_b, scores_c) = scratch[:15]
    probs_a, probs_b, probs_c, sems, head_sems = scratch[15:]
    width = heads * HEAD
    cols = slice(first * HEAD, first * HEAD + width)
    copies = [
        pltpu.make_async_copy(pool_ref, pool, sems.at[0]),
        pltpu.make_async_copy(q_ref.at[:, cols], q, sems.at[1]),
        pltpu.make_async_copy(k_ref.at[:, cols], k, sems.at[2]),
        pltpu.make_async_copy(v_ref.at[:, cols], v, sems.at[3]),
    ]
    for copy in copies:
        copy.start()
    row = lax.broadcasted_iota(jnp.int32, (BLOCK, BLOCK), 0)
    position = lax.broadcasted_iota(jnp.int32, (BLOCK, BLOCK), 1)
    bias[...] = jnp.where(row <= token_of(position), 0.0, NEG)
    copies[0].wait()
    copies[1].wait()

    offsets, _ = far_offsets(levels)
    for unit in range(UNITS):
        pooled = dot(pool[...], q[unit * BLOCK : (unit + 1) * BLOCK, :])
        ordered[unit * BLOCK : (unit + 1) * BLOCK, :] = pooled[:BLOCK].astype(jnp.bfloat16)
        if unit >= 2:
            coarse_q[(unit - 2) * 128 : (unit - 1) * 128, :] = pooled[BLOCK : BLOCK + 128].astype(jnp.bfloat16)
        start = BLOCK + 128
        for level in range(FIRST, levels + 1):
            count = count_of(level)
            place = offsets[level] + unit * count
            far[place : place + count, :] = pooled[start : start + count].astype(jnp.bfloat16)
            start += count
    sends = [pltpu.make_async_copy(far, far_out, sems.at[4])]
    sends[0].start()
    copies[2].wait()
    copies[3].wait()
    for unit in range(2):
        rows = slice(unit * BLOCK, (unit + 1) * BLOCK)
        half = slice(unit * 128, (unit + 1) * 128)
        coarse_k[half, :] = dot(pool[BLOCK : BLOCK + 128, :], k[rows, :]).astype(jnp.bfloat16)
        coarse_v[half, :] = dot(pool[BLOCK : BLOCK + 128, :], v[rows, :]).astype(jnp.bfloat16)

    def num_copy(head, tile):
        rows = lane_block(head)
        lanes = slice(tile * 2 * BLOCK, (tile + 1) * 2 * BLOCK)
        return pltpu.make_async_copy(num.at[rows, lanes], num_out.at[rows, lanes], head_sems.at[head, tile])

    def dot_pieces(head):
        slot, own = head % 2, lane_block(head)

        def coarse():
            scores_c[slot] = dot_t(coarse_k[:, own], coarse_q[:, own])

        def part(tile, piece):
            base = 2 * tile * BLOCK
            if piece < 2:
                rows = slice(base + piece * BLOCK, base + (piece + 1) * BLOCK)
                scores_a[slot, tile, :, piece * BLOCK : (piece + 1) * BLOCK] = dot_t(
                    k[base : base + BLOCK, own], ordered[rows, own]
                )
            else:
                rows = slice(base + BLOCK, base + 2 * BLOCK)
                scores_b[slot, tile] = dot_t(k[rows, own], ordered[rows, own])

        return [coarse] + [functools.partial(part, tile, piece) for tile in (1, 0) for piece in range(3)]

    def soft_a(head, tile, block):
        slot, lanes = head % 2, lane_block(block)
        return soft_columns(
            [lambda span: scores_a[slot, tile, span, lanes] + bias[span, lanes]], [probs_a.at[slot, tile, :, lanes]]
        )

    def soft_b(head, tile, block):
        slot, lanes, late = head % 2, lane_block(block), lane_block(2 + block)
        return soft_columns(
            [
                lambda span: scores_a[slot, tile, span, late],
                lambda span: scores_b[slot, tile, span, lanes] + bias[span, lanes],
            ],
            [probs_a.at[slot, tile, :, late], probs_b.at[slot, tile, :, lanes]],
        )

    def soft_c(head, block):
        slot, lanes = head % 2, lane_block(block)
        return soft_columns([lambda span: scores_c[slot, span, lanes]], [probs_c.at[slot, :, lanes]])

    def weigh(head, tile):
        slot, own, base = head % 2, lane_block(head), 2 * tile * BLOCK
        both = dot_first(v[base : base + BLOCK, own], probs_a[slot, tile])
        more = dot_first(v[base + BLOCK : base + 2 * BLOCK, own], probs_b[slot, tile])
        nums = [both[:, lane_block(0)], both[:, lane_block(1)]]
        return nums + [both[:, lane_block(2 + block)] + more[:, lane_block(block)] for block in range(2)]

    def keep(head, tile, states):
        for index, state in enumerate(states):
            lanes = lane_block(4 * tile + index)
            num[lane_block(head), lanes] = state[0]
            stat[head, 0:1, lanes] = state[1]
            stat[head, 1:2, lanes] = state[2]
        num_copy(head, tile).start()

    def finish_late(head, nums, stats, coarse_num, coarse_stats):
        states = []
        for block in range(4):
            unit = block // 2
            coarse = (2.0 * coarse_num[:, lane_block(unit)], coarse_stats[unit][0], 2.0 * coarse_stats[unit][1])
            states.append(merge((nums[block],) + stats[block], coarse))
        keep(head, 1, states)

    for piece in dot_pieces(0):
        piece()
    pending = None
    for head in range(heads):
        pieces = dot_pieces(head + 1) if head + 1 < heads else []

        def more():
            if pieces:
                pieces.pop(0)()

        coarse_stats = [soft_c(head, 0)]
        more()
        if pending is not None:
            pending()
        coarse_stats.append(soft_c(head, 1))
        more()
        coarse_num = dot_first(coarse_v[:, lane_block(head)], probs_c[head % 2])
        late_stats = []
        for block in range(2):
            late_stats.append(soft_a(head, 1, block))
            more()
        for block in range(2):
            late_stats.append(soft_b(head, 1, block))
            more()
        nums = weigh(head, 1)
        stats = [soft_a(head, 0, 0)]
        more()
        stats.append(soft_a(head, 0, 1))
        finish_late(head, nums, late_stats, coarse_num, coarse_stats)
        for block in range(2):
            stats.append(soft_b(head, 0, block))

        def pending(head=head, stats=stats):
            keep(head, 0, [(item,) + pair for item, pair in zip(weigh(head, 0), stats)])

    pending()
    sends.append(pltpu.make_async_copy(stat, stat_out, sems.at[5]))
    sends[-1].start()
    for send in sends:
        send.wait()
    for head in range(heads):
        for tile in range(2):
            num_copy(head, tile).wait()


def near_call(queries, keys, values, levels, index):
    pool = as_bf16(padded(np.concatenate([pool_rows(level) for level in range(levels + 1)]), 16))
    first, heads = SLICES[index]
    width = heads * HEAD
    _, far_rows = far_offsets(levels)
    bf16, f32 = jnp.bfloat16, jnp.float32
    return pl.pallas_call(
        functools.partial(near_kernel, levels, first, heads),
        in_specs=[HBM] * 4,
        out_specs=[HBM] * 3,
        out_shape=[
            jax.ShapeDtypeStruct((width, TOK), f32),
            jax.ShapeDtypeStruct((heads, 8, TOK), f32),
            jax.ShapeDtypeStruct((far_rows, width), bf16),
        ],
        scratch_shapes=[
            pltpu.VMEM(pool.shape, bf16),
            pltpu.VMEM((TOK, width), bf16),
            pltpu.VMEM((TOK, width), bf16),
            pltpu.VMEM((TOK, width), bf16),
            pltpu.VMEM((width, TOK), f32),
            pltpu.VMEM((heads, 8, TOK), f32),
            pltpu.VMEM((far_rows, width), bf16),
            pltpu.VMEM((TOK, width), bf16),
            pltpu.VMEM((BLOCK, width), bf16),
            pltpu.VMEM((BLOCK, width), bf16),
            pltpu.VMEM((BLOCK, width), bf16),
            pltpu.VMEM((BLOCK, BLOCK), f32),
            pltpu.VMEM((2, 2, BLOCK, 2 * BLOCK), f32),
            pltpu.VMEM((2, 2, BLOCK, BLOCK), f32),
            pltpu.VMEM((2, BLOCK, BLOCK), f32),
            pltpu.VMEM((2, 2, BLOCK, 2 * BLOCK), bf16),
            pltpu.VMEM((2, 2, BLOCK, BLOCK), bf16),
            pltpu.VMEM((2, BLOCK, BLOCK), bf16),
            pltpu.SemaphoreType.DMA((6,)),
            pltpu.SemaphoreType.DMA((heads, 2)),
        ],
        compiler_params=pltpu.CompilerParams(vmem_limit_bytes=VMEM_CLAIM),
        cost_estimate=pl.CostEstimate(flops=8_000_000_000, bytes_accessed=4 * MIB, transcendentals=0),
        name="near_levels",
    )(pool, queries, keys, values)


def by_lane_group(arrays, size):
    lane = lax.broadcasted_iota(jnp.int32, arrays[0].shape, 1)
    result = arrays[-1]
    for index in range(len(arrays) - 2, -1, -1):
        result = jnp.where(lane < (index + 1) * size, arrays[index], result)
    return result


def widen_to_second(array):
    r32, r64, r96 = [pltpu.roll(array, shift, 1) for shift in (32, 64, 96)]
    return [by_lane_group([array, r32, r32, r64], 32), by_lane_group([r64, r96, r96, array], 32)]


def widen_to_units(arrays):
    units = []
    for array in arrays:
        turned = pltpu.roll(array, 64, 1)
        units += [by_lane_group([array, turned], 64), by_lane_group([turned, array], 64)]
    return units


def far_kernel(levels, plan, *refs):
    crossing = range(FIRST, levels + 1)
    bundles = 1 + max(bundle for _, bundle, _ in plan)
    kv_refs = refs[:bundles]
    refs = refs[bundles:]
    slices = len(SLICES)
    far_refs, num_refs, stat_refs = refs[:slices], refs[slices : 2 * slices], refs[2 * slices : 3 * slices]
    turn_ref, w_ref, out_ref = refs[3 * slices : 3 * slices + 3]
    kv, queries, num, stat, turn, weights, scores, probs = refs[3 * slices + 3 : 3 * slices + 11]
    mixed, natural, stage, partial, kv_sems, near_sems, out_sems = refs[3 * slices + 11 :]
    pair = 2 * HEAD
    model = w_ref.shape[1]
    step = 256
    offsets, far_rows = far_offsets(levels)

    def kv_copies(index):
        cols = slice(index * pair, (index + 1) * pair)
        made = []
        for number, (level, bundle, spans) in enumerate(plan):
            source_start, target_start, rows = spans
            made.append(
                pltpu.make_async_copy(
                    kv_refs[bundle].at[:, source_start : source_start + rows, cols],
                    kv.at[level - FIRST, :, target_start : target_start + rows, cols],
                    kv_sems.at[index, number],
                )
            )
        return made

    far_copies, near_copies = [], []
    for index, (first, heads) in enumerate(SLICES):
        cols = slice(first * HEAD, (first + heads) * HEAD)
        group = slice(first, first + heads)
        sems = [near_sems.at[place * slices + index] for place in range(3)]
        far_copies.append(pltpu.make_async_copy(far_refs[index], queries.at[:, cols], sems[0]))
        near_copies.append(
            [
                pltpu.make_async_copy(num_refs[index], num.at[cols, :], sems[1]),
                pltpu.make_async_copy(stat_refs[index], stat.at[group], sems[2]),
            ]
        )
    turn_copy = pltpu.make_async_copy(turn_ref, turn, near_sems.at[3 * slices])
    half = WIDTH // 2
    w_copies = [
        pltpu.make_async_copy(w_ref.at[rows], weights.at[rows], near_sems.at[3 * slices + 1 + index])
        for index, rows in enumerate((slice(0, half), slice(half, WIDTH)))
    ]
    stages = [
        far_copies[:1] + kv_copies(0) + near_copies[0],
        far_copies[1:2] + kv_copies(1) + [turn_copy],
        far_copies[2:] + kv_copies(2) + near_copies[1] + w_copies[:1],
        kv_copies(3) + near_copies[2] + w_copies[1:],
    ]

    def start_stage(number):
        for copy in stages[number]:
            copy.start()

    start_stage(0)
    start_stage(1)

    def turned(part):
        cols = slice(part * half, (part + 1) * half)
        for unit in range(UNITS):
            rows = slice(unit * BLOCK, (unit + 1) * BLOCK)
            natural[rows, cols] = dot_t(turn[...], mixed[cols, rows]).astype(jnp.bfloat16)

    def first_product(index):
        cols = slice(index * step, (index + 1) * step)
        partial[:, cols] = dot(natural[:, :half], weights[:half, cols])

    def score(head, level):
        own = lane_block(head)
        span = slice(offsets[level], offsets[level] + UNITS * count_of(level))
        scores[head % 2, :, span] = dot_t(kv[level - FIRST, 0, :, own], queries[span, own])

    def soft(head, level):
        blocks = range(offsets[level] // HEAD, (offsets[level] + UNITS * count_of(level)) // HEAD)
        return [
            soft_columns(
                [lambda span, block=block: scores[head % 2, span, lane_block(block)]], [probs.at[head % 2, :, lane_block(block)]]
            )
            for block in blocks
        ]

    def weigh(head, level, stats):
        own = lane_block(head)
        span = slice(offsets[level], offsets[level] + UNITS * count_of(level))
        live = ((position >> (level - FIRST)) & 1) == 1
        factor = jnp.where(live, 2.0**level, 0.0)
        weighted = factor * dot_first(kv[level - FIRST, 1, :, own], probs[head % 2, :, span])
        return [
            (weighted[:, lane_block(block)], jnp.where(live, peak, NEG), factor * total)
            for block, (peak, total) in enumerate(stats)
        ]

    def join(state, terms):
        if state is None:
            return terms
        if len(terms) > len(state):
            wide = [widen_to_second(item) for item in state[0]]
            state = [tuple(item[side] for item in wide) for side in range(2)]
        return [merge(old, new) for old, new in zip(state, terms)]

    def mix(head, state):
        own = lane_block(head)
        wide = [widen_to_units([half[place] for half in state]) for place in range(3)]
        for unit in range(UNITS):
            far_num, far_peak, far_total = [item[unit] for item in wide]
            for block in range(2 * unit, 2 * unit + 2):
                peak = stat[head, 0:1, lane_block(block)]
                total = stat[head, 1:2, lane_block(block)]
                top = jnp.maximum(peak, far_peak)
                a = jnp.exp(peak - top)
                b = jnp.exp(far_peak - top)
                inverse = 1.0 / (a * total + b * far_total)
                both = (a * inverse) * num[own, lane_block(block)] + (b * inverse) * far_num
                mixed[own, lane_block(block)] = both.astype(jnp.bfloat16)

    position = lax.axis_index("seq")
    order = list(range(levels, FIRST - 1, -1))
    for copy in far_copies[:1] + kv_copies(0):
        copy.wait()
    start_stage(2)
    for level in order:
        score(0, level)
    for copy in near_copies[0]:
        copy.wait()
    pending = None
    products = [functools.partial(first_product, index) for index in range(model // step)]
    for head in range(HEADS):
        if head % 2 == 1 and head + 1 < HEADS:
            for copy in kv_copies((head + 1) // 2):
                copy.wait()
        for index, (first, _) in enumerate(SLICES):
            if index and first == head + 1:
                far_copies[index].wait()
        if head == 1:
            start_stage(3)
        for index, (first, _) in enumerate(SLICES):
            if index and first == head:
                for copy in near_copies[index]:
                    copy.wait()
        terms = []
        for level in order:
            stats = soft(head, level)
            if head + 1 < HEADS:
                score(head + 1, level)
            if level == order[0] and pending is not None:
                pending()
                if head == HEADS // 2:
                    turn_copy.wait()
                    w_copies[0].wait()
                    turned(0)
            elif head >= HEADS // 2 and products:
                products.pop(0)()
            terms.append(weigh(head, level, stats))

        def pending(head=head, terms=terms):
            mix(head, functools.reduce(join, terms, None))

    pending()

    for product in products:
        product()
    turned(1)
    w_copies[1].wait()
    sends = []
    for index in range(model // step):
        cols = slice(index * step, (index + 1) * step)
        stage[:, cols] = (partial[:, cols] + dot(natural[:, half:], weights[half:, cols])).astype(jnp.bfloat16)
        sends.append(pltpu.make_async_copy(stage.at[:, cols], out_ref.at[:, cols], out_sems.at[index]))
        sends[-1].start()
    for send in sends:
        send.wait()


def far_call(bundles, plan, near, w_out, levels):
    turn = np.zeros((BLOCK, BLOCK))
    turn[token_of(np.arange(BLOCK)), np.arange(BLOCK)] = 1.0
    nums, stats, fars = [[item[place] for item in near] for place in range(3)]
    model = w_out.shape[1]
    _, far_rows = far_offsets(levels)
    count = levels - FIRST + 1
    bf16, f32 = jnp.bfloat16, jnp.float32
    return pl.pallas_call(
        functools.partial(far_kernel, levels, plan),
        in_specs=[HBM] * (len(bundles) + 3 * len(SLICES) + 2),
        out_specs=HBM,
        out_shape=jax.ShapeDtypeStruct((TOK, model), bf16),
        scratch_shapes=[
            pltpu.VMEM((count, 2, BLOCK, WIDTH), bf16),
            pltpu.VMEM((far_rows, WIDTH), bf16),
            pltpu.VMEM((WIDTH, TOK), f32),
            pltpu.VMEM((HEADS, 8, TOK), f32),
            pltpu.VMEM((BLOCK, BLOCK), bf16),
            pltpu.VMEM((WIDTH, model), bf16),
            pltpu.VMEM((2, BLOCK, far_rows), f32),
            pltpu.VMEM((2, BLOCK, far_rows), bf16),
            pltpu.VMEM((WIDTH, TOK), bf16),
            pltpu.VMEM((TOK, WIDTH), bf16),
            pltpu.VMEM((TOK, model), bf16),
            pltpu.VMEM((TOK, model), f32),
            pltpu.SemaphoreType.DMA((HEADS // 2, len(plan))),
            pltpu.SemaphoreType.DMA((3 * len(SLICES) + 3,)),
            pltpu.SemaphoreType.DMA((model // 256,)),
        ],
        compiler_params=pltpu.CompilerParams(vmem_limit_bytes=VMEM_CLAIM),
        cost_estimate=pl.CostEstimate(flops=6_500_000_000, bytes_accessed=18 * MIB, transcendentals=3_000_000),
        name="far_levels_projection",
    )(*bundles, *fars, *nums, *stats, as_bf16(turn), w_out)


def moved(array, distance):
    return lax.ppermute(array, "seq", [(i ^ distance, i) for i in range(lax.axis_size("seq"))])


def gathered(blocks, distance):
    sent = jnp.concatenate(blocks, axis=1) if len(blocks) > 1 else blocks[0]
    got = moved(sent, distance)
    joined, start = [], 0
    for block in blocks:
        rows = block.shape[1]
        joined.append(jnp.concatenate([block, got[:, start : start + rows]], axis=1))
        start += rows
    return joined


def after(arrays, others):
    return lax.optimization_barrier((arrays, others))[0]


def on_device(queries, keys, values, w_out):
    size = lax.axis_size("seq")
    levels = (TOK * size // (2 * BLOCK)).bit_length() - 1
    pooled = pool_call(keys, values, levels)

    places, _ = packed(levels)
    blocks = {2: pooled[0], 4: pooled[3]}
    for level in range(TOP, levels + 1):
        place, first = places[level]
        blocks[level] = pooled[place][:, first : first + (TOK >> level)]
    high = list(range(TOP, levels + 1))

    for distance in [1 << (level - FIRST) for level in high]:
        members = [level for level in high if 1 << (level - FIRST) >= distance]
        sent = pooled[-1] if distance == GROUP else jnp.concatenate([blocks[level] for level in members], axis=1)
        got = moved(sent, distance)
        start = 0
        for level in members:
            rows = blocks[level].shape[1]
            piece = got[:, start : start + rows]
            start += rows
            if 1 << (level - FIRST) == distance:
                blocks[level] = piece
            else:
                blocks[level] = jnp.concatenate([blocks[level], piece], axis=1)
        if distance == GROUP:
            fourth = moved(blocks[4], 4)
            third = [moved(pooled[1], 2)]
            arrived = blocks[TOP]
            third.append(moved(after(pooled[2], arrived), 2))
            second = moved(after(blocks[2], arrived), 1)

    upper = [blocks[level] for level in high[1:]]
    five = gathered([arrived], 2)
    near = [near_call(after(queries, arrived), keys, values, levels, 0)]
    upper = gathered(after(upper, near[0]), 4)
    five_y = gathered(after(five, near[0]), 4)
    fourth = gathered([after(fourth, near[0])], 2)[0]
    near.append(near_call(after(queries, (near[0], five)), keys, values, levels, 1))
    upper_x = gathered(after(upper, near[1]), 2)
    low = jnp.concatenate([*after(third, near[1]), fourth], axis=1)
    low_got = moved(low, 1)
    near.append(near_call(after(queries, (near[1], upper)), keys, values, levels, 2))
    top = jnp.concatenate(after(five_y + upper_x, near[2]), axis=1)
    top_got = moved(top, 1)
    plan = [(2, 4, (0, 0, BLOCK))]
    for level in (3, 4):
        plan += [(level, bundle, ((level - 3) * 128, bundle * 128, 128)) for bundle in (0, 1)]
    for level in high:
        plan += [(level, bundle, ((level - TOP) * 128, (bundle - 2) * 128, 128)) for bundle in (2, 3)]
    return far_call([low, low_got, top, top_got, second], plan, near, w_out, levels)


def solution(mesh):
    return jax.shard_map(
        on_device,
        mesh=mesh,
        in_specs=(P("seq", None), P("seq", None), P("seq", None), P()),
        out_specs=P("seq", None),
        check_vma=False,
    )
```

```python
import functools

import jax
import jax.numpy as jnp
import numpy as np
from jax import lax
from jax.experimental import pallas as pl
from jax.experimental.pallas import tpu as pltpu
from jax.sharding import PartitionSpec as P

HEADS = 8
HEAD = 128
BLOCK = 256
TOK = 1024
UNITS = TOK // BLOCK
WIDTH = HEADS * HEAD
NEG = -1e30
FIRST = 2
TOP = 5
GROUP = 8
SCALE = HEAD**-0.5
LOG2E = 1.4426950408889634
MIB = 1 << 20
SLICES = ((0, 3), (3, 2), (5, 3))
VMEM_CLAIM = 60 * MIB
HBM = pl.BlockSpec(memory_space=pltpu.HBM)


def token_of(position):
    return ((position & 31) << 3) | (((position >> 5) & 1) << 2) | (((position >> 6) & 1) << 1) | (position >> 7)


def count_of(level):
    return max(BLOCK >> level, 32)


def pool_rows(level):
    rows = token_of(np.arange(count_of(level))) >> level
    columns = np.arange(BLOCK) >> level
    return (rows[:, None] == columns[None, :]) * 2.0**-level


def natural_pool(level, span):
    rows = np.arange(span >> level)
    return (rows[:, None] == (np.arange(span) >> level)[None, :]) * 2.0**-level


def padded(array, multiple):
    return np.pad(array, ((0, -len(array) % multiple), (0, 0)))


def as_bf16(array):
    return jnp.asarray(array.astype(np.float32)).astype(jnp.bfloat16)


def dot(a, b):
    return jnp.dot(a, b, preferred_element_type=jnp.float32)


def dot_t(a, b):
    return lax.dot_general(a, b, (((1,), (1,)), ((), ())), preferred_element_type=jnp.float32)


def dot_first(a, b):
    return lax.dot_general(a, b, (((0,), (0,)), ((), ())), preferred_element_type=jnp.float32)


def merge(first, second):
    top = jnp.maximum(first[1], second[1])
    a = jnp.exp(first[1] - top)
    b = jnp.exp(second[1] - top)
    return (a * first[0] + b * second[0], top, a * first[2] + b * second[2])


ROWS = 64


def soft_columns(loads, targets):
    spans = [slice(start, start + ROWS) for start in range(0, BLOCK, ROWS)]
    peak = None
    for load in loads:
        for span in spans:
            rows = jnp.max(load(span).reshape(ROWS // 8, 8, HEAD), axis=0)
            peak = rows if peak is None else jnp.maximum(peak, rows)
    peak = jnp.max(peak, axis=0, keepdims=True)
    total = jnp.zeros((8, HEAD), jnp.float32)
    for load, target in zip(loads, targets):
        for span in spans:
            probs = jnp.exp2((load(span) - peak) * (SCALE * LOG2E))
            total = total + jnp.sum(probs.reshape(ROWS // 8, 8, HEAD), axis=0)
            target[span, :] = probs.astype(jnp.bfloat16)
    return peak * SCALE, jnp.sum(total, axis=0, keepdims=True)


def packed(levels):
    places, rows = {2: (0, 0), 3: (1, 0), 4: (3, 0)}, 0
    for level in range(TOP, levels + 1):
        places[level] = (4, rows)
        rows += TOK >> level
    return places, [TOK >> 2, TOK >> 4, TOK >> 4, TOK >> 4, rows]


def pool_kernel(levels, small_ref, large_ref, keys_ref, values_ref, *refs):
    places, sizes = packed(levels)
    count = len(sizes)
    targets, (small, large, buffers, *outs, sems, out_sems) = refs[:count], refs[count:]
    step = WIDTH // 4
    fixed = [pltpu.make_async_copy(small_ref, small, sems.at[8]), pltpu.make_async_copy(large_ref, large, sems.at[9])]
    copies = []
    for index, source in enumerate((keys_ref, values_ref)):
        for part in range(4):
            cols = slice(part * step, (part + 1) * step)
            copies.append(pltpu.make_async_copy(source.at[:, cols], buffers.at[index, :, cols], sems.at[index * 4 + part]))
    for copy in fixed + copies:
        copy.start()
    for copy in fixed:
        copy.wait()
    sends = []
    for index in range(2):
        for part in range(4):
            cols = slice(part * step, (part + 1) * step)
            copies[index * 4 + part].wait()
            tiles = [
                dot(small[...], buffers[index, i * 2 * BLOCK : (i + 1) * 2 * BLOCK, cols]) for i in range(UNITS // 2)
            ]
            offset = 0
            for level in range(FIRST, min(levels, 6) + 1):
                rows = 2 * BLOCK >> level
                if level == 3:
                    for place, tile in enumerate(tiles):
                        outs[1 + place][index, :, cols] = tile[offset : offset + rows].astype(jnp.bfloat16)
                    offset += rows
                    continue
                both = jnp.concatenate([tile[offset : offset + rows] for tile in tiles], axis=0)
                place, first = places[level]
                outs[place][index, first : first + 2 * rows, cols] = both.astype(jnp.bfloat16)
                offset += rows
            if levels > 6:
                rest = dot(large[...], buffers[index, :, cols])
                for level in range(7, levels + 1):
                    start = (level - 7) * 8
                    place, first = places[level]
                    outs[place][index, first : first + (TOK >> level), cols] = rest[start : start + (TOK >> level)].astype(jnp.bfloat16)
            for place, (out, target) in enumerate(zip(outs, targets)):
                span = (index, slice(None), cols)
                sends.append(pltpu.make_async_copy(out.at[span], target.at[span], out_sems.at[index * 4 + part, place]))
                sends[-1].start()
    for send in sends:
        send.wait()


def pool_call(keys, values, levels):
    small = as_bf16(padded(np.concatenate([natural_pool(level, 2 * BLOCK) for level in range(FIRST, min(levels, 6) + 1)]), 16))
    parts = [padded(natural_pool(level, TOK), 8) for level in range(7, levels + 1)] + [np.zeros((8, TOK))]
    large = as_bf16(padded(np.concatenate(parts), 16))
    _, sizes = packed(levels)
    return pl.pallas_call(
        functools.partial(pool_kernel, levels),
        in_specs=[HBM] * 4,
        out_specs=[HBM] * len(sizes),
        out_shape=[jax.ShapeDtypeStruct((2, rows, WIDTH), jnp.bfloat16) for rows in sizes],
        scratch_shapes=[
            pltpu.VMEM(small.shape, jnp.bfloat16),
            pltpu.VMEM(large.shape, jnp.bfloat16),
            pltpu.VMEM((2, TOK, WIDTH), jnp.bfloat16),
        ]
        + [pltpu.VMEM((2, rows, WIDTH), jnp.bfloat16) for rows in sizes]
        + [
            pltpu.SemaphoreType.DMA((10,)),
            pltpu.SemaphoreType.DMA((8, len(sizes))),
        ],
        compiler_params=pltpu.CompilerParams(vmem_limit_bytes=VMEM_CLAIM),
        cost_estimate=pl.CostEstimate(flops=2 * 256 * 512 * 4096, bytes_accessed=6 * MIB, transcendentals=0),
        name="pool_keys_values",
    )(small, large, keys, values)


def far_offsets(levels):
    offsets, total = {}, 0
    for level in range(FIRST, levels + 1):
        offsets[level] = total
        total += UNITS * count_of(level)
    return offsets, total


def lane_block(index):
    return slice(index * HEAD, (index + 1) * HEAD)


def near_kernel(levels, first, heads, pool_ref, q_ref, k_ref, v_ref, num_out, stat_out, far_out, *scratch):
    (pool, q, k, v, num, stat, far, ordered, coarse_q, coarse_k, coarse_v, bias, scores_a, scores_b, scores_c) = scratch[:15]
    probs_a, probs_b, probs_c, sems, head_sems = scratch[15:]
    width = heads * HEAD
    cols = slice(first * HEAD, first * HEAD + width)
    copies = [
        pltpu.make_async_copy(pool_ref, pool, sems.at[0]),
        pltpu.make_async_copy(q_ref.at[:, cols], q, sems.at[1]),
        pltpu.make_async_copy(k_ref.at[:, cols], k, sems.at[2]),
        pltpu.make_async_copy(v_ref.at[:, cols], v, sems.at[3]),
    ]
    for copy in copies:
        copy.start()
    row = lax.broadcasted_iota(jnp.int32, (BLOCK, BLOCK), 0)
    position = lax.broadcasted_iota(jnp.int32, (BLOCK, BLOCK), 1)
    bias[...] = jnp.where(row <= token_of(position), 0.0, NEG)
    copies[0].wait()
    copies[1].wait()

    offsets, _ = far_offsets(levels)
    for unit in range(UNITS):
        pooled = dot(pool[...], q[unit * BLOCK : (unit + 1) * BLOCK, :])
        ordered[unit * BLOCK : (unit + 1) * BLOCK, :] = pooled[:BLOCK].astype(jnp.bfloat16)
        if unit >= 2:
            coarse_q[(unit - 2) * 128 : (unit - 1) * 128, :] = pooled[BLOCK : BLOCK + 128].astype(jnp.bfloat16)
        start = BLOCK + 128
        for level in range(FIRST, levels + 1):
            count = count_of(level)
            place = offsets[level] + unit * count
            far[place : place + count, :] = pooled[start : start + count].astype(jnp.bfloat16)
            start += count
    sends = [pltpu.make_async_copy(far, far_out, sems.at[4])]
    sends[0].start()
    copies[2].wait()
    copies[3].wait()
    for unit in range(2):
        rows = slice(unit * BLOCK, (unit + 1) * BLOCK)
        half = slice(unit * 128, (unit + 1) * 128)
        coarse_k[half, :] = dot(pool[BLOCK : BLOCK + 128, :], k[rows, :]).astype(jnp.bfloat16)
        coarse_v[half, :] = dot(pool[BLOCK : BLOCK + 128, :], v[rows, :]).astype(jnp.bfloat16)

    def num_copy(head, tile):
        rows = lane_block(head)
        lanes = slice(tile * 2 * BLOCK, (tile + 1) * 2 * BLOCK)
        return pltpu.make_async_copy(num.at[rows, lanes], num_out.at[rows, lanes], head_sems.at[head, tile])

    def dot_pieces(head):
        slot, own = head % 2, lane_block(head)

        def coarse():
            scores_c[slot] = dot_t(coarse_k[:, own], coarse_q[:, own])

        def part(tile, piece):
            base = 2 * tile * BLOCK
            if piece < 2:
                rows = slice(base + piece * BLOCK, base + (piece + 1) * BLOCK)
                scores_a[slot, tile, :, piece * BLOCK : (piece + 1) * BLOCK] = dot_t(
                    k[base : base + BLOCK, own], ordered[rows, own]
                )
            else:
                rows = slice(base + BLOCK, base + 2 * BLOCK)
                scores_b[slot, tile] = dot_t(k[rows, own], ordered[rows, own])

        return [coarse] + [functools.partial(part, tile, piece) for tile in (1, 0) for piece in range(3)]

    def soft_a(head, tile, block):
        slot, lanes = head % 2, lane_block(block)
        return soft_columns(
            [lambda span: scores_a[slot, tile, span, lanes] + bias[span, lanes]], [probs_a.at[slot, tile, :, lanes]]
        )

    def soft_b(head, tile, block):
        slot, lanes, late = head % 2, lane_block(block), lane_block(2 + block)
        return soft_columns(
            [
                lambda span: scores_a[slot, tile, span, late],
                lambda span: scores_b[slot, tile, span, lanes] + bias[span, lanes],
            ],
            [probs_a.at[slot, tile, :, late], probs_b.at[slot, tile, :, lanes]],
        )

    def soft_c(head, block):
        slot, lanes = head % 2, lane_block(block)
        return soft_columns([lambda span: scores_c[slot, span, lanes]], [probs_c.at[slot, :, lanes]])

    def weigh(head, tile):
        slot, own, base = head % 2, lane_block(head), 2 * tile * BLOCK
        both = dot_first(v[base : base + BLOCK, own], probs_a[slot, tile])
        more = dot_first(v[base + BLOCK : base + 2 * BLOCK, own], probs_b[slot, tile])
        nums = [both[:, lane_block(0)], both[:, lane_block(1)]]
        return nums + [both[:, lane_block(2 + block)] + more[:, lane_block(block)] for block in range(2)]

    def keep(head, tile, states):
        for index, state in enumerate(states):
            lanes = lane_block(4 * tile + index)
            num[lane_block(head), lanes] = state[0]
            stat[head, 0:1, lanes] = state[1]
            stat[head, 1:2, lanes] = state[2]
        num_copy(head, tile).start()

    def finish_late(head, nums, stats, coarse_num, coarse_stats):
        states = []
        for block in range(4):
            unit = block // 2
            coarse = (2.0 * coarse_num[:, lane_block(unit)], coarse_stats[unit][0], 2.0 * coarse_stats[unit][1])
            states.append(merge((nums[block],) + stats[block], coarse))
        keep(head, 1, states)

    for piece in dot_pieces(0):
        piece()
    pending = None
    for head in range(heads):
        pieces = dot_pieces(head + 1) if head + 1 < heads else []

        def more():
            if pieces:
                pieces.pop(0)()

        coarse_stats = [soft_c(head, 0)]
        more()
        if pending is not None:
            pending()
        coarse_stats.append(soft_c(head, 1))
        more()
        coarse_num = dot_first(coarse_v[:, lane_block(head)], probs_c[head % 2])
        late_stats = []
        for block in range(2):
            late_stats.append(soft_a(head, 1, block))
            more()
        for block in range(2):
            late_stats.append(soft_b(head, 1, block))
            more()
        nums = weigh(head, 1)
        stats = [soft_a(head, 0, 0)]
        more()
        stats.append(soft_a(head, 0, 1))
        finish_late(head, nums, late_stats, coarse_num, coarse_stats)
        for block in range(2):
            stats.append(soft_b(head, 0, block))

        def pending(head=head, stats=stats):
            keep(head, 0, [(item,) + pair for item, pair in zip(weigh(head, 0), stats)])

    pending()
    sends.append(pltpu.make_async_copy(stat, stat_out, sems.at[5]))
    sends[-1].start()
    for send in sends:
        send.wait()
    for head in range(heads):
        for tile in range(2):
            num_copy(head, tile).wait()


def near_call(queries, keys, values, levels, index):
    pool = as_bf16(padded(np.concatenate([pool_rows(level) for level in range(levels + 1)]), 16))
    first, heads = SLICES[index]
    width = heads * HEAD
    _, far_rows = far_offsets(levels)
    bf16, f32 = jnp.bfloat16, jnp.float32
    return pl.pallas_call(
        functools.partial(near_kernel, levels, first, heads),
        in_specs=[HBM] * 4,
        out_specs=[HBM] * 3,
        out_shape=[
            jax.ShapeDtypeStruct((width, TOK), f32),
            jax.ShapeDtypeStruct((heads, 8, TOK), f32),
            jax.ShapeDtypeStruct((far_rows, width), bf16),
        ],
        scratch_shapes=[
            pltpu.VMEM(pool.shape, bf16),
            pltpu.VMEM((TOK, width), bf16),
            pltpu.VMEM((TOK, width), bf16),
            pltpu.VMEM((TOK, width), bf16),
            pltpu.VMEM((width, TOK), f32),
            pltpu.VMEM((heads, 8, TOK), f32),
            pltpu.VMEM((far_rows, width), bf16),
            pltpu.VMEM((TOK, width), bf16),
            pltpu.VMEM((BLOCK, width), bf16),
            pltpu.VMEM((BLOCK, width), bf16),
            pltpu.VMEM((BLOCK, width), bf16),
            pltpu.VMEM((BLOCK, BLOCK), f32),
            pltpu.VMEM((2, 2, BLOCK, 2 * BLOCK), f32),
            pltpu.VMEM((2, 2, BLOCK, BLOCK), f32),
            pltpu.VMEM((2, BLOCK, BLOCK), f32),
            pltpu.VMEM((2, 2, BLOCK, 2 * BLOCK), bf16),
            pltpu.VMEM((2, 2, BLOCK, BLOCK), bf16),
            pltpu.VMEM((2, BLOCK, BLOCK), bf16),
            pltpu.SemaphoreType.DMA((6,)),
            pltpu.SemaphoreType.DMA((heads, 2)),
        ],
        compiler_params=pltpu.CompilerParams(vmem_limit_bytes=VMEM_CLAIM),
        cost_estimate=pl.CostEstimate(flops=8_000_000_000, bytes_accessed=4 * MIB, transcendentals=0),
        name="near_levels",
    )(pool, queries, keys, values)


def by_lane_group(arrays, size):
    lane = lax.broadcasted_iota(jnp.int32, arrays[0].shape, 1)
    result = arrays[-1]
    for index in range(len(arrays) - 2, -1, -1):
        result = jnp.where(lane < (index + 1) * size, arrays[index], result)
    return result


def widen_to_second(array):
    r32, r64, r96 = [pltpu.roll(array, shift, 1) for shift in (32, 64, 96)]
    return [by_lane_group([array, r32, r32, r64], 32), by_lane_group([r64, r96, r96, array], 32)]


def widen_to_units(arrays):
    units = []
    for array in arrays:
        turned = pltpu.roll(array, 64, 1)
        units += [by_lane_group([array, turned], 64), by_lane_group([turned, array], 64)]
    return units


def far_kernel(levels, plan, *refs):
    crossing = range(FIRST, levels + 1)
    bundles = 1 + max(bundle for _, bundle, _ in plan)
    kv_refs = refs[:bundles]
    refs = refs[bundles:]
    slices = len(SLICES)
    far_refs, num_refs, stat_refs = refs[:slices], refs[slices : 2 * slices], refs[2 * slices : 3 * slices]
    turn_ref, w_ref, out_ref = refs[3 * slices : 3 * slices + 3]
    kv, queries, num, stat, turn, weights, scores, probs = refs[3 * slices + 3 : 3 * slices + 11]
    mixed, natural, stage, partial, kv_sems, near_sems, out_sems = refs[3 * slices + 11 :]
    pair = 2 * HEAD
    model = w_ref.shape[1]
    step = 256
    offsets, far_rows = far_offsets(levels)

    def kv_copies(index):
        cols = slice(index * pair, (index + 1) * pair)
        made = []
        for number, (level, bundle, spans) in enumerate(plan):
            source_start, target_start, rows = spans
            made.append(
                pltpu.make_async_copy(
                    kv_refs[bundle].at[:, source_start : source_start + rows, cols],
                    kv.at[level - FIRST, :, target_start : target_start + rows, cols],
                    kv_sems.at[index, number],
                )
            )
        return made

    far_copies, near_copies = [], []
    for index, (first, heads) in enumerate(SLICES):
        cols = slice(first * HEAD, (first + heads) * HEAD)
        group = slice(first, first + heads)
        sems = [near_sems.at[place * slices + index] for place in range(3)]
        far_copies.append(pltpu.make_async_copy(far_refs[index], queries.at[:, cols], sems[0]))
        near_copies.append(
            [
                pltpu.make_async_copy(num_refs[index], num.at[cols, :], sems[1]),
                pltpu.make_async_copy(stat_refs[index], stat.at[group], sems[2]),
            ]
        )
    turn_copy = pltpu.make_async_copy(turn_ref, turn, near_sems.at[3 * slices])
    half = WIDTH // 2
    w_copies = [
        pltpu.make_async_copy(w_ref.at[rows], weights.at[rows], near_sems.at[3 * slices + 1 + index])
        for index, rows in enumerate((slice(0, half), slice(half, WIDTH)))
    ]
    stages = [
        far_copies[:1] + kv_copies(0) + near_copies[0],
        far_copies[1:2] + kv_copies(1) + [turn_copy],
        far_copies[2:] + kv_copies(2) + near_copies[1] + w_copies[:1],
        kv_copies(3) + near_copies[2] + w_copies[1:],
    ]

    def start_stage(number):
        for copy in stages[number]:
            copy.start()

    start_stage(0)
    start_stage(1)

    def turned(part):
        cols = slice(part * half, (part + 1) * half)
        for unit in range(UNITS):
            rows = slice(unit * BLOCK, (unit + 1) * BLOCK)
            natural[rows, cols] = dot_t(turn[...], mixed[cols, rows]).astype(jnp.bfloat16)

    def first_product(index):
        cols = slice(index * step, (index + 1) * step)
        partial[:, cols] = dot(natural[:, :half], weights[:half, cols])

    def score(head, level):
        own = lane_block(head)
        span = slice(offsets[level], offsets[level] + UNITS * count_of(level))
        scores[head % 2, :, span] = dot_t(kv[level - FIRST, 0, :, own], queries[span, own])

    def soft(head, level):
        blocks = range(offsets[level] // HEAD, (offsets[level] + UNITS * count_of(level)) // HEAD)
        return [
            soft_columns(
                [lambda span, block=block: scores[head % 2, span, lane_block(block)]], [probs.at[head % 2, :, lane_block(block)]]
            )
            for block in blocks
        ]

    def weigh(head, level, stats):
        own = lane_block(head)
        span = slice(offsets[level], offsets[level] + UNITS * count_of(level))
        live = ((position >> (level - FIRST)) & 1) == 1
        factor = jnp.where(live, 2.0**level, 0.0)
        weighted = factor * dot_first(kv[level - FIRST, 1, :, own], probs[head % 2, :, span])
        return [
            (weighted[:, lane_block(block)], jnp.where(live, peak, NEG), factor * total)
            for block, (peak, total) in enumerate(stats)
        ]

    def join(state, terms):
        if state is None:
            return terms
        if len(terms) > len(state):
            wide = [widen_to_second(item) for item in state[0]]
            state = [tuple(item[side] for item in wide) for side in range(2)]
        return [merge(old, new) for old, new in zip(state, terms)]

    def mix(head, state):
        own = lane_block(head)
        wide = [widen_to_units([half[place] for half in state]) for place in range(3)]
        for unit in range(UNITS):
            far_num, far_peak, far_total = [item[unit] for item in wide]
            for block in range(2 * unit, 2 * unit + 2):
                peak = stat[head, 0:1, lane_block(block)]
                total = stat[head, 1:2, lane_block(block)]
                top = jnp.maximum(peak, far_peak)
                a = jnp.exp(peak - top)
                b = jnp.exp(far_peak - top)
                inverse = 1.0 / (a * total + b * far_total)
                both = (a * inverse) * num[own, lane_block(block)] + (b * inverse) * far_num
                mixed[own, lane_block(block)] = both.astype(jnp.bfloat16)

    position = lax.axis_index("seq")
    order = list(range(levels, FIRST - 1, -1))
    for copy in far_copies[:1] + kv_copies(0):
        copy.wait()
    start_stage(2)
    for level in order:
        score(0, level)
    for copy in near_copies[0]:
        copy.wait()
    pending = None
    products = [functools.partial(first_product, index) for index in range(model // step)]
    for head in range(HEADS):
        if head % 2 == 1 and head + 1 < HEADS:
            for copy in kv_copies((head + 1) // 2):
                copy.wait()
        for index, (first, _) in enumerate(SLICES):
            if index and first == head + 1:
                far_copies[index].wait()
        if head == 1:
            start_stage(3)
        for index, (first, _) in enumerate(SLICES):
            if index and first == head:
                for copy in near_copies[index]:
                    copy.wait()
        terms = []
        for level in order:
            stats = soft(head, level)
            if head + 1 < HEADS:
                score(head + 1, level)
            if level == order[0] and pending is not None:
                pending()
                if head == HEADS // 2:
                    turn_copy.wait()
                    w_copies[0].wait()
                    turned(0)
            elif head >= HEADS // 2 and products:
                products.pop(0)()
            terms.append(weigh(head, level, stats))

        def pending(head=head, terms=terms):
            mix(head, functools.reduce(join, terms, None))

    pending()

    for product in products:
        product()
    turned(1)
    w_copies[1].wait()
    sends = []
    for index in range(model // step):
        cols = slice(index * step, (index + 1) * step)
        stage[:, cols] = (partial[:, cols] + dot(natural[:, half:], weights[half:, cols])).astype(jnp.bfloat16)
        sends.append(pltpu.make_async_copy(stage.at[:, cols], out_ref.at[:, cols], out_sems.at[index]))
        sends[-1].start()
    for send in sends:
        send.wait()


def far_call(bundles, plan, near, w_out, levels):
    turn = np.zeros((BLOCK, BLOCK))
    turn[token_of(np.arange(BLOCK)), np.arange(BLOCK)] = 1.0
    nums, stats, fars = [[item[place] for item in near] for place in range(3)]
    model = w_out.shape[1]
    _, far_rows = far_offsets(levels)
    count = levels - FIRST + 1
    bf16, f32 = jnp.bfloat16, jnp.float32
    return pl.pallas_call(
        functools.partial(far_kernel, levels, plan),
        in_specs=[HBM] * (len(bundles) + 3 * len(SLICES) + 2),
        out_specs=HBM,
        out_shape=jax.ShapeDtypeStruct((TOK, model), bf16),
        scratch_shapes=[
            pltpu.VMEM((count, 2, BLOCK, WIDTH), bf16),
            pltpu.VMEM((far_rows, WIDTH), bf16),
            pltpu.VMEM((WIDTH, TOK), f32),
            pltpu.VMEM((HEADS, 8, TOK), f32),
            pltpu.VMEM((BLOCK, BLOCK), bf16),
            pltpu.VMEM((WIDTH, model), bf16),
            pltpu.VMEM((2, BLOCK, far_rows), f32),
            pltpu.VMEM((2, BLOCK, far_rows), bf16),
            pltpu.VMEM((WIDTH, TOK), bf16),
            pltpu.VMEM((TOK, WIDTH), bf16),
            pltpu.VMEM((TOK, model), bf16),
            pltpu.VMEM((TOK, model), f32),
            pltpu.SemaphoreType.DMA((HEADS // 2, len(plan))),
            pltpu.SemaphoreType.DMA((3 * len(SLICES) + 3,)),
            pltpu.SemaphoreType.DMA((model // 256,)),
        ],
        compiler_params=pltpu.CompilerParams(vmem_limit_bytes=VMEM_CLAIM),
        cost_estimate=pl.CostEstimate(flops=6_500_000_000, bytes_accessed=18 * MIB, transcendentals=3_000_000),
        name="far_levels_projection",
    )(*bundles, *fars, *nums, *stats, as_bf16(turn), w_out)


def moved(array, distance):
    return lax.ppermute(array, "seq", [(i ^ distance, i) for i in range(lax.axis_size("seq"))])


def gathered(blocks, distance):
    sent = jnp.concatenate(blocks, axis=1) if len(blocks) > 1 else blocks[0]
    got = moved(sent, distance)
    joined, start = [], 0
    for block in blocks:
        rows = block.shape[1]
        joined.append(jnp.concatenate([block, got[:, start : start + rows]], axis=1))
        start += rows
    return joined


def after(arrays, others):
    return lax.optimization_barrier((arrays, others))[0]


def on_device(queries, keys, values, w_out):
    size = lax.axis_size("seq")
    levels = (TOK * size // (2 * BLOCK)).bit_length() - 1
    pooled = pool_call(keys, values, levels)

    places, _ = packed(levels)
    blocks = {2: pooled[0], 4: pooled[3]}
    for level in range(TOP, levels + 1):
        place, first = places[level]
        blocks[level] = pooled[place][:, first : first + (TOK >> level)]
    high = list(range(TOP, levels + 1))

    for distance in [1 << (level - FIRST) for level in high]:
        members = [level for level in high if 1 << (level - FIRST) >= distance]
        sent = pooled[-1] if distance == GROUP else jnp.concatenate([blocks[level] for level in members], axis=1)
        got = moved(sent, distance)
        start = 0
        for level in members:
            rows = blocks[level].shape[1]
            piece = got[:, start : start + rows]
            start += rows
            if 1 << (level - FIRST) == distance:
                blocks[level] = piece
            else:
                blocks[level] = jnp.concatenate([blocks[level], piece], axis=1)
        if distance == GROUP:
            fourth = moved(blocks[4], 4)
            third = [moved(pooled[1], 2)]
            arrived = blocks[TOP]
            third.append(moved(after(pooled[2], arrived), 2))
            second = moved(after(blocks[2], arrived), 1)

    upper = [blocks[level] for level in high[1:]]
    five = gathered([arrived], 2)
    near = [near_call(after(queries, arrived), keys, values, levels, 0)]
    upper = gathered(after(upper, near[0]), 4)
    five_y = gathered(after(five, near[0]), 4)
    fourth = gathered([after(fourth, near[0])], 2)[0]
    near.append(near_call(after(queries, (near[0], five)), keys, values, levels, 1))
    upper_x = gathered(after(upper, near[1]), 2)
    low = jnp.concatenate([*after(third, near[1]), fourth], axis=1)
    low_got = moved(low, 1)
    near.append(near_call(after(queries, (near[1], upper)), keys, values, levels, 2))
    top = jnp.concatenate(after(five_y + upper_x, near[2]), axis=1)
    top_got = moved(top, 1)
    plan = [(2, 4, (0, 0, BLOCK))]
    for level in (3, 4):
        plan += [(level, bundle, ((level - 3) * 128, bundle * 128, 128)) for bundle in (0, 1)]
    for level in high:
        plan += [(level, bundle, ((level - TOP) * 128, (bundle - 2) * 128, 128)) for bundle in (2, 3)]
    return far_call([low, low_got, top, top_got, second], plan, near, w_out, levels)


def solution(mesh):
    return jax.shard_map(
        on_device,
        mesh=mesh,
        in_specs=(P("seq", None), P("seq", None), P("seq", None), P()),
        out_specs=P("seq", None),
        check_vma=False,
    )
```

```python
import functools

import jax
import jax.numpy as jnp
import numpy as np
from jax import lax
from jax.experimental import pallas as pl
from jax.experimental.pallas import tpu as pltpu
from jax.sharding import PartitionSpec as P

HEADS = 8
HEAD = 128
BLOCK = 256
TOK = 1024
UNITS = TOK // BLOCK
WIDTH = HEADS * HEAD
NEG = -1e30
FIRST = 2
TOP = 5
GROUP = 8
SCALE = HEAD**-0.5
LOG2E = 1.4426950408889634
MIB = 1 << 20
SLICES = ((0, 3), (3, 1), (4, 4))
VMEM_CLAIM = 60 * MIB
HBM = pl.BlockSpec(memory_space=pltpu.HBM)


def token_of(position):
    return ((position & 31) << 3) | (((position >> 5) & 1) << 2) | (((position >> 6) & 1) << 1) | (position >> 7)


def count_of(level):
    return max(BLOCK >> level, 32)


def pool_rows(level):
    rows = token_of(np.arange(count_of(level))) >> level
    columns = np.arange(BLOCK) >> level
    return (rows[:, None] == columns[None, :]) * 2.0**-level


def natural_pool(level, span):
    rows = np.arange(span >> level)
    return (rows[:, None] == (np.arange(span) >> level)[None, :]) * 2.0**-level


def padded(array, multiple):
    return np.pad(array, ((0, -len(array) % multiple), (0, 0)))


def as_bf16(array):
    return jnp.asarray(array.astype(np.float32)).astype(jnp.bfloat16)


def dot(a, b):
    return jnp.dot(a, b, preferred_element_type=jnp.float32)


def dot_t(a, b):
    return lax.dot_general(a, b, (((1,), (1,)), ((), ())), preferred_element_type=jnp.float32)


def dot_first(a, b):
    return lax.dot_general(a, b, (((0,), (0,)), ((), ())), preferred_element_type=jnp.float32)


def merge(first, second):
    top = jnp.maximum(first[1], second[1])
    a = jnp.exp(first[1] - top)
    b = jnp.exp(second[1] - top)
    return (a * first[0] + b * second[0], top, a * first[2] + b * second[2])


ROWS = 64


def soft_columns(loads, targets):
    spans = [slice(start, start + ROWS) for start in range(0, BLOCK, ROWS)]
    peak = None
    for load in loads:
        for span in spans:
            rows = jnp.max(load(span).reshape(ROWS // 8, 8, HEAD), axis=0)
            peak = rows if peak is None else jnp.maximum(peak, rows)
    peak = jnp.max(peak, axis=0, keepdims=True)
    total = jnp.zeros((8, HEAD), jnp.float32)
    for load, target in zip(loads, targets):
        for span in spans:
            probs = jnp.exp2((load(span) - peak) * (SCALE * LOG2E))
            total = total + jnp.sum(probs.reshape(ROWS // 8, 8, HEAD), axis=0)
            target[span, :] = probs.astype(jnp.bfloat16)
    return peak * SCALE, jnp.sum(total, axis=0, keepdims=True)


def packed(levels):
    places, rows = {2: (0, 0), 3: (1, 0), 4: (3, 0)}, 0
    for level in range(TOP, levels + 1):
        places[level] = (4, rows)
        rows += TOK >> level
    return places, [TOK >> 2, TOK >> 4, TOK >> 4, TOK >> 4, rows]


def pool_kernel(levels, small_ref, large_ref, keys_ref, values_ref, *refs):
    places, sizes = packed(levels)
    count = len(sizes)
    targets, (small, large, buffers, *outs, sems, out_sems) = refs[:count], refs[count:]
    step = WIDTH // 4
    fixed = [pltpu.make_async_copy(small_ref, small, sems.at[8]), pltpu.make_async_copy(large_ref, large, sems.at[9])]
    copies = []
    for index, source in enumerate((keys_ref, values_ref)):
        for part in range(4):
            cols = slice(part * step, (part + 1) * step)
            copies.append(pltpu.make_async_copy(source.at[:, cols], buffers.at[index, :, cols], sems.at[index * 4 + part]))
    for copy in fixed + copies:
        copy.start()
    for copy in fixed:
        copy.wait()
    sends = []
    for index in range(2):
        for part in range(4):
            cols = slice(part * step, (part + 1) * step)
            copies[index * 4 + part].wait()
            tiles = [
                dot(small[...], buffers[index, i * 2 * BLOCK : (i + 1) * 2 * BLOCK, cols]) for i in range(UNITS // 2)
            ]
            offset = 0
            for level in range(FIRST, min(levels, 6) + 1):
                rows = 2 * BLOCK >> level
                if level == 3:
                    for place, tile in enumerate(tiles):
                        outs[1 + place][index, :, cols] = tile[offset : offset + rows].astype(jnp.bfloat16)
                    offset += rows
                    continue
                both = jnp.concatenate([tile[offset : offset + rows] for tile in tiles], axis=0)
                place, first = places[level]
                outs[place][index, first : first + 2 * rows, cols] = both.astype(jnp.bfloat16)
                offset += rows
            if levels > 6:
                rest = dot(large[...], buffers[index, :, cols])
                for level in range(7, levels + 1):
                    start = (level - 7) * 8
                    place, first = places[level]
                    outs[place][index, first : first + (TOK >> level), cols] = rest[start : start + (TOK >> level)].astype(jnp.bfloat16)
            for place, (out, target) in enumerate(zip(outs, targets)):
                span = (index, slice(None), cols)
                sends.append(pltpu.make_async_copy(out.at[span], target.at[span], out_sems.at[index * 4 + part, place]))
                sends[-1].start()
    for send in sends:
        send.wait()


def pool_call(keys, values, levels):
    small = as_bf16(padded(np.concatenate([natural_pool(level, 2 * BLOCK) for level in range(FIRST, min(levels, 6) + 1)]), 16))
    parts = [padded(natural_pool(level, TOK), 8) for level in range(7, levels + 1)] + [np.zeros((8, TOK))]
    large = as_bf16(padded(np.concatenate(parts), 16))
    _, sizes = packed(levels)
    return pl.pallas_call(
        functools.partial(pool_kernel, levels),
        in_specs=[HBM] * 4,
        out_specs=[HBM] * len(sizes),
        out_shape=[jax.ShapeDtypeStruct((2, rows, WIDTH), jnp.bfloat16) for rows in sizes],
        scratch_shapes=[
            pltpu.VMEM(small.shape, jnp.bfloat16),
            pltpu.VMEM(large.shape, jnp.bfloat16),
            pltpu.VMEM((2, TOK, WIDTH), jnp.bfloat16),
        ]
        + [pltpu.VMEM((2, rows, WIDTH), jnp.bfloat16) for rows in sizes]
        + [
            pltpu.SemaphoreType.DMA((10,)),
            pltpu.SemaphoreType.DMA((8, len(sizes))),
        ],
        compiler_params=pltpu.CompilerParams(vmem_limit_bytes=VMEM_CLAIM),
        cost_estimate=pl.CostEstimate(flops=2 * 256 * 512 * 4096, bytes_accessed=6 * MIB, transcendentals=0),
        name="pool_keys_values",
    )(small, large, keys, values)


def far_offsets(levels):
    offsets, total = {}, 0
    for level in range(FIRST, levels + 1):
        offsets[level] = total
        total += UNITS * count_of(level)
    return offsets, total


def lane_block(index):
    return slice(index * HEAD, (index + 1) * HEAD)


def near_kernel(levels, first, heads, pool_ref, q_ref, k_ref, v_ref, num_out, stat_out, far_out, *scratch):
    (pool, q, k, v, num, stat, far, ordered, coarse_q, coarse_k, coarse_v, bias, scores_a, scores_b, scores_c) = scratch[:15]
    probs_a, probs_b, probs_c, sems, head_sems = scratch[15:]
    width = heads * HEAD
    cols = slice(first * HEAD, first * HEAD + width)
    copies = [
        pltpu.make_async_copy(pool_ref, pool, sems.at[0]),
        pltpu.make_async_copy(q_ref.at[:, cols], q, sems.at[1]),
        pltpu.make_async_copy(k_ref.at[:, cols], k, sems.at[2]),
        pltpu.make_async_copy(v_ref.at[:, cols], v, sems.at[3]),
    ]
    for copy in copies:
        copy.start()
    row = lax.broadcasted_iota(jnp.int32, (BLOCK, BLOCK), 0)
    position = lax.broadcasted_iota(jnp.int32, (BLOCK, BLOCK), 1)
    bias[...] = jnp.where(row <= token_of(position), 0.0, NEG)
    copies[0].wait()
    copies[1].wait()

    offsets, _ = far_offsets(levels)
    for unit in range(UNITS):
        pooled = dot(pool[...], q[unit * BLOCK : (unit + 1) * BLOCK, :])
        ordered[unit * BLOCK : (unit + 1) * BLOCK, :] = pooled[:BLOCK].astype(jnp.bfloat16)
        if unit >= 2:
            coarse_q[(unit - 2) * 128 : (unit - 1) * 128, :] = pooled[BLOCK : BLOCK + 128].astype(jnp.bfloat16)
        start = BLOCK + 128
        for level in range(FIRST, levels + 1):
            count = count_of(level)
            place = offsets[level] + unit * count
            far[place : place + count, :] = pooled[start : start + count].astype(jnp.bfloat16)
            start += count
    sends = [pltpu.make_async_copy(far, far_out, sems.at[4])]
    sends[0].start()
    copies[2].wait()
    copies[3].wait()
    for unit in range(2):
        rows = slice(unit * BLOCK, (unit + 1) * BLOCK)
        half = slice(unit * 128, (unit + 1) * 128)
        coarse_k[half, :] = dot(pool[BLOCK : BLOCK + 128, :], k[rows, :]).astype(jnp.bfloat16)
        coarse_v[half, :] = dot(pool[BLOCK : BLOCK + 128, :], v[rows, :]).astype(jnp.bfloat16)

    def num_copy(head, tile):
        rows = lane_block(head)
        lanes = slice(tile * 2 * BLOCK, (tile + 1) * 2 * BLOCK)
        return pltpu.make_async_copy(num.at[rows, lanes], num_out.at[rows, lanes], head_sems.at[head, tile])

    def dot_pieces(head):
        slot, own = head % 2, lane_block(head)

        def coarse():
            scores_c[slot] = dot_t(coarse_k[:, own], coarse_q[:, own])

        def part(tile, piece):
            base = 2 * tile * BLOCK
            if piece < 2:
                rows = slice(base + piece * BLOCK, base + (piece + 1) * BLOCK)
                scores_a[slot, tile, :, piece * BLOCK : (piece + 1) * BLOCK] = dot_t(
                    k[base : base + BLOCK, own], ordered[rows, own]
                )
            else:
                rows = slice(base + BLOCK, base + 2 * BLOCK)
                scores_b[slot, tile] = dot_t(k[rows, own], ordered[rows, own])

        return [coarse] + [functools.partial(part, tile, piece) for tile in (1, 0) for piece in range(3)]

    def soft_a(head, tile, block):
        slot, lanes = head % 2, lane_block(block)
        return soft_columns(
            [lambda span: scores_a[slot, tile, span, lanes] + bias[span, lanes]], [probs_a.at[slot, tile, :, lanes]]
        )

    def soft_b(head, tile, block):
        slot, lanes, late = head % 2, lane_block(block), lane_block(2 + block)
        return soft_columns(
            [
                lambda span: scores_a[slot, tile, span, late],
                lambda span: scores_b[slot, tile, span, lanes] + bias[span, lanes],
            ],
            [probs_a.at[slot, tile, :, late], probs_b.at[slot, tile, :, lanes]],
        )

    def soft_c(head, block):
        slot, lanes = head % 2, lane_block(block)
        return soft_columns([lambda span: scores_c[slot, span, lanes]], [probs_c.at[slot, :, lanes]])

    def weigh(head, tile):
        slot, own, base = head % 2, lane_block(head), 2 * tile * BLOCK
        both = dot_first(v[base : base + BLOCK, own], probs_a[slot, tile])
        more = dot_first(v[base + BLOCK : base + 2 * BLOCK, own], probs_b[slot, tile])
        nums = [both[:, lane_block(0)], both[:, lane_block(1)]]
        return nums + [both[:, lane_block(2 + block)] + more[:, lane_block(block)] for block in range(2)]

    def keep(head, tile, states):
        for index, state in enumerate(states):
            lanes = lane_block(4 * tile + index)
            num[lane_block(head), lanes] = state[0]
            stat[head, 0:1, lanes] = state[1]
            stat[head, 1:2, lanes] = state[2]
        num_copy(head, tile).start()

    def finish_late(head, nums, stats, coarse_num, coarse_stats):
        states = []
        for block in range(4):
            unit = block // 2
            coarse = (2.0 * coarse_num[:, lane_block(unit)], coarse_stats[unit][0], 2.0 * coarse_stats[unit][1])
            states.append(merge((nums[block],) + stats[block], coarse))
        keep(head, 1, states)

    for piece in dot_pieces(0):
        piece()
    pending = None
    for head in range(heads):
        pieces = dot_pieces(head + 1) if head + 1 < heads else []

        def more():
            if pieces:
                pieces.pop(0)()

        coarse_stats = [soft_c(head, 0)]
        more()
        if pending is not None:
            pending()
        coarse_stats.append(soft_c(head, 1))
        more()
        coarse_num = dot_first(coarse_v[:, lane_block(head)], probs_c[head % 2])
        late_stats = []
        for block in range(2):
            late_stats.append(soft_a(head, 1, block))
            more()
        for block in range(2):
            late_stats.append(soft_b(head, 1, block))
            more()
        nums = weigh(head, 1)
        stats = [soft_a(head, 0, 0)]
        more()
        stats.append(soft_a(head, 0, 1))
        finish_late(head, nums, late_stats, coarse_num, coarse_stats)
        for block in range(2):
            stats.append(soft_b(head, 0, block))

        def pending(head=head, stats=stats):
            keep(head, 0, [(item,) + pair for item, pair in zip(weigh(head, 0), stats)])

    pending()
    sends.append(pltpu.make_async_copy(stat, stat_out, sems.at[5]))
    sends[-1].start()
    for send in sends:
        send.wait()
    for head in range(heads):
        for tile in range(2):
            num_copy(head, tile).wait()


def near_call(queries, keys, values, levels, index):
    pool = as_bf16(padded(np.concatenate([pool_rows(level) for level in range(levels + 1)]), 16))
    first, heads = SLICES[index]
    width = heads * HEAD
    _, far_rows = far_offsets(levels)
    bf16, f32 = jnp.bfloat16, jnp.float32
    return pl.pallas_call(
        functools.partial(near_kernel, levels, first, heads),
        in_specs=[HBM] * 4,
        out_specs=[HBM] * 3,
        out_shape=[
            jax.ShapeDtypeStruct((width, TOK), f32),
            jax.ShapeDtypeStruct((heads, 8, TOK), f32),
            jax.ShapeDtypeStruct((far_rows, width), bf16),
        ],
        scratch_shapes=[
            pltpu.VMEM(pool.shape, bf16),
            pltpu.VMEM((TOK, width), bf16),
            pltpu.VMEM((TOK, width), bf16),
            pltpu.VMEM((TOK, width), bf16),
            pltpu.VMEM((width, TOK), f32),
            pltpu.VMEM((heads, 8, TOK), f32),
            pltpu.VMEM((far_rows, width), bf16),
            pltpu.VMEM((TOK, width), bf16),
            pltpu.VMEM((BLOCK, width), bf16),
            pltpu.VMEM((BLOCK, width), bf16),
            pltpu.VMEM((BLOCK, width), bf16),
            pltpu.VMEM((BLOCK, BLOCK), f32),
            pltpu.VMEM((2, 2, BLOCK, 2 * BLOCK), f32),
            pltpu.VMEM((2, 2, BLOCK, BLOCK), f32),
            pltpu.VMEM((2, BLOCK, BLOCK), f32),
            pltpu.VMEM((2, 2, BLOCK, 2 * BLOCK), bf16),
            pltpu.VMEM((2, 2, BLOCK, BLOCK), bf16),
            pltpu.VMEM((2, BLOCK, BLOCK), bf16),
            pltpu.SemaphoreType.DMA((6,)),
            pltpu.SemaphoreType.DMA((heads, 2)),
        ],
        compiler_params=pltpu.CompilerParams(vmem_limit_bytes=VMEM_CLAIM),
        cost_estimate=pl.CostEstimate(flops=8_000_000_000, bytes_accessed=4 * MIB, transcendentals=0),
        name="near_levels",
    )(pool, queries, keys, values)


def by_lane_group(arrays, size):
    lane = lax.broadcasted_iota(jnp.int32, arrays[0].shape, 1)
    result = arrays[-1]
    for index in range(len(arrays) - 2, -1, -1):
        result = jnp.where(lane < (index + 1) * size, arrays[index], result)
    return result


def widen_to_second(array):
    r32, r64, r96 = [pltpu.roll(array, shift, 1) for shift in (32, 64, 96)]
    return [by_lane_group([array, r32, r32, r64], 32), by_lane_group([r64, r96, r96, array], 32)]


def widen_to_units(arrays):
    units = []
    for array in arrays:
        turned = pltpu.roll(array, 64, 1)
        units += [by_lane_group([array, turned], 64), by_lane_group([turned, array], 64)]
    return units


def far_kernel(levels, plan, *refs):
    crossing = range(FIRST, levels + 1)
    bundles = 1 + max(bundle for _, bundle, _ in plan)
    kv_refs = refs[:bundles]
    refs = refs[bundles:]
    slices = len(SLICES)
    far_refs, num_refs, stat_refs = refs[:slices], refs[slices : 2 * slices], refs[2 * slices : 3 * slices]
    turn_ref, w_ref, out_ref = refs[3 * slices : 3 * slices + 3]
    kv, queries, num, stat, turn, weights, scores, probs = refs[3 * slices + 3 : 3 * slices + 11]
    mixed, natural, stage, partial, kv_sems, near_sems, out_sems = refs[3 * slices + 11 :]
    pair = 2 * HEAD
    model = w_ref.shape[1]
    step = 256
    offsets, far_rows = far_offsets(levels)

    def kv_copies(index):
        cols = slice(index * pair, (index + 1) * pair)
        made = []
        for number, (level, bundle, spans) in enumerate(plan):
            source_start, target_start, rows = spans
            made.append(
                pltpu.make_async_copy(
                    kv_refs[bundle].at[:, source_start : source_start + rows, cols],
                    kv.at[level - FIRST, :, target_start : target_start + rows, cols],
                    kv_sems.at[index, number],
                )
            )
        return made

    far_copies, near_copies = [], []
    for index, (first, heads) in enumerate(SLICES):
        cols = slice(first * HEAD, (first + heads) * HEAD)
        group = slice(first, first + heads)
        sems = [near_sems.at[place * slices + index] for place in range(3)]
        far_copies.append(pltpu.make_async_copy(far_refs[index], queries.at[:, cols], sems[0]))
        near_copies.append(
            [
                pltpu.make_async_copy(num_refs[index], num.at[cols, :], sems[1]),
                pltpu.make_async_copy(stat_refs[index], stat.at[group], sems[2]),
            ]
        )
    turn_copy = pltpu.make_async_copy(turn_ref, turn, near_sems.at[3 * slices])
    half = WIDTH // 2
    w_copies = [
        pltpu.make_async_copy(w_ref.at[rows], weights.at[rows], near_sems.at[3 * slices + 1 + index])
        for index, rows in enumerate((slice(0, half), slice(half, WIDTH)))
    ]
    stages = [
        far_copies[:1] + kv_copies(0) + near_copies[0],
        far_copies[1:2] + kv_copies(1) + [turn_copy],
        far_copies[2:] + kv_copies(2) + near_copies[1] + w_copies[:1],
        kv_copies(3) + near_copies[2] + w_copies[1:],
    ]

    def start_stage(number):
        for copy in stages[number]:
            copy.start()

    start_stage(0)
    start_stage(1)

    def turned(part):
        cols = slice(part * half, (part + 1) * half)
        for unit in range(UNITS):
            rows = slice(unit * BLOCK, (unit + 1) * BLOCK)
            natural[rows, cols] = dot_t(turn[...], mixed[cols, rows]).astype(jnp.bfloat16)

    def first_product(index):
        cols = slice(index * step, (index + 1) * step)
        partial[:, cols] = dot(natural[:, :half], weights[:half, cols])

    def score(head, level):
        own = lane_block(head)
        span = slice(offsets[level], offsets[level] + UNITS * count_of(level))
        scores[head % 2, :, span] = dot_t(kv[level - FIRST, 0, :, own], queries[span, own])

    def soft(head, level):
        blocks = range(offsets[level] // HEAD, (offsets[level] + UNITS * count_of(level)) // HEAD)
        return [
            soft_columns(
                [lambda span, block=block: scores[head % 2, span, lane_block(block)]], [probs.at[head % 2, :, lane_block(block)]]
            )
            for block in blocks
        ]

    def weigh(head, level, stats):
        own = lane_block(head)
        span = slice(offsets[level], offsets[level] + UNITS * count_of(level))
        live = ((position >> (level - FIRST)) & 1) == 1
        factor = jnp.where(live, 2.0**level, 0.0)
        weighted = factor * dot_first(kv[level - FIRST, 1, :, own], probs[head % 2, :, span])
        return [
            (weighted[:, lane_block(block)], jnp.where(live, peak, NEG), factor * total)
            for block, (peak, total) in enumerate(stats)
        ]

    def join(state, terms):
        if state is None:
            return terms
        if len(terms) > len(state):
            wide = [widen_to_second(item) for item in state[0]]
            state = [tuple(item[side] for item in wide) for side in range(2)]
        return [merge(old, new) for old, new in zip(state, terms)]

    def mix(head, state):
        own = lane_block(head)
        wide = [widen_to_units([half[place] for half in state]) for place in range(3)]
        for unit in range(UNITS):
            far_num, far_peak, far_total = [item[unit] for item in wide]
            for block in range(2 * unit, 2 * unit + 2):
                peak = stat[head, 0:1, lane_block(block)]
                total = stat[head, 1:2, lane_block(block)]
                top = jnp.maximum(peak, far_peak)
                a = jnp.exp(peak - top)
                b = jnp.exp(far_peak - top)
                inverse = 1.0 / (a * total + b * far_total)
                both = (a * inverse) * num[own, lane_block(block)] + (b * inverse) * far_num
                mixed[own, lane_block(block)] = both.astype(jnp.bfloat16)

    position = lax.axis_index("seq")
    order = list(range(levels, FIRST - 1, -1))
    for copy in far_copies[:1] + kv_copies(0):
        copy.wait()
    start_stage(2)
    for level in order:
        score(0, level)
    for copy in near_copies[0]:
        copy.wait()
    pending = None
    products = [functools.partial(first_product, index) for index in range(model // step)]
    for head in range(HEADS):
        if head % 2 == 1 and head + 1 < HEADS:
            for copy in kv_copies((head + 1) // 2):
                copy.wait()
        for index, (first, _) in enumerate(SLICES):
            if index and first == head + 1:
                far_copies[index].wait()
        if head == 1:
            start_stage(3)
        for index, (first, _) in enumerate(SLICES):
            if index and first == head:
                for copy in near_copies[index]:
                    copy.wait()
        terms = []
        for level in order:
            stats = soft(head, level)
            if head + 1 < HEADS:
                score(head + 1, level)
            if level == order[0] and pending is not None:
                pending()
                if head == HEADS // 2:
                    turn_copy.wait()
                    w_copies[0].wait()
                    turned(0)
            elif head >= HEADS // 2 and products:
                products.pop(0)()
            terms.append(weigh(head, level, stats))

        def pending(head=head, terms=terms):
            mix(head, functools.reduce(join, terms, None))

    pending()

    for product in products:
        product()
    turned(1)
    w_copies[1].wait()
    sends = []
    for index in range(model // step):
        cols = slice(index * step, (index + 1) * step)
        stage[:, cols] = (partial[:, cols] + dot(natural[:, half:], weights[half:, cols])).astype(jnp.bfloat16)
        sends.append(pltpu.make_async_copy(stage.at[:, cols], out_ref.at[:, cols], out_sems.at[index]))
        sends[-1].start()
    for send in sends:
        send.wait()


def far_call(bundles, plan, near, w_out, levels):
    turn = np.zeros((BLOCK, BLOCK))
    turn[token_of(np.arange(BLOCK)), np.arange(BLOCK)] = 1.0
    nums, stats, fars = [[item[place] for item in near] for place in range(3)]
    model = w_out.shape[1]
    _, far_rows = far_offsets(levels)
    count = levels - FIRST + 1
    bf16, f32 = jnp.bfloat16, jnp.float32
    return pl.pallas_call(
        functools.partial(far_kernel, levels, plan),
        in_specs=[HBM] * (len(bundles) + 3 * len(SLICES) + 2),
        out_specs=HBM,
        out_shape=jax.ShapeDtypeStruct((TOK, model), bf16),
        scratch_shapes=[
            pltpu.VMEM((count, 2, BLOCK, WIDTH), bf16),
            pltpu.VMEM((far_rows, WIDTH), bf16),
            pltpu.VMEM((WIDTH, TOK), f32),
            pltpu.VMEM((HEADS, 8, TOK), f32),
            pltpu.VMEM((BLOCK, BLOCK), bf16),
            pltpu.VMEM((WIDTH, model), bf16),
            pltpu.VMEM((2, BLOCK, far_rows), f32),
            pltpu.VMEM((2, BLOCK, far_rows), bf16),
            pltpu.VMEM((WIDTH, TOK), bf16),
            pltpu.VMEM((TOK, WIDTH), bf16),
            pltpu.VMEM((TOK, model), bf16),
            pltpu.VMEM((TOK, model), f32),
            pltpu.SemaphoreType.DMA((HEADS // 2, len(plan))),
            pltpu.SemaphoreType.DMA((3 * len(SLICES) + 3,)),
            pltpu.SemaphoreType.DMA((model // 256,)),
        ],
        compiler_params=pltpu.CompilerParams(vmem_limit_bytes=VMEM_CLAIM),
        cost_estimate=pl.CostEstimate(flops=6_500_000_000, bytes_accessed=18 * MIB, transcendentals=3_000_000),
        name="far_levels_projection",
    )(*bundles, *fars, *nums, *stats, as_bf16(turn), w_out)


def moved(array, distance):
    return lax.ppermute(array, "seq", [(i ^ distance, i) for i in range(lax.axis_size("seq"))])


def gathered(blocks, distance):
    sent = jnp.concatenate(blocks, axis=1) if len(blocks) > 1 else blocks[0]
    got = moved(sent, distance)
    joined, start = [], 0
    for block in blocks:
        rows = block.shape[1]
        joined.append(jnp.concatenate([block, got[:, start : start + rows]], axis=1))
        start += rows
    return joined


def after(arrays, others):
    return lax.optimization_barrier((arrays, others))[0]


def on_device(queries, keys, values, w_out):
    size = lax.axis_size("seq")
    levels = (TOK * size // (2 * BLOCK)).bit_length() - 1
    pooled = pool_call(keys, values, levels)

    places, _ = packed(levels)
    blocks = {2: pooled[0], 4: pooled[3]}
    for level in range(TOP, levels + 1):
        place, first = places[level]
        blocks[level] = pooled[place][:, first : first + (TOK >> level)]
    high = list(range(TOP, levels + 1))

    for distance in [1 << (level - FIRST) for level in high]:
        members = [level for level in high if 1 << (level - FIRST) >= distance]
        sent = pooled[-1] if distance == GROUP else jnp.concatenate([blocks[level] for level in members], axis=1)
        got = moved(sent, distance)
        start = 0
        for level in members:
            rows = blocks[level].shape[1]
            piece = got[:, start : start + rows]
            start += rows
            if 1 << (level - FIRST) == distance:
                blocks[level] = piece
            else:
                blocks[level] = jnp.concatenate([blocks[level], piece], axis=1)
        if distance == GROUP:
            fourth = moved(blocks[4], 4)
            third = [moved(pooled[1], 2)]
            arrived = blocks[TOP]
            third.append(moved(after(pooled[2], arrived), 2))
            second = moved(after(blocks[2], arrived), 1)

    upper = [blocks[level] for level in high[1:]]
    five = gathered([arrived], 2)
    near = [near_call(after(queries, arrived), keys, values, levels, 0)]
    upper = gathered(after(upper, near[0]), 4)
    five_y = gathered(after(five, near[0]), 4)
    fourth = gathered([after(fourth, near[0])], 2)[0]
    near.append(near_call(after(queries, (near[0], five)), keys, values, levels, 1))
    upper_x = gathered(after(upper, near[1]), 2)
    low = jnp.concatenate([*after(third, near[1]), fourth], axis=1)
    low_got = moved(low, 1)
    near.append(near_call(after(queries, (near[1], upper)), keys, values, levels, 2))
    top = jnp.concatenate(after(five_y + upper_x, near[2]), axis=1)
    top_got = moved(top, 1)
    plan = [(2, 4, (0, 0, BLOCK))]
    for level in (3, 4):
        plan += [(level, bundle, ((level - 3) * 128, bundle * 128, 128)) for bundle in (0, 1)]
    for level in high:
        plan += [(level, bundle, ((level - TOP) * 128, (bundle - 2) * 128, 128)) for bundle in (2, 3)]
    return far_call([low, low_got, top, top_got, second], plan, near, w_out, levels)


def solution(mesh):
    return jax.shard_map(
        on_device,
        mesh=mesh,
        in_specs=(P("seq", None), P("seq", None), P("seq", None), P()),
        out_specs=P("seq", None),
        check_vma=False,
    )
```
